32 devices in a mesh: grp: 2 (over x), gx: 16 (over z, y, core).
Axes of the slice: x: 2, y: 2, z: 4, core: 2. Of those that a mesh axis runs over, the one named last changes fastest.
Arguments:
- rhs: float32 [2048, 16, 128], P('gx', 'grp'), parts along dimension 1
- ham: bfloat16 [2048, 5, 64, 128], P('gx')
- ovl: bfloat16 [2048, 5, 64, 128], P('gx')
- sigma: bfloat16 [8192, 128, 128], P('gx'), as said below
- neighbours: int32 [2048, 5], P('gx'), may hold values from 0 to 2047, as said below
- contact: int32 [128], P('gx'), may hold values from 0 to 2047, as said below
- pole_real: float32 [16], P('grp'), parts along dimension 0, may hold values from -1 to 1
- pole_imag: float32 [16], P('grp'), parts along dimension 0, may hold values from 0.2 to 1.5
Outputs:
- solution: float32 [2048, 16, 128], P('gx', 'grp'), parts along dimension 1
- residual: float32 [2048, 16, 128], P('gx', 'grp'), parts along dimension 1
The draws below stay inside these ranges and needn't reach their ends.
There are 2 independent parts, one for each index of `grp`. The reference program is written for one: setup_inputs(seed, part) draws one part's arguments, and reference() takes and returns one part's arrays. A program takes and returns all parts, laid end to end along the dimension named above; an argument that names none is the same for every part. Nothing has to cross between parts.
Inputs may be any that keep to these rules, and one draw needn't show every extreme that they name: `neighbours`: block index = x column * 16 + row. Row b lists b itself, then a block of the next x column, a block of the previous x column (columns wrap around), and two blocks of its own column. The pattern is symmetric: c stands in slot 1 of b exactly when b stands in slot 2 of c, and in slot 3 of b exactly when b stands in slot 4 of c. contact[s] is a block of x column s. sigma holds a complex symmetric matrix: part g of entry (i, j) equals part g of entry (j, i).
All inputs are finite; a program needn't handle non-finite values.
Results may differ from the reference program's by a relative error of at most 0.0058.
Values may be sent and summed in bfloat16 or wider, within the bound.
No kernel may reach another device: no remote copies, remote signals or barrier semaphores. Data moves between devices by JAX's collectives and lax.ppermute only.
A program may use at most 192 MiB of HBM per device.

```python
import jax
import jax.numpy as jnp
from jax import lax

BO = 64
NNZ = 5
POLES = 8
ITERS = 2
CONTACT = 128
NYB = 16
NBLK = 2048
CO = 8192


def bond_pattern(key):
    key_right, key_column = jax.random.split(key, 2)
    right_perm = jax.vmap(lambda sub_key: jax.random.permutation(sub_key, NYB))(jax.random.split(key_right, CONTACT))
    column_perm = jax.vmap(lambda sub_key: jax.random.permutation(sub_key, NYB))(jax.random.split(key_column, CONTACT))
    right_inverse = jnp.argsort(right_perm, axis=1)
    column_inverse = jnp.argsort(column_perm, axis=1)
    row_ids = jnp.arange(NYB, dtype=jnp.int32)
    column_ids = jnp.arange(CONTACT, dtype=jnp.int32)
    self_index = column_ids[:, None] * NYB + row_ids[None, :]
    right_index = (column_ids[:, None] + 1) % CONTACT * NYB + right_perm
    left_columns = (column_ids - 1) % CONTACT
    left_index = left_columns[:, None] * NYB + right_inverse[left_columns]
    upper_index = column_ids[:, None] * NYB + column_perm
    lower_index = column_ids[:, None] * NYB + column_inverse
    stacked = jnp.stack([self_index, right_index, left_index, upper_index, lower_index], axis=-1)
    return stacked.reshape(NBLK, NNZ).astype(jnp.int32)


def adjoint_blocks(blocks):
    return jnp.stack([jnp.swapaxes(blocks[:, 0], 1, 2), -jnp.swapaxes(blocks[:, 1], 1, 2)], axis=1)


def hermitian_slots(pattern, raw_values, shift):
    diag_raw = raw_values[0]
    right_raw = raw_values[1]
    column_raw = raw_values[2]
    self_block = 0.5 * (diag_raw + adjoint_blocks(diag_raw))
    identity = jnp.eye(BO, dtype=jnp.float32)
    self_block = self_block + shift * jnp.stack([identity, jnp.zeros_like(identity)])[None]
    left_block = adjoint_blocks(right_raw)[pattern[:, 2]]
    lower_block = adjoint_blocks(column_raw)[pattern[:, 4]]
    slots = jnp.stack([self_block, right_raw, left_block, column_raw, lower_block], axis=1)
    return jnp.transpose(slots, (0, 1, 3, 2, 4)).reshape(NBLK, NNZ, BO, 2 * BO)


def drawn_pole(key):
    return jax.random.randint(key, (), 0, POLES, dtype=jnp.int32)


def draw_neighbours(key, part):
    return bond_pattern(key)


def draw_ham(key, part):
    pattern = bond_pattern(key)
    key = jax.random.fold_in(key, 11)
    value_shape = (3, NBLK, 2, BO, BO)
    raw_values = jax.random.normal(key, value_shape, jnp.float32)
    raw_values = raw_values * (1.0 / (NNZ * 2 * BO) ** 0.5)
    return hermitian_slots(pattern, raw_values, 0.0).astype(jnp.bfloat16)


def draw_ovl(key, part):
    pattern = bond_pattern(key)
    key = jax.random.fold_in(key, 13)
    value_shape = (3, NBLK, 2, BO, BO)
    raw_values = jax.random.normal(key, value_shape, jnp.float32)
    raw_values = raw_values * (0.3 / (NNZ * 2 * BO) ** 0.5)
    return hermitian_slots(pattern, raw_values, 1.0).astype(jnp.bfloat16)


def draw_sigma(key, part):
    key = jax.random.fold_in(key, 23)
    value_shape = (2, CO, CO)
    raw_values = jax.random.normal(key, value_shape, jnp.float32)
    symmetric = (raw_values + jnp.swapaxes(raw_values, 1, 2)) * (0.7 / (4.0 * CO) ** 0.5)
    arranged = jnp.transpose(symmetric.reshape(2, CO, CONTACT, BO), (1, 2, 0, 3))
    return arranged.reshape(CO, CONTACT, 2 * BO).astype(jnp.bfloat16)


def draw_rhs(key, part):
    key = jax.random.fold_in(key, 37)
    column_pos = (jnp.arange(NBLK) // NYB).astype(jnp.float32) / (CONTACT - 1)
    value_shape = (NBLK, POLES, 2 * BO)
    raw_values = jax.random.normal(key, value_shape, jnp.float32)
    growth = 0.5 * 3.0 ** column_pos
    return raw_values * growth[:, None, None]


def draw_contact(key, part):
    key = jax.random.fold_in(key, 41)
    row_offsets = jax.random.randint(key, (CONTACT,), 0, NYB, dtype=jnp.int32)
    row_offsets = row_offsets.at[0].set(0).at[CONTACT - 1].set(NYB - 1)
    return (jnp.arange(CONTACT, dtype=jnp.int32) * NYB + row_offsets).astype(jnp.int32)


def draw_pole_real(key, part):
    chosen = drawn_pole(key)
    key = jax.random.fold_in(key, 53)
    key_wide, key_near = jax.random.split(key, 2)
    spread_values = jax.random.uniform(key_wide, (POLES,), jnp.float32, -1.0, 1.0)
    near_values = jax.random.uniform(key_near, (POLES,), jnp.float32, -0.03, 0.03)
    return jnp.where(jnp.arange(POLES, dtype=jnp.int32) == chosen, near_values, spread_values)


def draw_pole_imag(key, part):
    chosen = drawn_pole(key)
    key = jax.random.fold_in(key, 59)
    key_wide, key_near = jax.random.split(key, 2)
    log_values = jax.random.uniform(key_wide, (POLES,), jnp.float32, jnp.log(0.2), jnp.log(1.5))
    spread_values = jnp.clip(jnp.exp(log_values), 0.2, 1.5)
    near_values = jax.random.uniform(key_near, (POLES,), jnp.float32, 0.2, 0.21)
    return jnp.where(jnp.arange(POLES, dtype=jnp.int32) == chosen, near_values, spread_values)


def setup_inputs(seed: int = 0, part: int = 0) -> dict:
    key_of = jax.random.split(jax.random.key(seed), 9)
    part_splits = jax.random.split(jax.random.fold_in(key_of[8], part), 9)
    rhs = draw_rhs(jax.random.fold_in(jax.random.fold_in(key_of[8], part), 71), part)
    ham = draw_ham(jax.random.fold_in(key_of[8], 71), part)
    ovl = draw_ovl(jax.random.fold_in(key_of[8], 71), part)
    sigma = draw_sigma(jax.random.fold_in(key_of[8], 71), part)
    neighbours = draw_neighbours(jax.random.fold_in(key_of[8], 71), part)
    contact = draw_contact(jax.random.fold_in(key_of[8], 71), part)
    pole_real = draw_pole_real(jax.random.fold_in(jax.random.fold_in(key_of[8], part), 71), part)
    pole_imag = draw_pole_imag(jax.random.fold_in(jax.random.fold_in(key_of[8], part), 71), part)
    return {"rhs": rhs, "ham": ham, "ovl": ovl, "sigma": sigma, "neighbours": neighbours, "contact": contact, "pole_real": pole_real, "pole_imag": pole_imag}


FLOOR_SHARE = 0.0625
SMALL_EPS = 1e-6


def split_halves(vector):
    return vector[..., :BO], vector[..., BO:]


def twin_columns(vector):
    real_part, imag_part = split_halves(vector)
    return (jnp.concatenate([real_part, -imag_part], axis=-1),
            jnp.concatenate([imag_part, real_part], axis=-1))


def inner_product(left_vec, right_vec):
    left_re, left_im = split_halves(left_vec)
    right_re, right_im = split_halves(right_vec)
    return (jnp.sum(left_re * right_re + left_im * right_im, axis=(0, 2)),
            jnp.sum(left_re * right_im - left_im * right_re, axis=(0, 2)))


def sum_squares(vector):
    return jnp.sum(vector * vector, axis=(0, 2))


def complex_mul(first_pair, second_pair):
    return (first_pair[0] * second_pair[0] - first_pair[1] * second_pair[1],
            first_pair[0] * second_pair[1] + first_pair[1] * second_pair[0])


def guarded_quotient(numerator, denominator, bound_sq):
    scaled = complex_mul(numerator, (denominator[0], -denominator[1]))
    size_sq = jnp.maximum(denominator[0] * denominator[0] + denominator[1] * denominator[1], FLOOR_SHARE * bound_sq)
    return (scaled[0] / size_sq, scaled[1] / size_sq)


def pole_scale(factor, vector):
    vec_re, vec_im = split_halves(vector)
    fac_re = factor[0][:, None]
    fac_im = factor[1][:, None]
    return jnp.concatenate([fac_re * vec_re - fac_im * vec_im, fac_re * vec_im + fac_im * vec_re], axis=-1)


def apply_matrix(vector, ham, ovl, sigma, neighbours, contact, pole_real, pole_imag):
    rounded = lax.optimization_barrier(vector.astype(jnp.bfloat16)).astype(jnp.float32)
    near_rows = rounded[neighbours]
    front_half, back_half = twin_columns(near_rows)
    wide_rows = jnp.stack([front_half, back_half], axis=2)
    ham_part = jnp.einsum('bkhpc,bkic->bphi', wide_rows, ham.astype(jnp.float32)).reshape(NBLK, POLES, 2 * BO)
    ovl_part = jnp.einsum('bkhpc,bkic->bphi', wide_rows, ovl.astype(jnp.float32)).reshape(NBLK, POLES, 2 * BO)
    contact_vec = rounded[contact]
    front_half, back_half = twin_columns(contact_vec)
    contact_wide = jnp.stack([front_half, back_half], axis=0)
    sigma_four = sigma.astype(jnp.float32).reshape(CONTACT, BO, CONTACT, 2 * BO)
    contact_part = jnp.einsum('losc,hspc->lpho', sigma_four, contact_wide).reshape(CONTACT, POLES, 2 * BO)
    image_vec = pole_scale((pole_real, pole_imag), ovl_part) - ham_part
    return image_vec.at[contact].add(-contact_part)


def reference(rhs, ham, ovl, sigma, neighbours, contact, pole_real, pole_imag):
    def apply_operator(vector):
        return apply_matrix(vector, ham, ovl, sigma, neighbours, contact, pole_real, pole_imag)

    solution = jnp.zeros_like(rhs)
    residual = rhs
    direction = rhs
    norm_b = sum_squares(rhs)
    rho_now = (norm_b, jnp.zeros_like(norm_b))
    for iteration in range(ITERS):
        image_vec = apply_operator(direction)
        alpha_step = guarded_quotient(rho_now, inner_product(rhs, image_vec), norm_b * sum_squares(image_vec))
        half_step = residual - pole_scale(alpha_step, image_vec)
        turned = apply_operator(half_step)
        turned_half = inner_product(turned, half_step)
        turned_raw = sum_squares(turned)
        turned_sq = turned_raw + SMALL_EPS
        omega_step = (turned_half[0] / turned_sq, turned_half[1] / turned_sq)
        solution = solution + pole_scale(alpha_step, direction) + pole_scale(omega_step, half_step)
        residual = half_step - pole_scale(omega_step, turned)
        if iteration + 1 < ITERS:
            rho_next = inner_product(rhs, residual)
            inverse_omega = guarded_quotient((turned_sq, jnp.zeros_like(turned_sq)), turned_half,
                                             turned_raw * sum_squares(half_step))
            ratio_pair = complex_mul(rho_next, complex_mul(alpha_step, inverse_omega))
            rho_size = rho_now[0] * rho_now[0] + rho_now[1] * rho_now[1]
            beta_step = complex_mul(ratio_pair, (rho_now[0] / rho_size, -rho_now[1] / rho_size))
            direction = residual + pole_scale(beta_step, direction - pole_scale(omega_step, image_vec))
            rho_now = rho_next
    return solution, residual
```

```python
import jax
import jax.numpy as jnp
from jax import lax
from jax.experimental import pallas as pl
from jax.experimental.pallas import tpu as pltpu
from jax.sharding import PartitionSpec as P

BO = 64
NYB = 16
NNZ = 5
CONTACT = 128
LANES = 2 * BO
TILE = 16
FLOOR_SHARE = 0.0625
SMALL_EPS = 1e-06
F32 = jnp.float32
BF16 = jnp.bfloat16
VMEM = pl.BlockSpec(memory_space=pltpu.VMEM)
SMEM = pl.BlockSpec(memory_space=pltpu.SMEM)


def dot_nt(left, right):
    return lax.dot_general(left, right, (((1,), (1,)), ((), ())), preferred_element_type=F32)


def swap_halves(vec):
    return pltpu.roll(vec, BO, axis=vec.ndim - 1)


def half_sign(ndim):
    lane = lax.broadcasted_iota(jnp.int32, (1,) * (ndim - 1) + (LANES,), ndim - 1)
    return jnp.where(lane < BO, -1.0, 1.0).astype(F32)


def scale(factor, vec):
    fac_re = factor[0]
    fac_im = factor[1] * half_sign(2)
    return fac_re * vec + fac_im * swap_halves(vec)


def complex_mul(a, b):
    return (a[0] * b[0] - a[1] * b[1], a[0] * b[1] + a[1] * b[0])


def guarded_quotient(num, den, bound_sq):
    top = complex_mul(num, (den[0], -den[1]))
    size = jnp.maximum(den[0] * den[0] + den[1] * den[1], FLOOR_SHARE * bound_sq)
    return (top[0] / size, top[1] / size)


def spread(column):
    return jnp.broadcast_to(column, (column.shape[0], LANES))


def pack_columns(columns):
    poles = columns[0].shape[0]
    lane = lax.broadcasted_iota(jnp.int32, (poles, LANES), 1)
    packed = jnp.zeros((poles, LANES), F32)
    for index, column in enumerate(columns):
        packed = jnp.where(lane == index, column, packed)
    return packed


def take_columns(packed, count):
    return [spread(packed[:, index : index + 1]) for index in range(count)]


def lane_sum(vec):
    return jnp.sum(vec, axis=1, keepdims=True)


def store_wide(wide, start, rows, vec):
    lane = lax.broadcasted_iota(jnp.int32, (1, 1, LANES), 2)
    front = jnp.where(lane < BO, vec, -vec)
    wide[pl.ds(start, rows)] = jnp.concatenate([front, swap_halves(vec)], axis=1).astype(BF16)


def chunk_of(partner, me, count):
    slot = jnp.bitwise_xor(partner, me)
    inner = jnp.right_shift(slot, 1)
    y_bit = jnp.bitwise_and(inner, 1)
    return jnp.bitwise_and(slot, 1), y_bit * (count // 4) + jnp.right_shift(inner, 1)


def gathered_sums(near_side, far_side, row):
    total = None
    for index in range(near_side.shape[0]):
        pair = near_side[index, row] + far_side[index, row]
        total = pair if total is None else total + pair
    return total


def place_gathered(target, offset, me, near_side, far_side, cols):
    half = near_side.shape[0]
    for index in range(half):
        y_bit, z_part = index // (half // 2), index % (half // 2)
        partner = jnp.bitwise_xor(me, 2 * y_bit + 4 * z_part)
        target[pl.ds(offset + partner * cols, cols)] = near_side[index, :cols]
        partner = jnp.bitwise_xor(partner, 1)
        target[pl.ds(offset + partner * cols, cols)] = far_side[index, :cols]


def over_rows(count, step, body):
    def run(index, carry):
        body(pl.multiple_of(index * step, step))
        return carry

    lax.fori_loop(0, count // step, run, 0)


def sum_rows(count, step, body, terms, poles):
    def run(index, carry):
        parts = body(pl.multiple_of(index * step, step))
        return tuple(c + jnp.sum(p, axis=0) for c, p in zip(carry, parts))

    zero = jnp.zeros((poles, LANES), F32)
    return lax.fori_loop(0, count // step, run, (zero,) * terms)


def fill_extended(ext, low, own, high, me, near_side, far_side, cols):
    blocks = own.shape[0]
    ext[0:NYB] = low[...]
    ext[NYB : NYB + blocks] = own[...]
    ext[NYB + blocks : 2 * NYB + blocks] = high[...]
    place_gathered(ext, 2 * NYB + blocks, me, near_side, far_side, cols)


def apply_operator(near, spots, poles_ref, wide, ham, ovl, sigma, acc, image):
    blocks = image.shape[0]
    poles = image.shape[1]
    cols = spots.shape[0]
    first_contact = blocks + 2 * NYB
    z_re, z_im = take_columns(poles_ref[...], 2)
    left = lax.broadcasted_iota(jnp.int32, (poles, LANES), 1) < BO

    def one_block(result, b):
        top, low = result[:poles], result[poles:]
        ham_part = jnp.where(left, top, swap_halves(low))
        ovl_part = jnp.where(left, swap_halves(top), low)
        image[b] = scale((z_re, z_im), ovl_part) - ham_part

    unroll = min(16, blocks // 2)

    def sparse_step(group, carry):
        for j in range(unroll):
            b = group * (2 * unroll) + 2 * j
            vectors, matrices = [], []
            for q in range(2):
                vectors.append(
                    jnp.concatenate([wide[near[b + q, k]] for k in range(NNZ)], axis=1)
                )
                for matrix in (ham, ovl):
                    matrices.append(
                        jnp.concatenate([matrix[b + q, k] for k in range(NNZ)], axis=1)
                    )
            result = dot_nt(jnp.concatenate(vectors, axis=0), jnp.concatenate(matrices, axis=0))
            for q in range(2):
                one_block(
                    result[2 * poles * q : 2 * poles * (q + 1), LANES * q : LANES * (q + 1)], b + q
                )
        return carry

    lax.fori_loop(0, blocks // (2 * unroll), sparse_step, 0)

    rows = sigma.shape[0]
    group_rows = 64
    width = TILE * 2 * poles
    row_t = lax.broadcasted_iota(jnp.int32, (TILE, width), 0)
    col_t = lax.broadcasted_iota(jnp.int32, (TILE, width), 1) // (2 * poles)
    keep = (row_t == col_t)[None]
    for group in range(rows // group_rows):
        total = None
        for pair in range(CONTACT // (2 * TILE)):
            slabs, vectors = [], []
            for side in range(2):
                first = (2 * pair + side) * TILE
                slab = sigma[group * group_rows : (group + 1) * group_rows, first : first + TILE]
                slabs.append(slab.reshape(group_rows * TILE, LANES))
                vectors.append(
                    wide[first_contact + first : first_contact + first + TILE].reshape(width, LANES)
                )
            part = dot_nt(jnp.concatenate(slabs, axis=1), jnp.concatenate(vectors, axis=1))
            total = part if total is None else total + part
        kept = jnp.where(keep, total.reshape(group_rows, TILE, width), 0.0)
        acc[group * group_rows : (group + 1) * group_rows] = jnp.sum(kept, axis=1)
    fold_row = lax.broadcasted_iota(jnp.int32, (2 * poles, width), 0)
    fold_col = lax.broadcasted_iota(jnp.int32, (2 * poles, width), 1) % (2 * poles)
    fold = jnp.where(fold_row == fold_col, 1.0, 0.0).astype(BF16)
    rest = acc[...]
    folded = None
    for _ in range(3):
        piece = rest.astype(BF16)
        part = dot_nt(fold, piece)
        folded = part if folded is None else folded + part
        rest = rest - piece.astype(F32)
    for l in range(cols):
        contact_part = jnp.concatenate(
            [
                folded[:poles, BO * l : BO * (l + 1)],
                folded[poles:, BO * l : BO * (l + 1)],
            ],
            axis=1,
        )
        spot = spots[l]
        image[spot] = image[spot] - contact_part


def store_chunk(chunk, spots, image, sums):
    cols = spots.shape[0]
    for l in range(cols):
        chunk[l] = image[spots[l]]
    chunk[cols] = sums


def inner_terms(a, c):
    return a * c, a * swap_halves(c)


def inner_pair(re_acc, im_acc):
    return lane_sum(re_acc), lane_sum(im_acc * -half_sign(2))


def first_kernel(
    me_ref, near, spots, poles_ref, own, low, high, near_side, far_side, ham, ovl, sigma,
    rhs_ext, image, chunk, wide, acc,
):
    blocks, poles = own.shape[0], own.shape[1]
    fill_extended(rhs_ext, low, own, high, me_ref[0], near_side, far_side, spots.shape[0])
    over_rows(rhs_ext.shape[0], TILE, lambda s: store_wide(wide, s, TILE, rhs_ext[pl.ds(s, TILE)]))
    apply_operator(near, spots, poles_ref, wide, ham, ovl, sigma, acc, image)

    def terms(s):
        b, v = own[pl.ds(s, TILE)], image[pl.ds(s, TILE)]
        return (b * b, *inner_terms(b, v), v * v)

    bb, bv_re, bv_im, vv = sum_rows(blocks, TILE, terms, 4, poles)
    store_chunk(
        chunk, spots, image, pack_columns([lane_sum(bb), *inner_pair(bv_re, bv_im), lane_sum(vv)])
    )


def second_kernel(
    me_ref, near, spots, poles_ref, rhs_ext, own, low, high, near_side, far_side, ham, ovl, sigma,
    image_ext, half_ext, turned, chunk, scalars, wide, acc,
):
    blocks, poles = own.shape[0], own.shape[1]
    cols = spots.shape[0]
    fill_extended(image_ext, low, own, high, me_ref[0], near_side, far_side, cols)
    norm_b, bv_re, bv_im, vv = take_columns(gathered_sums(near_side, far_side, cols), 4)
    alpha = guarded_quotient((norm_b, jnp.zeros_like(norm_b)), (bv_re, bv_im), norm_b * vv)
    scalars[0] = norm_b
    scalars[1] = alpha[0]
    scalars[2] = alpha[1]

    def update(s):
        half = rhs_ext[pl.ds(s, TILE)] - scale(alpha, image_ext[pl.ds(s, TILE)])
        half_ext[pl.ds(s, TILE)] = half
        store_wide(wide, s, TILE, half)

    over_rows(half_ext.shape[0], TILE, update)
    apply_operator(near, spots, poles_ref, wide, ham, ovl, sigma, acc, turned)

    def terms(s):
        b = rhs_ext[pl.ds(NYB + s, TILE)]
        h = half_ext[pl.ds(NYB + s, TILE)]
        t = turned[pl.ds(s, TILE)]
        return (*inner_terms(t, h), t * t, h * h, *inner_terms(b, h), *inner_terms(b, t))

    th_re, th_im, tt, hh, bh_re, bh_im, bt_re, bt_im = sum_rows(blocks, TILE, terms, 8, poles)
    columns = [
        *inner_pair(th_re, th_im), lane_sum(tt), lane_sum(hh),
        *inner_pair(bh_re, bh_im), *inner_pair(bt_re, bt_im),
    ]
    store_chunk(chunk, spots, turned, pack_columns(columns))


def third_kernel(
    me_ref, near, spots, poles_ref, scalars, rhs_ext, image_ext, half_ext, own, low, high,
    near_side, far_side, ham, ovl, sigma,
    residual_own, direction_own, residual_rem, direction_rem, iterate, image, chunk, rho_out,
    turned_ext, wide, acc,
):
    blocks, poles = own.shape[0], own.shape[1]
    cols = spots.shape[0]
    fill_extended(turned_ext, low, own, high, me_ref[0], near_side, far_side, cols)
    sums = take_columns(gathered_sums(near_side, far_side, cols), 8)
    th, tt, hh, bh, bt = (sums[0], sums[1]), sums[2], sums[3], (sums[4], sums[5]), (sums[6], sums[7])
    norm_b, alpha = scalars[0], (scalars[1], scalars[2])
    turned_sq = tt + SMALL_EPS
    omega = (th[0] / turned_sq, th[1] / turned_sq)
    minus = complex_mul(omega, bt)
    rho_next = (bh[0] - minus[0], bh[1] - minus[1])
    zeros = jnp.zeros_like(tt)
    inverse_omega = guarded_quotient((turned_sq, zeros), th, tt * hh)
    ratio = complex_mul(rho_next, complex_mul(alpha, inverse_omega))
    beta = (ratio[0] / norm_b, ratio[1] / norm_b)
    rho_out[0] = rho_next[0]
    rho_out[1] = rho_next[1]
    rho_out[2] = norm_b

    def update(s):
        half = half_ext[pl.ds(s, TILE)]
        residual = half - scale(omega, turned_ext[pl.ds(s, TILE)])
        old = rhs_ext[pl.ds(s, TILE)]
        direction = residual + scale(beta, old - scale(omega, image_ext[pl.ds(s, TILE)]))
        store_wide(wide, s, TILE, direction)
        return residual, direction

    def update_own(s):
        residual, direction = update(NYB + s)
        residual_own[pl.ds(s, TILE)] = residual
        direction_own[pl.ds(s, TILE)] = direction
        iterate[pl.ds(s, TILE)] = scale(alpha, rhs_ext[pl.ds(NYB + s, TILE)]) + scale(
            omega, half_ext[pl.ds(NYB + s, TILE)]
        )

    def update_rest(source, target):
        residual, direction = update(source)
        residual_rem[pl.ds(target, TILE)] = residual
        direction_rem[pl.ds(target, TILE)] = direction

    over_rows(blocks, TILE, update_own)
    update_rest(0, 0)
    over_rows(NYB + CONTACT, TILE, lambda s: update_rest(NYB + blocks + s, NYB + s))
    apply_operator(near, spots, poles_ref, wide, ham, ovl, sigma, acc, image)

    def terms(s):
        b, v = rhs_ext[pl.ds(NYB + s, TILE)], image[pl.ds(s, TILE)]
        return (*inner_terms(b, v), v * v)

    bv_re, bv_im, vv = sum_rows(blocks, TILE, terms, 3, poles)
    store_chunk(chunk, spots, image, pack_columns([*inner_pair(bv_re, bv_im), lane_sum(vv)]))


def fourth_kernel(
    me_ref, near, spots, poles_ref, rho_in, residual_own, direction_own, residual_rem,
    direction_rem, iterate_in, own, low, high, near_side, far_side, ham, ovl, sigma,
    half_own, turned, iterate, sums_out, contact_image, wide, acc,
):
    blocks, poles = own.shape[0], own.shape[1]
    cols = spots.shape[0]
    place_gathered(contact_image, 0, me_ref[0], near_side, far_side, cols)
    bv_re, bv_im, vv = take_columns(gathered_sums(near_side, far_side, cols), 3)
    norm_b = rho_in[2]
    alpha = guarded_quotient((rho_in[0], rho_in[1]), (bv_re, bv_im), norm_b * vv)

    def update_own(s):
        here = pl.ds(s, TILE)
        half = residual_own[here] - scale(alpha, own[here])
        half_own[here] = half
        iterate[here] = iterate_in[here] + scale(alpha, direction_own[here])
        store_wide(wide, NYB + s, TILE, half)

    over_rows(blocks, TILE, update_own)
    store_wide(wide, 0, NYB, residual_rem[0:NYB] - scale(alpha, low[...]))
    store_wide(
        wide, NYB + blocks, NYB, residual_rem[NYB : 2 * NYB] - scale(alpha, high[...])
    )

    def update_contact(s):
        half = residual_rem[pl.ds(2 * NYB + s, TILE)] - scale(alpha, contact_image[pl.ds(s, TILE)])
        store_wide(wide, 2 * NYB + blocks + s, TILE, half)

    over_rows(CONTACT, TILE, update_contact)
    apply_operator(near, spots, poles_ref, wide, ham, ovl, sigma, acc, turned)

    def terms(s):
        h, t = half_own[pl.ds(s, TILE)], turned[pl.ds(s, TILE)]
        return (*inner_terms(t, h), t * t)

    th_re, th_im, tt = sum_rows(blocks, TILE, terms, 3, poles)
    sums_out[0] = pack_columns([*inner_pair(th_re, th_im), lane_sum(tt)])


def last_kernel(near_side, far_side, half_own, turned, iterate, solution_out, residual_out):
    th_re, th_im, tt = take_columns(gathered_sums(near_side, far_side, 0), 3)
    turned_sq = tt + SMALL_EPS
    omega = (th_re / turned_sq, th_im / turned_sq)

    def update(s):
        here = pl.ds(s, TILE)
        half = half_own[here]
        solution_out[here] = iterate[here] + scale(omega, half)
        residual_out[here] = half - scale(omega, turned[here])

    over_rows(half_own.shape[0], TILE, update)


def local(rhs, ham, ovl, sigma, neighbours, contact, pole_real, pole_imag):
    blocks, poles = rhs.shape[0], rhs.shape[1]
    cols = contact.shape[0]
    count = lax.axis_size("gx")
    me = lax.axis_index("gx")
    first_block = me * blocks
    near = (neighbours - first_block + NYB) % (blocks * count)
    spots = contact - first_block
    me_ref = jnp.reshape(me, (1,)).astype(jnp.int32)
    lane = jnp.arange(LANES)[None, :]
    poles_ref = jnp.where(lane == 0, pole_real[:, None], pole_imag[:, None])
    ext = blocks + 2 * NYB + CONTACT

    def flip(value, mask):
        return lax.ppermute(value, "gx", [(i, i ^ mask) for i in range(count)])

    def gather(chunk):
        parts = [chunk] + [flip(chunk, mask) for mask in range(4, count, 4)]
        line = jnp.stack(parts)
        plane = jnp.concatenate([line, flip(line, 2)])
        return plane, flip(plane, 1)

    def halo(vec):
        forward = [(i, (i + 1) % count) for i in range(count)]
        backward = [(i, (i - 1) % count) for i in range(count)]
        low = lax.ppermute(vec[blocks - NYB :], "gx", forward)
        high = lax.ppermute(vec[:NYB], "gx", backward)
        return low, high

    def vec_shape(rows):
        return jax.ShapeDtypeStruct((rows, poles, LANES), F32)

    def call(kernel, inputs, out_rows, scratch, name):
        scalars = 3 if scratch is not None else 0
        extra = [] if scratch is None else [pltpu.VMEM((r, poles, LANES), F32) for r in scratch]
        if scratch is not None:
            extra += [
                pltpu.VMEM((ext, 2 * poles, LANES), BF16),
                pltpu.VMEM((sigma.shape[0], TILE * 2 * poles), F32),
            ]
        return pl.pallas_call(
            kernel,
            in_specs=[SMEM] * scalars + [VMEM] * (len(inputs) - scalars),
            out_specs=[VMEM] * len(out_rows),
            out_shape=[vec_shape(rows) for rows in out_rows],
            scratch_shapes=extra,
            compiler_params=pltpu.CompilerParams(vmem_limit_bytes=12 << 20),
            name=name,
        )(*inputs)

    fixed = (me_ref, near, spots, poles_ref)
    mats = tuple(pltpu.with_memory_space_constraint(m, pltpu.VMEM) for m in (ham, ovl, sigma))
    rows = cols + 1

    own_contact = jnp.concatenate([rhs[spots], jnp.zeros((1, poles, LANES), F32)])
    rhs_ext, image, chunk = call(
        first_kernel,
        (*fixed, rhs, *halo(rhs), *gather(own_contact), *mats),
        [ext, blocks, rows], [], "first",
    )
    image_ext, half_ext, turned, chunk, scalars = call(
        second_kernel,
        (*fixed, rhs_ext, image, *halo(image), *gather(chunk), *mats),
        [ext, ext, blocks, rows, 3], [], "second",
    )
    remote = 2 * NYB + CONTACT
    res_own, dir_own, res_rem, dir_rem, iterate, image, chunk, rho = call(
        third_kernel,
        (*fixed, scalars, rhs_ext, image_ext, half_ext, turned, *halo(turned), *gather(chunk), *mats),
        [blocks, blocks, remote, remote, blocks, blocks, rows, 3], [ext], "third",
    )
    half_own, turned, iterate, sums = call(
        fourth_kernel,
        (*fixed, rho, res_own, dir_own, res_rem, dir_rem, iterate, image, *halo(image),
         *gather(chunk), *mats),
        [blocks, blocks, blocks, 1], [CONTACT], "fourth",
    )
    out = call(last_kernel, (*gather(sums), half_own, turned, iterate), [blocks, blocks], None, "last")
    return (out[0], out[1])


def solution(mesh):
    return jax.shard_map(
        local,
        mesh=mesh,
        in_specs=(
            P("gx", "grp", None),
            P("gx", None, None, None),
            P("gx", None, None, None),
            P("gx", None, None),
            P("gx", None),
            P("gx"),
            P("grp"),
            P("grp"),
        ),
        out_specs=(P("gx", "grp", None), P("gx", "grp", None)),
        check_vma=False,
    )
```

```python
import jax
import jax.numpy as jnp
from jax import lax
from jax.experimental import pallas as pl
from jax.experimental.pallas import tpu as pltpu
from jax.sharding import PartitionSpec as P

BO = 64
NYB = 16
NNZ = 5
CONTACT = 128
LANES = 2 * BO
TILE = 16
FLOOR_SHARE = 0.0625
SMALL_EPS = 1e-06
F32 = jnp.float32
BF16 = jnp.bfloat16
VMEM = pl.BlockSpec(memory_space=pltpu.VMEM)
SMEM = pl.BlockSpec(memory_space=pltpu.SMEM)


def dot_nt(left, right):
    return lax.dot_general(left, right, (((1,), (1,)), ((), ())), preferred_element_type=F32)


def swap_halves(vec):
    return pltpu.roll(vec, BO, axis=vec.ndim - 1)


def half_sign(ndim):
    lane = lax.broadcasted_iota(jnp.int32, (1,) * (ndim - 1) + (LANES,), ndim - 1)
    return jnp.where(lane < BO, -1.0, 1.0).astype(F32)


def scale(factor, vec):
    fac_re = factor[0]
    fac_im = factor[1] * half_sign(2)
    return fac_re * vec + fac_im * swap_halves(vec)


def complex_mul(a, b):
    return (a[0] * b[0] - a[1] * b[1], a[0] * b[1] + a[1] * b[0])


def guarded_quotient(num, den, bound_sq):
    top = complex_mul(num, (den[0], -den[1]))
    size = jnp.maximum(den[0] * den[0] + den[1] * den[1], FLOOR_SHARE * bound_sq)
    return (top[0] / size, top[1] / size)


def spread(column):
    return jnp.broadcast_to(column, (column.shape[0], LANES))


def pack_columns(columns):
    poles = columns[0].shape[0]
    lane = lax.broadcasted_iota(jnp.int32, (poles, LANES), 1)
    packed = jnp.zeros((poles, LANES), F32)
    for index, column in enumerate(columns):
        packed = jnp.where(lane == index, column, packed)
    return packed


def take_columns(packed, count):
    return [spread(packed[:, index : index + 1]) for index in range(count)]


def lane_sum(vec):
    return jnp.sum(vec, axis=1, keepdims=True)


def store_wide(wide, start, rows, vec):
    lane = lax.broadcasted_iota(jnp.int32, (1, 1, LANES), 2)
    front = jnp.where(lane < BO, vec, -vec)
    wide[pl.ds(start, rows)] = jnp.concatenate([front, swap_halves(vec)], axis=1).astype(BF16)


def chunk_of(partner, me, count):
    slot = jnp.bitwise_xor(partner, me)
    inner = jnp.right_shift(slot, 1)
    y_bit = jnp.bitwise_and(inner, 1)
    return jnp.bitwise_and(slot, 1), y_bit * (count // 4) + jnp.right_shift(inner, 1)


def gathered_sums(near_side, far_side, row):
    total = None
    for index in range(near_side.shape[0]):
        pair = near_side[index, row] + far_side[index, row]
        total = pair if total is None else total + pair
    return total


def place_gathered(target, offset, me, near_side, far_side, cols):
    half = near_side.shape[0]
    for index in range(half):
        y_bit, z_part = index // (half // 2), index % (half // 2)
        partner = jnp.bitwise_xor(me, 2 * y_bit + 4 * z_part)
        target[pl.ds(offset + partner * cols, cols)] = near_side[index, :cols]
        partner = jnp.bitwise_xor(partner, 1)
        target[pl.ds(offset + partner * cols, cols)] = far_side[index, :cols]


def over_rows(count, step, body):
    def run(index, carry):
        body(pl.multiple_of(index * step, step))
        return carry

    lax.fori_loop(0, count // step, run, 0)


def sum_rows(count, step, body, terms, poles):
    def run(index, carry):
        parts = body(pl.multiple_of(index * step, step))
        return tuple(c + jnp.sum(p, axis=0) for c, p in zip(carry, parts))

    zero = jnp.zeros((poles, LANES), F32)
    return lax.fori_loop(0, count // step, run, (zero,) * terms)


def fill_extended(ext, low, own, high, me, near_side, far_side, cols):
    blocks = own.shape[0]
    ext[0:NYB] = low[...]
    ext[NYB : NYB + blocks] = own[...]
    ext[NYB + blocks : 2 * NYB + blocks] = high[...]
    place_gathered(ext, 2 * NYB + blocks, me, near_side, far_side, cols)


def combine(poles_ref, result):
    poles = poles_ref.shape[0]
    z = take_columns(poles_ref[...], 2)
    left = lax.broadcasted_iota(jnp.int32, (poles, LANES), 1) < BO
    top, low = result[:poles], result[poles:]
    ham_part = jnp.where(left, top, swap_halves(low))
    ovl_part = jnp.where(left, swap_halves(top), low)
    return scale(z, ovl_part) - ham_part


def ovl_base(blocks):
    return blocks * NNZ // 2


def sparse_block(mats, base, pair, index):
    half = index % 2
    return mats[base + NNZ * pair + index // 2, BO * half : BO * (half + 1)]


def sparse_group(near, poles_ref, wide, mats, image, first, count):
    rows = 2 * image.shape[1]
    bases = (0, ovl_base(image.shape[0]))
    for pair in range(count // 2):
        b = first + 2 * pair
        vectors, matrices = [], []
        for q in range(2):
            vectors.append(jnp.concatenate([wide[near[b + q, k]] for k in range(NNZ)], axis=1))
            for base in bases:
                pieces = [
                    sparse_block(mats, base, first // 2 + pair, q * NNZ + k) for k in range(NNZ)
                ]
                matrices.append(jnp.concatenate(pieces, axis=1))
        result = dot_nt(jnp.concatenate(vectors, axis=0), jnp.concatenate(matrices, axis=0))
        for q in range(2):
            image[b + q] = combine(
                poles_ref, result[rows * q : rows * (q + 1), LANES * q : LANES * (q + 1)]
            )


def part_copies(source, mats, base, sem):
    parts = sem.shape[0]
    size = source.shape[0] // parts
    return [
        pltpu.make_async_copy(
            source.at[pl.ds(part * size, size)],
            mats.at[pl.ds(base + part * size, size)],
            sem.at[part],
        )
        for part in range(parts)
    ]


def start_matrices(ham, ovl, sigma, mats, sems):
    blocks = 2 * ham.shape[0] // NNZ
    copies = (
        part_copies(ham, mats, 0, sems[0]),
        part_copies(ovl, mats, ovl_base(blocks), sems[1]),
        part_copies(sigma, mats, blocks * NNZ, sems[2]),
    )
    for ham_copy, ovl_copy in zip(copies[0], copies[1]):
        ham_copy.start()
        ovl_copy.start()
    for copy in copies[2]:
        copy.start()
    return copies


def sparse_part(near, poles_ref, wide, mats, copies, image):
    parts = len(copies[0])
    size = image.shape[0] // parts
    for part in range(parts):
        copies[0][part].wait()
        copies[1][part].wait()
        sparse_group(near, poles_ref, wide, mats, image, part * size, size)


def edge_part(near, poles_ref, wide, mats, image):
    blocks = image.shape[0]
    for first, slot in ((0, 2), (blocks - NYB, 1)):
        for b in range(first, first + NYB):
            pieces = [
                sparse_block(mats, base, b // 2, (b % 2) * NNZ + slot)
                for base in (0, ovl_base(blocks))
            ]
            matrix = jnp.concatenate(pieces, axis=0)
            image[b] = image[b] + combine(poles_ref, dot_nt(wide[near[b, slot]], matrix))


def contact_part(spots, wide, mats, copies, acc, image):
    blocks, poles = image.shape[0], image.shape[1]
    cols = spots.shape[0]
    first_contact = blocks + 2 * NYB
    base = blocks * NNZ
    rows = mats.shape[0] - base
    group_rows = 64
    width = TILE * 2 * poles
    row_t = lax.broadcasted_iota(jnp.int32, (TILE, width), 0)
    col_t = lax.broadcasted_iota(jnp.int32, (TILE, width), 1) // (2 * poles)
    keep = (row_t == col_t)[None]
    for group in range(rows // group_rows):
        copies[group].wait()
        total = None
        for pair in range(CONTACT // (2 * TILE)):
            slabs, vectors = [], []
            for side in range(2):
                first = (2 * pair + side) * TILE
                start = base + group * group_rows
                slab = mats[start : start + group_rows, first : first + TILE]
                slabs.append(slab.reshape(group_rows * TILE, LANES))
                vectors.append(
                    wide[first_contact + first : first_contact + first + TILE].reshape(width, LANES)
                )
            part = dot_nt(jnp.concatenate(slabs, axis=1), jnp.concatenate(vectors, axis=1))
            total = part if total is None else total + part
        kept = jnp.where(keep, total.reshape(group_rows, TILE, width), 0.0)
        acc[group * group_rows : (group + 1) * group_rows] = jnp.sum(kept, axis=1)
    fold_row = lax.broadcasted_iota(jnp.int32, (2 * poles, width), 0)
    fold_col = lax.broadcasted_iota(jnp.int32, (2 * poles, width), 1) % (2 * poles)
    fold = jnp.where(fold_row == fold_col, 1.0, 0.0).astype(BF16)
    rest = acc[...]
    folded = None
    for _ in range(3):
        piece = rest.astype(BF16)
        part = dot_nt(fold, piece)
        folded = part if folded is None else folded + part
        rest = rest - piece.astype(F32)
    for l in range(cols):
        column = slice(BO * l, BO * (l + 1))
        product = jnp.concatenate([folded[:poles, column], folded[poles:, column]], axis=1)
        spot = spots[l]
        image[spot] = image[spot] - product


def apply_operator(near, spots, poles_ref, wide, mats, copies, acc, image):
    sparse_part(near, poles_ref, wide, mats, copies, image)
    contact_part(spots, wide, mats, copies[2], acc, image)


def store_chunk(chunk, low_edge, high_edge, spots, image, sums):
    cols = spots.shape[0]
    blocks = image.shape[0]
    low_edge[...] = image[0:NYB]
    high_edge[...] = image[blocks - NYB : blocks]
    for l in range(cols):
        chunk[l] = image[spots[l]]
    chunk[cols] = sums


def inner_terms(a, c):
    return a * c, a * swap_halves(c)


def inner_pair(re_acc, im_acc):
    return lane_sum(re_acc), lane_sum(im_acc * -half_sign(2))


def prepare_kernel(spots, rhs, chunk, low_edge, high_edge, sem):
    blocks, poles = rhs.shape[0], rhs.shape[1]
    cols = spots.shape[0]
    copies = [pltpu.make_async_copy(rhs.at[spots[l]], chunk.at[l], sem.at[l]) for l in range(cols)]
    copies.append(pltpu.make_async_copy(rhs.at[pl.ds(0, NYB)], low_edge, sem.at[cols]))
    copies.append(
        pltpu.make_async_copy(rhs.at[pl.ds(blocks - NYB, NYB)], high_edge, sem.at[cols + 1])
    )
    for copy in copies:
        copy.start()
    chunk[cols] = jnp.zeros((poles, LANES), F32)
    for copy in copies:
        copy.wait()


def own_kernel(near, poles_ref, own, ham, ovl, image, wide, mats, ham_sem, ovl_sem):
    blocks = own.shape[0]
    copies = (
        part_copies(ham, mats, 0, ham_sem),
        part_copies(ovl, mats, ovl_base(blocks), ovl_sem),
    )
    for ham_copy, ovl_copy in zip(*copies):
        ham_copy.start()
        ovl_copy.start()
    wide[0:NYB] = jnp.zeros((NYB, *wide.shape[1:]), BF16)
    wide[NYB + blocks : 2 * NYB + blocks] = jnp.zeros((NYB, *wide.shape[1:]), BF16)
    over_rows(blocks, TILE, lambda s: store_wide(wide, NYB + s, TILE, own[pl.ds(s, TILE)]))
    sparse_part(near, poles_ref, wide, mats, copies, image)


def first_kernel(
    me_ref, near, spots, poles_ref, own, image_in, low, high, near_side, far_side, ham, ovl, sigma,
    rhs_ext, image, chunk, low_edge, high_edge, wide, acc, mats, *sems,
):
    blocks, poles = own.shape[0], own.shape[1]
    edge_slabs = NYB * NNZ // 2
    edges = []
    for source, base, sem in ((ham, 0, sems[0]), (ovl, ovl_base(blocks), sems[1])):
        for side, start in enumerate((0, (blocks - NYB) * NNZ // 2)):
            edges.append(
                pltpu.make_async_copy(
                    source.at[pl.ds(start, edge_slabs)],
                    mats.at[pl.ds(base + start, edge_slabs)],
                    sem.at[side],
                )
            )
    contact_copies = part_copies(sigma, mats, blocks * NNZ, sems[2])
    for copy in edges + contact_copies:
        copy.start()
    fill_extended(rhs_ext, low, own, high, me_ref[0], near_side, far_side, spots.shape[0])
    store_wide(wide, 0, NYB, low[...])
    over_rows(
        NYB + CONTACT, TILE,
        lambda s: store_wide(wide, NYB + blocks + s, TILE, rhs_ext[pl.ds(NYB + blocks + s, TILE)]),
    )
    image[...] = image_in[...]
    for copy in edges:
        copy.wait()
    edge_part(near, poles_ref, wide, mats, image)
    contact_part(spots, wide, mats, contact_copies, acc, image)

    def terms(s):
        b, v = own[pl.ds(s, TILE)], image[pl.ds(s, TILE)]
        return (b * b, *inner_terms(b, v), v * v)

    bb, bv_re, bv_im, vv = sum_rows(blocks, TILE, terms, 4, poles)
    store_chunk(
        chunk, low_edge, high_edge, spots, image, pack_columns([lane_sum(bb), *inner_pair(bv_re, bv_im), lane_sum(vv)])
    )


def second_kernel(
    me_ref, near, spots, poles_ref, rhs_ext, own, low, high, near_side, far_side, ham, ovl, sigma,
    image_ext, half_ext, turned, chunk, low_edge, high_edge, scalars, wide, acc, mats,
    *sems,
):
    copies = start_matrices(ham, ovl, sigma, mats, sems)
    blocks, poles = own.shape[0], own.shape[1]
    cols = spots.shape[0]
    fill_extended(image_ext, low, own, high, me_ref[0], near_side, far_side, cols)
    norm_b, bv_re, bv_im, vv = take_columns(gathered_sums(near_side, far_side, cols), 4)
    alpha = guarded_quotient((norm_b, jnp.zeros_like(norm_b)), (bv_re, bv_im), norm_b * vv)
    scalars[0] = norm_b
    scalars[1] = alpha[0]
    scalars[2] = alpha[1]

    def update(s):
        half = rhs_ext[pl.ds(s, TILE)] - scale(alpha, image_ext[pl.ds(s, TILE)])
        half_ext[pl.ds(s, TILE)] = half
        store_wide(wide, s, TILE, half)

    over_rows(half_ext.shape[0], TILE, update)
    apply_operator(near, spots, poles_ref, wide, mats, copies, acc, turned)

    def terms(s):
        b = rhs_ext[pl.ds(NYB + s, TILE)]
        h = half_ext[pl.ds(NYB + s, TILE)]
        t = turned[pl.ds(s, TILE)]
        return (*inner_terms(t, h), t * t, h * h, *inner_terms(b, h), *inner_terms(b, t))

    th_re, th_im, tt, hh, bh_re, bh_im, bt_re, bt_im = sum_rows(blocks, TILE, terms, 8, poles)
    columns = [
        *inner_pair(th_re, th_im), lane_sum(tt), lane_sum(hh),
        *inner_pair(bh_re, bh_im), *inner_pair(bt_re, bt_im),
    ]
    store_chunk(chunk, low_edge, high_edge, spots, turned, pack_columns(columns))


def third_kernel(
    me_ref, near, spots, poles_ref, scalars, rhs_ext, image_ext, half_ext, own, low, high,
    near_side, far_side, ham, ovl, sigma,
    residual_own, direction_own, residual_rem, direction_rem, iterate, image, chunk, low_edge,
    high_edge, rho_out, turned_ext, wide, acc, mats, *sems,
):
    copies = start_matrices(ham, ovl, sigma, mats, sems)
    blocks, poles = own.shape[0], own.shape[1]
    cols = spots.shape[0]
    fill_extended(turned_ext, low, own, high, me_ref[0], near_side, far_side, cols)
    sums = take_columns(gathered_sums(near_side, far_side, cols), 8)
    th, tt, hh, bh, bt = (sums[0], sums[1]), sums[2], sums[3], (sums[4], sums[5]), (sums[6], sums[7])
    norm_b, alpha = scalars[0], (scalars[1], scalars[2])
    turned_sq = tt + SMALL_EPS
    omega = (th[0] / turned_sq, th[1] / turned_sq)
    minus = complex_mul(omega, bt)
    rho_next = (bh[0] - minus[0], bh[1] - minus[1])
    zeros = jnp.zeros_like(tt)
    inverse_omega = guarded_quotient((turned_sq, zeros), th, tt * hh)
    ratio = complex_mul(rho_next, complex_mul(alpha, inverse_omega))
    beta = (ratio[0] / norm_b, ratio[1] / norm_b)
    rho_out[0] = rho_next[0]
    rho_out[1] = rho_next[1]
    rho_out[2] = norm_b

    def update(s):
        half = half_ext[pl.ds(s, TILE)]
        residual = half - scale(omega, turned_ext[pl.ds(s, TILE)])
        old = rhs_ext[pl.ds(s, TILE)]
        direction = residual + scale(beta, old - scale(omega, image_ext[pl.ds(s, TILE)]))
        store_wide(wide, s, TILE, direction)
        return residual, direction

    def update_own(s):
        residual, direction = update(NYB + s)
        residual_own[pl.ds(s, TILE)] = residual
        direction_own[pl.ds(s, TILE)] = direction
        iterate[pl.ds(s, TILE)] = scale(alpha, rhs_ext[pl.ds(NYB + s, TILE)]) + scale(
            omega, half_ext[pl.ds(NYB + s, TILE)]
        )

    def update_rest(source, target):
        residual, direction = update(source)
        residual_rem[pl.ds(target, TILE)] = residual
        direction_rem[pl.ds(target, TILE)] = direction

    over_rows(blocks, TILE, update_own)
    update_rest(0, 0)
    over_rows(NYB + CONTACT, TILE, lambda s: update_rest(NYB + blocks + s, NYB + s))
    apply_operator(near, spots, poles_ref, wide, mats, copies, acc, image)

    def terms(s):
        b, v = rhs_ext[pl.ds(NYB + s, TILE)], image[pl.ds(s, TILE)]
        return (*inner_terms(b, v), v * v)

    bv_re, bv_im, vv = sum_rows(blocks, TILE, terms, 3, poles)
    store_chunk(chunk, low_edge, high_edge, spots, image, pack_columns([*inner_pair(bv_re, bv_im), lane_sum(vv)]))


def fourth_kernel(
    me_ref, near, spots, poles_ref, rho_in, residual_own, direction_own, residual_rem,
    direction_rem, iterate_in, own, low, high, near_side, far_side, ham, ovl, sigma,
    half_own, turned, iterate, sums_out, contact_image, wide, acc, mats, *sems,
):
    copies = start_matrices(ham, ovl, sigma, mats, sems)
    blocks, poles = own.shape[0], own.shape[1]
    cols = spots.shape[0]
    place_gathered(contact_image, 0, me_ref[0], near_side, far_side, cols)
    bv_re, bv_im, vv = take_columns(gathered_sums(near_side, far_side, cols), 3)
    norm_b = rho_in[2]
    alpha = guarded_quotient((rho_in[0], rho_in[1]), (bv_re, bv_im), norm_b * vv)

    def update_own(s):
        here = pl.ds(s, TILE)
        half = residual_own[here] - scale(alpha, own[here])
        half_own[here] = half
        iterate[here] = iterate_in[here] + scale(alpha, direction_own[here])
        store_wide(wide, NYB + s, TILE, half)

    over_rows(blocks, TILE, update_own)
    store_wide(wide, 0, NYB, residual_rem[0:NYB] - scale(alpha, low[...]))
    store_wide(
        wide, NYB + blocks, NYB, residual_rem[NYB : 2 * NYB] - scale(alpha, high[...])
    )

    def update_contact(s):
        half = residual_rem[pl.ds(2 * NYB + s, TILE)] - scale(alpha, contact_image[pl.ds(s, TILE)])
        store_wide(wide, 2 * NYB + blocks + s, TILE, half)

    over_rows(CONTACT, TILE, update_contact)
    apply_operator(near, spots, poles_ref, wide, mats, copies, acc, turned)

    def terms(s):
        h, t = half_own[pl.ds(s, TILE)], turned[pl.ds(s, TILE)]
        return (*inner_terms(t, h), t * t)

    th_re, th_im, tt = sum_rows(blocks, TILE, terms, 3, poles)
    sums_out[0] = pack_columns([*inner_pair(th_re, th_im), lane_sum(tt)])


def last_kernel(near_side, far_side, half_own, turned, iterate, solution_out, residual_out):
    th_re, th_im, tt = take_columns(gathered_sums(near_side, far_side, 0), 3)
    turned_sq = tt + SMALL_EPS
    omega = (th_re / turned_sq, th_im / turned_sq)

    def update(s):
        here = pl.ds(s, TILE)
        half = half_own[here]
        solution_out[here] = iterate[here] + scale(omega, half)
        residual_out[here] = half - scale(omega, turned[here])

    over_rows(half_own.shape[0], TILE, update)


def local(rhs, ham, ovl, sigma, neighbours, contact, pole_real, pole_imag):
    blocks, poles = rhs.shape[0], rhs.shape[1]
    cols = contact.shape[0]
    count = lax.axis_size("gx")
    me = lax.axis_index("gx")
    first_block = me * blocks
    near = (neighbours - first_block + NYB) % (blocks * count)
    spots = contact - first_block
    me_ref = jnp.reshape(me, (1,)).astype(jnp.int32)
    lane = jnp.arange(LANES)[None, :]
    poles_ref = jnp.where(lane == 0, pole_real[:, None], pole_imag[:, None])
    ext = blocks + 2 * NYB + CONTACT

    def flip(value, mask):
        return lax.ppermute(value, "gx", [(i, i ^ mask) for i in range(count)])

    def beside_first(rest, size):
        return (*rest[len(rest) - size :], *rest[: len(rest) - size])

    def exchange(chunk, edges=None, beside=()):
        halos = ()
        if edges is not None:
            forward = [(i, (i + 1) % count) for i in range(count)]
            backward = [(i, (i - 1) % count) for i in range(count)]
            halos = (
                lax.ppermute(edges[1], "gx", forward),
                lax.ppermute(edges[0], "gx", backward),
            )
        parts = [chunk] + [flip(chunk, mask) for mask in range(4, count, 4)]
        *rest, line = lax.optimization_barrier((*halos, *beside, jnp.stack(parts)))
        plane = jnp.concatenate([line, flip(line, 2)])
        return (*beside_first(rest, len(beside)), plane, flip(plane, 1))

    def vec_shape(rows):
        return jax.ShapeDtypeStruct((rows, poles, LANES), F32)

    slabs = (ham.reshape(-1, LANES, LANES), ovl.reshape(-1, LANES, LANES), sigma)
    small = pltpu.CompilerParams(vmem_limit_bytes=8 << 20)
    large = pltpu.CompilerParams(vmem_limit_bytes=46 << 20)
    wide = pltpu.VMEM((ext, 2 * poles, LANES), BF16)
    acc = pltpu.VMEM((sigma.shape[0], TILE * 2 * poles), F32)
    held = pltpu.VMEM((sum(m.shape[0] for m in slabs), LANES, LANES), BF16)
    parts = max(2, blocks // 32)
    sems = [pltpu.SemaphoreType.DMA((p,)) for p in (parts, parts, sigma.shape[0] // BO)]
    hbm = pl.BlockSpec(memory_space=pl.ANY)
    fixed = (me_ref, near, spots, poles_ref)
    remote = 2 * NYB + CONTACT
    rows = cols + 1

    def call(kernel, inputs, out_rows, scratch, name):
        scratch = [pltpu.VMEM((r, poles, LANES), F32) for r in scratch]
        return pl.pallas_call(
            kernel,
            in_specs=[SMEM] * 3 + [VMEM] * (len(inputs) - 3) + [hbm] * 3,
            out_specs=[VMEM] * len(out_rows),
            out_shape=[vec_shape(r) for r in out_rows],
            scratch_shapes=[*scratch, wide, acc, held, *sems],
            compiler_params=large,
            name=name,
        )(*inputs, *slabs)

    chunk, *edges = pl.pallas_call(
        prepare_kernel,
        in_specs=[SMEM, pl.BlockSpec(memory_space=pl.ANY)],
        out_specs=[VMEM] * 3,
        out_shape=[vec_shape(rows), vec_shape(NYB), vec_shape(NYB)],
        scratch_shapes=[pltpu.SemaphoreType.DMA((cols + 2,))],
        compiler_params=small,
        name="prepare",
    )(spots, rhs)
    image = pl.pallas_call(
        own_kernel,
        in_specs=[SMEM] + [VMEM] * 2 + [hbm] * 2,
        out_specs=VMEM,
        out_shape=vec_shape(blocks),
        scratch_shapes=[wide, held, *sems[:2]],
        compiler_params=large,
        cost_estimate=pl.CostEstimate(
            flops=2 * 2 * ham.size * 2 * poles,
            bytes_accessed=2 * (2 * ham.size),
            transcendentals=0,
        ),
        name="own",
    )(near, poles_ref, rhs, *slabs[:2])
    rhs_ext, image, chunk, low, high = call(
        first_kernel, (*fixed, rhs, *exchange(chunk, edges, (image,))),
        [ext, blocks, rows, NYB, NYB], [], "first",
    )
    image_ext, half_ext, turned, chunk, low, high, scalars = call(
        second_kernel, (*fixed, rhs_ext, image, *exchange(chunk, (low, high))),
        [ext, ext, blocks, rows, NYB, NYB, 3], [], "second",
    )
    res_own, dir_own, res_rem, dir_rem, iterate, image, chunk, low_edge, high_edge, rho = call(
        third_kernel,
        (*fixed, scalars, rhs_ext, image_ext, half_ext, turned, *exchange(chunk, (low, high))),
        [blocks, blocks, remote, remote, blocks, blocks, rows, NYB, NYB, 3], [ext], "third",
    )
    half_own, turned, iterate, sums = call(
        fourth_kernel,
        (*fixed, rho, res_own, dir_own, res_rem, dir_rem, iterate, image,
         *exchange(chunk, (low_edge, high_edge))),
        [blocks, blocks, blocks, 1], [CONTACT], "fourth",
    )
    return tuple(
        pl.pallas_call(
            last_kernel,
            in_specs=[VMEM] * 5,
            out_specs=[VMEM] * 2,
            out_shape=[vec_shape(blocks)] * 2,
            compiler_params=small,
            name="last",
        )(*exchange(sums), half_own, turned, iterate)
    )


def solution(mesh):
    return jax.shard_map(
        local,
        mesh=mesh,
        in_specs=(
            P("gx", "grp", None),
            P("gx", None, None, None),
            P("gx", None, None, None),
            P("gx", None, None),
            P("gx", None),
            P("gx"),
            P("grp"),
            P("grp"),
        ),
        out_specs=(P("gx", "grp", None), P("gx", "grp", None)),
        check_vma=False,
    )
```

```python
import functools

import jax
import jax.numpy as jnp
from jax import lax
from jax.experimental import pallas as pl
from jax.experimental.pallas import tpu as pltpu
from jax.sharding import PartitionSpec as P

BO = 64
NYB = 16
NNZ = 5
CONTACT = 128
LANES = 2 * BO
TILE = 16
FLOOR_SHARE = 0.0625
SMALL_EPS = 1e-06
F32 = jnp.float32
BF16 = jnp.bfloat16
VMEM = pl.BlockSpec(memory_space=pltpu.VMEM)
SMEM = pl.BlockSpec(memory_space=pltpu.SMEM)


def dot_nt(left, right):
    return lax.dot_general(left, right, (((1,), (1,)), ((), ())), preferred_element_type=F32)


def swap_halves(vec):
    return pltpu.roll(vec, BO, axis=vec.ndim - 1)


def half_sign(ndim):
    lane = lax.broadcasted_iota(jnp.int32, (1,) * (ndim - 1) + (LANES,), ndim - 1)
    return jnp.where(lane < BO, -1.0, 1.0).astype(F32)


def scale(factor, vec):
    fac_re = factor[0]
    fac_im = factor[1] * half_sign(2)
    return fac_re * vec + fac_im * swap_halves(vec)


def complex_mul(a, b):
    return (a[0] * b[0] - a[1] * b[1], a[0] * b[1] + a[1] * b[0])


def guarded_quotient(num, den, bound_sq):
    top = complex_mul(num, (den[0], -den[1]))
    size = jnp.maximum(den[0] * den[0] + den[1] * den[1], FLOOR_SHARE * bound_sq)
    return (top[0] / size, top[1] / size)


def spread(column):
    return jnp.broadcast_to(column, (column.shape[0], LANES))


def pack_columns(columns):
    poles = columns[0].shape[0]
    lane = lax.broadcasted_iota(jnp.int32, (poles, LANES), 1)
    packed = jnp.zeros((poles, LANES), F32)
    for index, column in enumerate(columns):
        packed = jnp.where(lane == index, column, packed)
    return packed


def take_columns(packed, count):
    return [spread(packed[:, index : index + 1]) for index in range(count)]


def lane_sum(vec):
    return jnp.sum(vec, axis=1, keepdims=True)


def store_wide(wide, start, rows, vec):
    lane = lax.broadcasted_iota(jnp.int32, (1, 1, LANES), 2)
    front = jnp.where(lane < BO, vec, -vec)
    wide[pl.ds(start, rows)] = jnp.concatenate([front, swap_halves(vec)], axis=1).astype(BF16)


def chunk_of(partner, me, count):
    slot = jnp.bitwise_xor(partner, me)
    inner = jnp.right_shift(slot, 1)
    y_bit = jnp.bitwise_and(inner, 1)
    return jnp.bitwise_and(slot, 1), y_bit * (count // 4) + jnp.right_shift(inner, 1)


def gathered_sums(near_side, far_side, row):
    total = None
    for index in range(near_side.shape[0]):
        pair = near_side[index, row] + far_side[index, row]
        total = pair if total is None else total + pair
    return total


def place_gathered(target, offset, me, near_side, far_side, cols):
    half = near_side.shape[0]
    for index in range(half):
        y_bit, z_part = index // (half // 2), index % (half // 2)
        partner = jnp.bitwise_xor(me, 2 * y_bit + 4 * z_part)
        target[pl.ds(offset + partner * cols, cols)] = near_side[index, :cols]
        partner = jnp.bitwise_xor(partner, 1)
        target[pl.ds(offset + partner * cols, cols)] = far_side[index, :cols]


def over_rows(count, step, body):
    def run(index, carry):
        body(pl.multiple_of(index * step, step))
        return carry

    lax.fori_loop(0, count // step, run, 0)


def sum_rows(count, step, body, terms, poles):
    def run(index, carry):
        parts = body(pl.multiple_of(index * step, step))
        return tuple(c + jnp.sum(p, axis=0) for c, p in zip(carry, parts))

    zero = jnp.zeros((poles, LANES), F32)
    return lax.fori_loop(0, count // step, run, (zero,) * terms)


def halo_starts(me, blocks):
    odd = jnp.bitwise_and(me, 1)
    return (1 - odd) * (NYB + blocks), odd * (NYB + blocks)


def edge_start(kind, me, blocks):
    odd = jnp.bitwise_and(me, 1)
    return (1 - odd if kind == 0 else odd) * (blocks - NYB)


def fill_extended(ext, partner, own, other, me, near_side, far_side, cols):
    blocks = own.shape[0]
    partner_start, other_start = halo_starts(me, blocks)
    ext[pl.ds(partner_start, NYB)] = partner[...]
    ext[pl.ds(other_start, NYB)] = other[...]
    ext[NYB : NYB + blocks] = own[...]
    place_gathered(ext, 2 * NYB + blocks, me, near_side, far_side, cols)


def combine(poles_ref, result):
    poles = poles_ref.shape[0]
    z = take_columns(poles_ref[...], 2)
    left = lax.broadcasted_iota(jnp.int32, (poles, LANES), 1) < BO
    top, low = result[:poles], result[poles:]
    ham_part = jnp.where(left, top, swap_halves(low))
    ovl_part = jnp.where(left, swap_halves(top), low)
    return scale(z, ovl_part) - ham_part


def ovl_base(blocks):
    return blocks * NNZ // 2


def sparse_block(mats, base, pair, index):
    half = index % 2
    return mats[base + NNZ * pair + index // 2, BO * half : BO * (half + 1)]


def sparse_group(near, poles_ref, wide, mats, blocks, image, first, count, shift=0):
    rows = 2 * image.shape[1]
    bases = (0, ovl_base(blocks))
    for pair in range(count // 2):
        b = first + 2 * pair
        vectors, matrices = [], []
        for q in range(2):
            vectors.append(jnp.concatenate([wide[near[(b + q) * NNZ + k]] for k in range(NNZ)], axis=1))
            for base in bases:
                pieces = [
                    sparse_block(mats, base, first // 2 + pair, q * NNZ + k) for k in range(NNZ)
                ]
                matrices.append(jnp.concatenate(pieces, axis=1))
        result = dot_nt(jnp.concatenate(vectors, axis=0), jnp.concatenate(matrices, axis=0))
        for q in range(2):
            image[b + q - shift] = combine(
                poles_ref, result[rows * q : rows * (q + 1), LANES * q : LANES * (q + 1)]
            )


def part_copy(source, mats, base, sem, part):
    size = source.shape[0] // sem.shape[0]
    return pltpu.make_async_copy(
        source.at[pl.ds(part * size, size)],
        mats.at[pl.ds(base + part * size, size)],
        sem.at[part],
    )


def start_sparse(ham, ovl, mats, sems):
    base = ovl_base(2 * ham.shape[0] // NNZ)
    for part in range(sems[0].shape[0]):
        part_copy(ham, mats, 0, sems[0], part).start()
        part_copy(ovl, mats, base, sems[1], part).start()


def start_sigma(sigma, mats, sem):
    base = mats.shape[0] - sigma.shape[0]
    for part in range(sem.shape[0]):
        part_copy(sigma, mats, base, sem, part).start()


def start_matrices(ham, ovl, sigma, mats, sems):
    start_sparse(ham, ovl, mats, sems)
    start_sigma(sigma, mats, sems[2])


def sparse_part(near, poles_ref, wide, ham, ovl, mats, sems, image):
    parts = sems[0].shape[0]
    blocks = image.shape[0]
    size = blocks // parts

    def step(part, carry):
        part_copy(ham, mats, 0, sems[0], part).wait()
        part_copy(ovl, mats, ovl_base(blocks), sems[1], part).wait()
        sparse_group(near, poles_ref, wide, mats, blocks, image, part * size, size)
        return carry

    lax.fori_loop(0, parts, step, 0)


def edge_part(near, poles_ref, wide, mats, image):
    blocks = image.shape[0]
    for first, slot in ((0, 2), (blocks - NYB, 1)):

        def step(group, carry, first=first, slot=slot):
            for index in range(4):
                pair = first // 2 + 4 * group + index
                for q in range(2):
                    b = 2 * pair + q
                    pieces = [
                        sparse_block(mats, base, pair, q * NNZ + slot)
                        for base in (0, ovl_base(blocks))
                    ]
                    product = dot_nt(wide[near[b * NNZ + slot]], jnp.concatenate(pieces, axis=0))
                    image[b] = image[b] + combine(poles_ref, product)
            return carry

        lax.fori_loop(0, NYB // 8, step, 0)


def contact_part(spots, wide, sigma, mats, sem, acc, image):
    blocks, poles = image.shape[0], image.shape[1]
    cols = spots.shape[0]
    first_contact = blocks + 2 * NYB
    base = blocks * NNZ
    group_rows = sigma.shape[0] // sem.shape[0]
    width = TILE * 2 * poles
    row_t = lax.broadcasted_iota(jnp.int32, (TILE, width), 0)
    col_t = lax.broadcasted_iota(jnp.int32, (TILE, width), 1) // (2 * poles)
    keep = (row_t == col_t)[None]

    def step(group, carry):
        part_copy(sigma, mats, base, sem, group).wait()
        start = base + group * group_rows
        total = None
        for pair in range(CONTACT // (2 * TILE)):
            slabs, vectors = [], []
            for side in range(2):
                first = (2 * pair + side) * TILE
                slab = mats[pl.ds(start, group_rows), first : first + TILE]
                slabs.append(slab.reshape(group_rows * TILE, LANES))
                vectors.append(
                    wide[first_contact + first : first_contact + first + TILE].reshape(width, LANES)
                )
            part = dot_nt(jnp.concatenate(slabs, axis=1), jnp.concatenate(vectors, axis=1))
            total = part if total is None else total + part
        kept = jnp.where(keep, total.reshape(group_rows, TILE, width), 0.0)
        acc[pl.ds(pl.multiple_of(group * group_rows, group_rows), group_rows)] = jnp.sum(kept, axis=1)
        return carry

    lax.fori_loop(0, sem.shape[0], step, 0)
    fold_row = lax.broadcasted_iota(jnp.int32, (2 * poles, width), 0)
    fold_col = lax.broadcasted_iota(jnp.int32, (2 * poles, width), 1) % (2 * poles)
    fold = jnp.where(fold_row == fold_col, 1.0, 0.0).astype(BF16)
    rest = acc[...]
    folded = None
    for _ in range(2):
        piece = rest.astype(BF16)
        part = dot_nt(fold, piece)
        folded = part if folded is None else folded + part
        rest = rest - piece.astype(F32)
    for l in range(cols):
        column = slice(BO * l, BO * (l + 1))
        product = jnp.concatenate([folded[:poles, column], folded[poles:, column]], axis=1)
        spot = spots[l]
        image[spot] = image[spot] - product


def apply_operator(near, spots, poles_ref, wide, ham, ovl, sigma, mats, sems, acc, image):
    sparse_part(near, poles_ref, wide, ham, ovl, mats, sems, image)
    contact_part(spots, wide, sigma, mats, sems[2], acc, image)


def store_chunk(chunk, edge_a, edge_b, me, spots, image, sums):
    cols = spots.shape[0]
    blocks = image.shape[0]
    edge_a[...] = image[pl.ds(edge_start(0, me, blocks), NYB)]
    edge_b[...] = image[pl.ds(edge_start(1, me, blocks), NYB)]
    for l in range(cols):
        chunk[l] = image[spots[l]]
    chunk[cols] = sums


def inner_terms(a, c):
    return a * c, a * swap_halves(c)


def inner_pair(re_acc, im_acc):
    return lane_sum(re_acc), lane_sum(im_acc * -half_sign(2))


def prepare_kernel(me_ref, spots, rhs, chunk, edge_a, edge_b, sem):
    blocks, poles = rhs.shape[0], rhs.shape[1]
    cols = spots.shape[0]
    copies = [pltpu.make_async_copy(rhs.at[spots[l]], chunk.at[l], sem.at[l]) for l in range(cols)]
    for kind, edge in enumerate((edge_a, edge_b)):
        here = pl.ds(edge_start(kind, me_ref[0], blocks), NYB)
        copies.append(pltpu.make_async_copy(rhs.at[here], edge, sem.at[cols + kind]))
    for copy in copies:
        copy.start()
    chunk[cols] = jnp.zeros((poles, LANES), F32)
    for copy in copies:
        copy.wait()


def own_kernel(first, near, poles_ref, own, ham, ovl, image, wide, mats, *sems):
    blocks = own.shape[0]
    parts = sems[0].shape[0]
    size = image.shape[0] // parts
    slabs = size * NNZ // 2
    start = first * NNZ // 2

    def copies(part):
        for source, base, sem in ((ham, 0, sems[0]), (ovl, ovl_base(blocks), sems[1])):
            yield pltpu.make_async_copy(
                source.at[pl.ds(start + part * slabs, slabs)],
                mats.at[pl.ds(base + start + part * slabs, slabs)],
                sem.at[part],
            )

    for part in range(parts):
        for copy in copies(part):
            copy.start()
    wide[0:NYB] = jnp.zeros((NYB, *wide.shape[1:]), BF16)
    wide[NYB + blocks : 2 * NYB + blocks] = jnp.zeros((NYB, *wide.shape[1:]), BF16)
    low = max(0, first - NYB)
    needed = min(blocks, first + image.shape[0] + NYB) - low
    over_rows(
        needed, TILE,
        lambda s: store_wide(wide, NYB + low + s, TILE, own[pl.ds(low + s, TILE)]),
    )

    def step(part, carry):
        for copy in copies(part):
            copy.wait()
        sparse_group(
            near, poles_ref, wide, mats, blocks, image, first + part * size, size, shift=first
        )
        return carry

    lax.fori_loop(0, parts, step, 0)


def first_kernel(
    me_ref, near, spots, poles_ref, own, image_front, image_back, partner, other, near_side, far_side, ham, ovl, sigma,
    rhs_ext, image, chunk, edge_a, edge_b, wide, acc, mats, *sems,
):
    blocks, poles = own.shape[0], own.shape[1]
    edge_slabs = NYB * NNZ // 2
    edges = []
    for source, base, sem in ((ham, 0, sems[0]), (ovl, ovl_base(blocks), sems[1])):
        for side, start in enumerate((0, (blocks - NYB) * NNZ // 2)):
            edges.append(
                pltpu.make_async_copy(
                    source.at[pl.ds(start, edge_slabs)],
                    mats.at[pl.ds(base + start, edge_slabs)],
                    sem.at[side],
                )
            )
    for copy in edges:
        copy.start()
    start_sigma(sigma, mats, sems[2])
    fill_extended(rhs_ext, partner, own, other, me_ref[0], near_side, far_side, spots.shape[0])
    store_wide(wide, 0, NYB, rhs_ext[0:NYB])
    over_rows(
        NYB + CONTACT, TILE,
        lambda s: store_wide(wide, NYB + blocks + s, TILE, rhs_ext[pl.ds(NYB + blocks + s, TILE)]),
    )
    image[0 : blocks // 2] = image_front[...]
    image[blocks // 2 : blocks] = image_back[...]
    for copy in edges:
        copy.wait()
    edge_part(near, poles_ref, wide, mats, image)
    contact_part(spots, wide, sigma, mats, sems[2], acc, image)

    def terms(s):
        b, v = own[pl.ds(s, TILE)], image[pl.ds(s, TILE)]
        return (b * b, *inner_terms(b, v), v * v)

    bb, bv_re, bv_im, vv = sum_rows(blocks, TILE, terms, 4, poles)
    store_chunk(
        chunk, edge_a, edge_b, me_ref[0], spots, image, pack_columns([lane_sum(bb), *inner_pair(bv_re, bv_im), lane_sum(vv)])
    )


def second_kernel(
    me_ref, near, spots, poles_ref, rhs_ext, own, partner, other, near_side, far_side, ham, ovl, sigma,
    image_ext, half_ext, turned, chunk, edge_a, edge_b, scalars, wide, acc, mats,
    *sems,
):
    start_matrices(ham, ovl, sigma, mats, sems)
    blocks, poles = own.shape[0], own.shape[1]
    cols = spots.shape[0]
    fill_extended(image_ext, partner, own, other, me_ref[0], near_side, far_side, cols)
    norm_b, bv_re, bv_im, vv = take_columns(gathered_sums(near_side, far_side, cols), 4)
    alpha = guarded_quotient((norm_b, jnp.zeros_like(norm_b)), (bv_re, bv_im), norm_b * vv)
    scalars[0] = norm_b
    scalars[1] = alpha[0]
    scalars[2] = alpha[1]

    def update(s):
        half = rhs_ext[pl.ds(s, TILE)] - scale(alpha, image_ext[pl.ds(s, TILE)])
        half_ext[pl.ds(s, TILE)] = half
        store_wide(wide, s, TILE, half)

    over_rows(half_ext.shape[0], TILE, update)
    apply_operator(near, spots, poles_ref, wide, ham, ovl, sigma, mats, sems, acc, turned)

    def terms(s):
        b = rhs_ext[pl.ds(NYB + s, TILE)]
        h = half_ext[pl.ds(NYB + s, TILE)]
        t = turned[pl.ds(s, TILE)]
        return (*inner_terms(t, h), t * t, h * h, *inner_terms(b, h), *inner_terms(b, t))

    th_re, th_im, tt, hh, bh_re, bh_im, bt_re, bt_im = sum_rows(blocks, TILE, terms, 8, poles)
    columns = [
        *inner_pair(th_re, th_im), lane_sum(tt), lane_sum(hh),
        *inner_pair(bh_re, bh_im), *inner_pair(bt_re, bt_im),
    ]
    store_chunk(chunk, edge_a, edge_b, me_ref[0], spots, turned, pack_columns(columns))


def third_kernel(
    me_ref, near, spots, poles_ref, scalars, rhs_ext, image_ext, half_ext, own, partner, other,
    near_side, far_side, ham, ovl, sigma,
    residual_own, direction_own, residual_rem, direction_rem, iterate, image, chunk, edge_a,
    edge_b, rho_out, turned_ext, wide, acc, mats, *sems,
):
    start_matrices(ham, ovl, sigma, mats, sems)
    blocks, poles = own.shape[0], own.shape[1]
    cols = spots.shape[0]
    fill_extended(turned_ext, partner, own, other, me_ref[0], near_side, far_side, cols)
    sums = take_columns(gathered_sums(near_side, far_side, cols), 8)
    th, tt, hh, bh, bt = (sums[0], sums[1]), sums[2], sums[3], (sums[4], sums[5]), (sums[6], sums[7])
    norm_b, alpha = scalars[0], (scalars[1], scalars[2])
    turned_sq = tt + SMALL_EPS
    omega = (th[0] / turned_sq, th[1] / turned_sq)
    minus = complex_mul(omega, bt)
    rho_next = (bh[0] - minus[0], bh[1] - minus[1])
    zeros = jnp.zeros_like(tt)
    inverse_omega = guarded_quotient((turned_sq, zeros), th, tt * hh)
    ratio = complex_mul(rho_next, complex_mul(alpha, inverse_omega))
    beta = (ratio[0] / norm_b, ratio[1] / norm_b)
    rho_out[0] = rho_next[0]
    rho_out[1] = rho_next[1]
    rho_out[2] = norm_b

    def update(s):
        half = half_ext[pl.ds(s, TILE)]
        residual = half - scale(omega, turned_ext[pl.ds(s, TILE)])
        old = rhs_ext[pl.ds(s, TILE)]
        direction = residual + scale(beta, old - scale(omega, image_ext[pl.ds(s, TILE)]))
        store_wide(wide, s, TILE, direction)
        return residual, direction

    def update_own(s):
        residual, direction = update(NYB + s)
        residual_own[pl.ds(s, TILE)] = residual
        direction_own[pl.ds(s, TILE)] = direction
        iterate[pl.ds(s, TILE)] = scale(alpha, rhs_ext[pl.ds(NYB + s, TILE)]) + scale(
            omega, half_ext[pl.ds(NYB + s, TILE)]
        )

    def update_rest(source, target):
        residual, direction = update(source)
        residual_rem[pl.ds(target, TILE)] = residual
        direction_rem[pl.ds(target, TILE)] = direction

    over_rows(blocks, TILE, update_own)
    update_rest(0, 0)
    over_rows(NYB + CONTACT, TILE, lambda s: update_rest(NYB + blocks + s, NYB + s))
    apply_operator(near, spots, poles_ref, wide, ham, ovl, sigma, mats, sems, acc, image)

    def terms(s):
        b, v = rhs_ext[pl.ds(NYB + s, TILE)], image[pl.ds(s, TILE)]
        return (*inner_terms(b, v), v * v)

    bv_re, bv_im, vv = sum_rows(blocks, TILE, terms, 3, poles)
    store_chunk(chunk, edge_a, edge_b, me_ref[0], spots, image, pack_columns([*inner_pair(bv_re, bv_im), lane_sum(vv)]))


def fourth_kernel(
    me_ref, near, spots, poles_ref, rho_in, residual_own, direction_own, residual_rem,
    direction_rem, iterate_in, own, partner, other, near_side, far_side, ham, ovl, sigma,
    half_own, turned, iterate, sums_out, contact_image, wide, acc, mats, *sems,
):
    start_matrices(ham, ovl, sigma, mats, sems)
    blocks, poles = own.shape[0], own.shape[1]
    cols = spots.shape[0]
    place_gathered(contact_image, 0, me_ref[0], near_side, far_side, cols)
    bv_re, bv_im, vv = take_columns(gathered_sums(near_side, far_side, cols), 3)
    norm_b = rho_in[2]
    alpha = guarded_quotient((rho_in[0], rho_in[1]), (bv_re, bv_im), norm_b * vv)

    def update_own(s):
        here = pl.ds(s, TILE)
        half = residual_own[here] - scale(alpha, own[here])
        half_own[here] = half
        iterate[here] = iterate_in[here] + scale(alpha, direction_own[here])
        store_wide(wide, NYB + s, TILE, half)

    over_rows(blocks, TILE, update_own)
    for start, image in zip(halo_starts(me_ref[0], blocks), (partner, other)):
        remote = jnp.where(start == 0, 0, NYB)
        half = residual_rem[pl.ds(remote, NYB)] - scale(alpha, image[...])
        store_wide(wide, start, NYB, half)

    def update_contact(s):
        half = residual_rem[pl.ds(2 * NYB + s, TILE)] - scale(alpha, contact_image[pl.ds(s, TILE)])
        store_wide(wide, 2 * NYB + blocks + s, TILE, half)

    over_rows(CONTACT, TILE, update_contact)
    apply_operator(near, spots, poles_ref, wide, ham, ovl, sigma, mats, sems, acc, turned)

    def terms(s):
        h, t = half_own[pl.ds(s, TILE)], turned[pl.ds(s, TILE)]
        return (*inner_terms(t, h), t * t)

    th_re, th_im, tt = sum_rows(blocks, TILE, terms, 3, poles)
    sums_out[0] = pack_columns([*inner_pair(th_re, th_im), lane_sum(tt)])


def last_kernel(near_side, far_side, half_own, turned, iterate, solution_out, residual_out):
    th_re, th_im, tt = take_columns(gathered_sums(near_side, far_side, 0), 3)
    turned_sq = tt + SMALL_EPS
    omega = (th_re / turned_sq, th_im / turned_sq)

    def update(s):
        here = pl.ds(s, TILE)
        half = half_own[here]
        solution_out[here] = iterate[here] + scale(omega, half)
        residual_out[here] = half - scale(omega, turned[here])

    over_rows(half_own.shape[0], TILE, update)


def local(rhs, ham, ovl, sigma, neighbours, contact, pole_real, pole_imag):
    blocks, poles = rhs.shape[0], rhs.shape[1]
    cols = contact.shape[0]
    count = lax.axis_size("gx")
    me = lax.axis_index("gx")
    first_block = me * blocks
    near = ((neighbours - first_block + NYB) % (blocks * count)).reshape(-1)
    spots = contact - first_block
    me_ref = jnp.reshape(me, (1,)).astype(jnp.int32)
    lane = jnp.arange(LANES)[None, :]
    poles_ref = jnp.where(lane == 0, pole_real[:, None], pole_imag[:, None])
    ext = blocks + 2 * NYB + CONTACT

    def flip(value, mask):
        return lax.ppermute(value, "gx", [(i, i ^ mask) for i in range(count)])

    def exchange(chunk, edges=None, beside=()):
        parts = [chunk] + [flip(chunk, mask) for mask in range(4, count, 4)]
        far = ()
        if edges is not None:
            other = [(i, (i + 1 if i % 2 else i - 1) % count) for i in range(count)]
            far = (lax.ppermute(edges[1], "gx", other),)
        early, line = lax.optimization_barrier((beside[:1], jnp.stack(parts)))
        plane = jnp.concatenate([line, flip(line, 2)])
        if edges is None:
            return plane, flip(plane, 1)
        far, late, plane = lax.optimization_barrier((far, beside[1:], plane))
        return (*early, *late, flip(edges[0], 1), *far, plane, flip(plane, 1))

    def vec_shape(rows):
        return jax.ShapeDtypeStruct((rows, poles, LANES), F32)

    slabs = (ham.reshape(-1, LANES, LANES), ovl.reshape(-1, LANES, LANES), sigma)
    small = pltpu.CompilerParams(vmem_limit_bytes=8 << 20)
    large = pltpu.CompilerParams(vmem_limit_bytes=43 << 20)
    wide = pltpu.VMEM((ext, 2 * poles, LANES), BF16)
    acc = pltpu.VMEM((sigma.shape[0], TILE * 2 * poles), F32)
    held = pltpu.VMEM((sum(m.shape[0] for m in slabs), LANES, LANES), BF16)
    parts = max(2, blocks // 32)
    sems = [pltpu.SemaphoreType.DMA((p,)) for p in (parts, parts, sigma.shape[0] // BO)]
    hbm = pl.BlockSpec(memory_space=pl.ANY)
    fixed = (me_ref, near, spots, poles_ref)
    remote = 2 * NYB + CONTACT
    rows = cols + 1

    def call(kernel, inputs, out_rows, scratch, name):
        scratch = [pltpu.VMEM((r, poles, LANES), F32) for r in scratch]
        return pl.pallas_call(
            kernel,
            in_specs=[SMEM] * 3 + [VMEM] * (len(inputs) - 3) + [hbm] * 3,
            out_specs=[VMEM] * len(out_rows),
            out_shape=[vec_shape(r) for r in out_rows],
            scratch_shapes=[*scratch, wide, acc, held, *sems],
            compiler_params=large,
            name=name,
        )(*inputs, *slabs)

    chunk, *edges = pl.pallas_call(
        prepare_kernel,
        in_specs=[SMEM, SMEM, pl.BlockSpec(memory_space=pl.ANY)],
        out_specs=[VMEM] * 3,
        out_shape=[vec_shape(rows), vec_shape(NYB), vec_shape(NYB)],
        scratch_shapes=[pltpu.SemaphoreType.DMA((cols + 2,))],
        compiler_params=small,
        name="prepare",
    )(me_ref, spots, rhs)
    half = blocks // 2

    def own_part(first):
        return pl.pallas_call(
            functools.partial(own_kernel, first),
            in_specs=[SMEM] + [VMEM] * 2 + [hbm] * 2,
            out_specs=VMEM,
            out_shape=vec_shape(half),
            scratch_shapes=[wide, held, *([pltpu.SemaphoreType.DMA((max(1, half // 32),))] * 2)],
            compiler_params=pltpu.CompilerParams(vmem_limit_bytes=54 << 20),
            cost_estimate=pl.CostEstimate(
                flops=2 * ham.size * 2 * poles, bytes_accessed=2 * ham.size, transcendentals=0
            ),
            name="own",
        )(near, poles_ref, rhs, *slabs[:2])

    rhs_ext, image, chunk, edge_a, edge_b = call(
        first_kernel, (*fixed, rhs, *exchange(chunk, edges, (own_part(0), own_part(half)))),
        [ext, blocks, rows, NYB, NYB], [], "first",
    )
    image_ext, half_ext, turned, chunk, edge_a, edge_b, scalars = call(
        second_kernel, (*fixed, rhs_ext, image, *exchange(chunk, (edge_a, edge_b))),
        [ext, ext, blocks, rows, NYB, NYB, 3], [], "second",
    )
    res_own, dir_own, res_rem, dir_rem, iterate, image, chunk, edge_a, edge_b, rho = call(
        third_kernel,
        (*fixed, scalars, rhs_ext, image_ext, half_ext, turned, *exchange(chunk, (edge_a, edge_b))),
        [blocks, blocks, remote, remote, blocks, blocks, rows, NYB, NYB, 3], [ext], "third",
    )
    half_own, turned, iterate, sums = call(
        fourth_kernel,
        (*fixed, rho, res_own, dir_own, res_rem, dir_rem, iterate, image,
         *exchange(chunk, (edge_a, edge_b))),
        [blocks, blocks, blocks, 1], [CONTACT], "fourth",
    )
    return tuple(
        pl.pallas_call(
            last_kernel,
            in_specs=[VMEM] * 5,
            out_specs=[VMEM] * 2,
            out_shape=[vec_shape(blocks)] * 2,
            compiler_params=small,
            name="last",
        )(*exchange(sums), half_own, turned, iterate)
    )


def solution(mesh):
    return jax.shard_map(
        local,
        mesh=mesh,
        in_specs=(
            P("gx", "grp", None),
            P("gx", None, None, None),
            P("gx", None, None, None),
            P("gx", None, None),
            P("gx", None),
            P("gx"),
            P("grp"),
            P("grp"),
        ),
        out_specs=(P("gx", "grp", None), P("gx", "grp", None)),
        check_vma=False,
    )
```

```python
import functools

import jax
import jax.numpy as jnp
from jax import lax
from jax.experimental import pallas as pl
from jax.experimental.pallas import tpu as pltpu
from jax.sharding import PartitionSpec as P

BO = 64
NYB = 16
NNZ = 5
CONTACT = 128
LANES = 2 * BO
TILE = 16
FLOOR_SHARE = 0.0625
SMALL_EPS = 1e-06
F32 = jnp.float32
BF16 = jnp.bfloat16
VMEM = pl.BlockSpec(memory_space=pltpu.VMEM)
SMEM = pl.BlockSpec(memory_space=pltpu.SMEM)


def dot_nt(left, right):
    return lax.dot_general(left, right, (((1,), (1,)), ((), ())), preferred_element_type=F32)


def swap_halves(vec):
    return pltpu.roll(vec, BO, axis=vec.ndim - 1)


def half_sign(ndim):
    lane = lax.broadcasted_iota(jnp.int32, (1,) * (ndim - 1) + (LANES,), ndim - 1)
    return jnp.where(lane < BO, -1.0, 1.0).astype(F32)


def scale(factor, vec):
    fac_re = factor[0]
    fac_im = factor[1] * half_sign(2)
    return fac_re * vec + fac_im * swap_halves(vec)


def complex_mul(a, b):
    return (a[0] * b[0] - a[1] * b[1], a[0] * b[1] + a[1] * b[0])


def guarded_quotient(num, den, bound_sq):
    top = complex_mul(num, (den[0], -den[1]))
    size = jnp.maximum(den[0] * den[0] + den[1] * den[1], FLOOR_SHARE * bound_sq)
    return (top[0] / size, top[1] / size)


def spread(column):
    return jnp.broadcast_to(column, (column.shape[0], LANES))


def pack_columns(columns):
    poles = columns[0].shape[0]
    lane = lax.broadcasted_iota(jnp.int32, (poles, LANES), 1)
    packed = jnp.zeros((poles, LANES), F32)
    for index, column in enumerate(columns):
        packed = jnp.where(lane == index, column, packed)
    return packed


def take_columns(packed, count):
    return [spread(packed[:, index : index + 1]) for index in range(count)]


def lane_sum(vec):
    return jnp.sum(vec, axis=1, keepdims=True)


def store_wide(wide, start, rows, vec):
    lane = lax.broadcasted_iota(jnp.int32, (1, 1, LANES), 2)
    front = jnp.where(lane < BO, vec, -vec)
    wide[pl.ds(start, rows)] = jnp.concatenate([front, swap_halves(vec)], axis=1).astype(BF16)


def chunk_of(partner, me, count):
    slot = jnp.bitwise_xor(partner, me)
    inner = jnp.right_shift(slot, 1)
    y_bit = jnp.bitwise_and(inner, 1)
    return jnp.bitwise_and(slot, 1), y_bit * (count // 4) + jnp.right_shift(inner, 1)


def gathered_sums(near_side, far_side, row):
    total = None
    for index in range(near_side.shape[0]):
        pair = near_side[index, row] + far_side[index, row]
        total = pair if total is None else total + pair
    return total


def place_gathered(target, offset, me, near_side, far_side, cols):
    half = near_side.shape[0]
    for index in range(half):
        y_bit, z_part = index // (half // 2), index % (half // 2)
        partner = jnp.bitwise_xor(me, 2 * y_bit + 4 * z_part)
        target[pl.ds(offset + partner * cols, cols)] = near_side[index, :cols]
        partner = jnp.bitwise_xor(partner, 1)
        target[pl.ds(offset + partner * cols, cols)] = far_side[index, :cols]


def over_rows(count, step, body):
    def run(index, carry):
        body(pl.multiple_of(index * step, step))
        return carry

    lax.fori_loop(0, count // step, run, 0)


def sum_rows(count, step, body, terms, poles):
    def run(index, carry):
        parts = body(pl.multiple_of(index * step, step))
        return tuple(c + jnp.sum(p, axis=0) for c, p in zip(carry, parts))

    zero = jnp.zeros((poles, LANES), F32)
    return lax.fori_loop(0, count // step, run, (zero,) * terms)


def contact_spots(contact, me, blocks):
    return [contact[l] - me * blocks for l in range(contact.shape[0])]


def halo_starts(me, blocks):
    odd = jnp.bitwise_and(me, 1)
    return (1 - odd) * (NYB + blocks), odd * (NYB + blocks)


def edge_start(kind, me, blocks):
    odd = jnp.bitwise_and(me, 1)
    return (1 - odd if kind == 0 else odd) * (blocks - NYB)


def fill_extended(ext, partner, own, other, me, near_side, far_side, cols):
    blocks = own.shape[0]
    partner_start, other_start = halo_starts(me, blocks)
    ext[pl.ds(partner_start, NYB)] = partner[...]
    ext[pl.ds(other_start, NYB)] = other[...]
    ext[NYB : NYB + blocks] = own[...]
    place_gathered(ext, 2 * NYB + blocks, me, near_side, far_side, cols)


def pole_factor(values):
    poles = values.shape[0]
    row = lax.broadcasted_iota(jnp.int32, (poles, LANES), 0)
    factor = jnp.zeros((poles, LANES), F32)
    for pole in range(poles):
        factor = jnp.where(row == pole, values[pole], factor)
    return factor


def combine(z, result):
    poles = z[0].shape[0]
    left = lax.broadcasted_iota(jnp.int32, (poles, LANES), 1) < BO
    top, low = result[:poles], result[poles:]
    ham_part = jnp.where(left, top, swap_halves(low))
    ovl_part = jnp.where(left, swap_halves(top), low)
    return scale(z, ovl_part) - ham_part


def ovl_base(blocks):
    return blocks * NNZ // 2


def sparse_block(mats, base, pair, index):
    half = index % 2
    return mats[base + NNZ * pair + index // 2, BO * half : BO * (half + 1)]


def sparse_group(near, z, wide, mats, blocks, image, first, count, shift=0):
    rows = 2 * image.shape[1]
    bases = (0, ovl_base(blocks))
    for pair in range(count // 2):
        b = first + 2 * pair
        vectors, matrices = [], []
        for q in range(2):
            vectors.append(jnp.concatenate([wide[near[(b + q) * NNZ + k]] for k in range(NNZ)], axis=1))
            for base in bases:
                pieces = [
                    sparse_block(mats, base, first // 2 + pair, q * NNZ + k) for k in range(NNZ)
                ]
                matrices.append(jnp.concatenate(pieces, axis=1))
        result = dot_nt(jnp.concatenate(vectors, axis=0), jnp.concatenate(matrices, axis=0))
        for q in range(2):
            image[b + q - shift] = combine(
                z, result[rows * q : rows * (q + 1), LANES * q : LANES * (q + 1)]
            )


def part_copy(source, mats, base, sem, part):
    size = source.shape[0] // sem.shape[0]
    return pltpu.make_async_copy(
        source.at[pl.ds(part * size, size)],
        mats.at[pl.ds(base + part * size, size)],
        sem.at[part],
    )


def start_sparse(ham, ovl, mats, sems):
    base = ovl_base(2 * ham.shape[0] // NNZ)
    for part in range(sems[0].shape[0]):
        part_copy(ham, mats, 0, sems[0], part).start()
        part_copy(ovl, mats, base, sems[1], part).start()


def start_sigma(sigma, mats, sem):
    base = mats.shape[0] - sigma.shape[0]
    for part in range(sem.shape[0]):
        part_copy(sigma, mats, base, sem, part).start()


def start_matrices(ham, ovl, sigma, mats, sems):
    start_sparse(ham, ovl, mats, sems)
    start_sigma(sigma, mats, sems[2])


def sparse_part(near, z, wide, ham, ovl, mats, sems, image):
    parts = sems[0].shape[0]
    blocks = image.shape[0]
    size = blocks // parts

    def step(part, carry):
        part_copy(ham, mats, 0, sems[0], part).wait()
        part_copy(ovl, mats, ovl_base(blocks), sems[1], part).wait()
        sparse_group(near, z, wide, mats, blocks, image, part * size, size)
        return carry

    lax.fori_loop(0, parts, step, 0)


def edge_part(near, z, wide, mats, image):
    blocks = image.shape[0]
    for first, slot in ((0, 2), (blocks - NYB, 1)):

        def step(group, carry, first=first, slot=slot):
            for index in range(4):
                pair = first // 2 + 4 * group + index
                for q in range(2):
                    b = 2 * pair + q
                    pieces = [
                        sparse_block(mats, base, pair, q * NNZ + slot)
                        for base in (0, ovl_base(blocks))
                    ]
                    product = dot_nt(wide[near[b * NNZ + slot]], jnp.concatenate(pieces, axis=0))
                    image[b] = image[b] + combine(z, product)
            return carry

        lax.fori_loop(0, NYB // 8, step, 0)


def contact_part(spots, wide, sigma, mats, sem, acc, image):
    blocks, poles = image.shape[0], image.shape[1]
    cols = len(spots)
    first_contact = blocks + 2 * NYB
    base = blocks * NNZ
    group_rows = sigma.shape[0] // sem.shape[0]
    width = TILE * 2 * poles
    row_t = lax.broadcasted_iota(jnp.int32, (TILE, width), 0)
    col_t = lax.broadcasted_iota(jnp.int32, (TILE, width), 1) // (2 * poles)
    keep = (row_t == col_t)[None]

    def step(group, carry):
        part_copy(sigma, mats, base, sem, group).wait()
        start = base + group * group_rows
        total = None
        for pair in range(CONTACT // (2 * TILE)):
            slabs, vectors = [], []
            for side in range(2):
                first = (2 * pair + side) * TILE
                slab = mats[pl.ds(start, group_rows), first : first + TILE]
                slabs.append(slab.reshape(group_rows * TILE, LANES))
                vectors.append(
                    wide[first_contact + first : first_contact + first + TILE].reshape(width, LANES)
                )
            part = dot_nt(jnp.concatenate(slabs, axis=1), jnp.concatenate(vectors, axis=1))
            total = part if total is None else total + part
        kept = jnp.where(keep, total.reshape(group_rows, TILE, width), 0.0)
        acc[pl.ds(pl.multiple_of(group * group_rows, group_rows), group_rows)] = jnp.sum(kept, axis=1)
        return carry

    lax.fori_loop(0, sem.shape[0], step, 0)
    fold_row = lax.broadcasted_iota(jnp.int32, (2 * poles, width), 0)
    fold_col = lax.broadcasted_iota(jnp.int32, (2 * poles, width), 1) % (2 * poles)
    fold = jnp.where(fold_row == fold_col, 1.0, 0.0).astype(BF16)
    rest = acc[...]
    folded = None
    for _ in range(2):
        piece = rest.astype(BF16)
        part = dot_nt(fold, piece)
        folded = part if folded is None else folded + part
        rest = rest - piece.astype(F32)
    for l in range(cols):
        column = slice(BO * l, BO * (l + 1))
        product = jnp.concatenate([folded[:poles, column], folded[poles:, column]], axis=1)
        spot = spots[l]
        image[spot] = image[spot] - product


def apply_operator(near, spots, z, wide, ham, ovl, sigma, mats, sems, acc, image):
    sparse_part(near, z, wide, ham, ovl, mats, sems, image)
    contact_part(spots, wide, sigma, mats, sems[2], acc, image)


def store_chunk(chunk, edge_a, edge_b, me, spots, image, sums):
    cols = len(spots)
    blocks = image.shape[0]
    edge_a[...] = image[pl.ds(edge_start(0, me, blocks), NYB)]
    edge_b[...] = image[pl.ds(edge_start(1, me, blocks), NYB)]
    for l in range(cols):
        chunk[l] = image[spots[l]]
    chunk[cols] = sums


def inner_terms(a, c):
    return a * c, a * swap_halves(c)


def inner_pair(re_acc, im_acc):
    return lane_sum(re_acc), lane_sum(im_acc * -half_sign(2))


def prepare_kernel(me_ref, contact, rhs, chunk, edge_a, edge_b, sem):
    blocks, poles = rhs.shape[0], rhs.shape[1]
    spots = contact_spots(contact, me_ref[0], blocks)
    cols = len(spots)
    copies = [pltpu.make_async_copy(rhs.at[spots[l]], chunk.at[l], sem.at[l]) for l in range(cols)]
    for kind, edge in enumerate((edge_a, edge_b)):
        here = pl.ds(edge_start(kind, me_ref[0], blocks), NYB)
        copies.append(pltpu.make_async_copy(rhs.at[here], edge, sem.at[cols + kind]))
    for copy in copies:
        copy.start()
    chunk[cols] = jnp.zeros((poles, LANES), F32)
    for copy in copies:
        copy.wait()


def own_kernel(first, near, pole_re, pole_im, own, ham, ovl, image, wide, mats, *sems):
    z = (pole_factor(pole_re), pole_factor(pole_im))
    blocks = own.shape[0]
    parts = sems[0].shape[0]
    size = image.shape[0] // parts
    slabs = size * NNZ // 2
    start = first * NNZ // 2

    def copies(part):
        for source, base, sem in ((ham, 0, sems[0]), (ovl, ovl_base(blocks), sems[1])):
            yield pltpu.make_async_copy(
                source.at[pl.ds(start + part * slabs, slabs)],
                mats.at[pl.ds(base + start + part * slabs, slabs)],
                sem.at[part],
            )

    for part in range(parts):
        for copy in copies(part):
            copy.start()
    wide[0:NYB] = jnp.zeros((NYB, *wide.shape[1:]), BF16)
    wide[NYB + blocks : 2 * NYB + blocks] = jnp.zeros((NYB, *wide.shape[1:]), BF16)
    low = max(0, first - NYB)
    needed = min(blocks, first + image.shape[0] + NYB) - low
    over_rows(
        needed, TILE,
        lambda s: store_wide(wide, NYB + low + s, TILE, own[pl.ds(low + s, TILE)]),
    )

    def step(part, carry):
        for copy in copies(part):
            copy.wait()
        sparse_group(
            near, z, wide, mats, blocks, image, first + part * size, size, shift=first
        )
        return carry

    lax.fori_loop(0, parts, step, 0)


def first_kernel(
    me_ref, near, contact, pole_re, pole_im, own, image_in, partner, other, near_side, far_side, ham, ovl, sigma,
    rhs_ext, image, chunk, edge_a, edge_b, wide, acc, mats, *sems,
):
    blocks, poles = own.shape[0], own.shape[1]
    z = (pole_factor(pole_re), pole_factor(pole_im))
    spots = contact_spots(contact, me_ref[0], blocks)
    edge_slabs = NYB * NNZ // 2
    edges = []
    for source, base, sem in ((ham, 0, sems[0]), (ovl, ovl_base(blocks), sems[1])):
        for side, start in enumerate((0, (blocks - NYB) * NNZ // 2)):
            edges.append(
                pltpu.make_async_copy(
                    source.at[pl.ds(start, edge_slabs)],
                    mats.at[pl.ds(base + start, edge_slabs)],
                    sem.at[side],
                )
            )
    for copy in edges:
        copy.start()
    start_sigma(sigma, mats, sems[2])
    fill_extended(rhs_ext, partner, own, other, me_ref[0], near_side, far_side, len(spots))
    store_wide(wide, 0, NYB, rhs_ext[0:NYB])
    over_rows(
        NYB + CONTACT, TILE,
        lambda s: store_wide(wide, NYB + blocks + s, TILE, rhs_ext[pl.ds(NYB + blocks + s, TILE)]),
    )
    image[...] = image_in[...]
    for copy in edges:
        copy.wait()
    edge_part(near, z, wide, mats, image)
    contact_part(spots, wide, sigma, mats, sems[2], acc, image)

    def terms(s):
        b, v = own[pl.ds(s, 2 * TILE)], image[pl.ds(s, 2 * TILE)]
        return (b * b, *inner_terms(b, v), v * v)

    bb, bv_re, bv_im, vv = sum_rows(blocks, 2 * TILE, terms, 4, poles)
    store_chunk(
        chunk, edge_a, edge_b, me_ref[0], spots, image, pack_columns([lane_sum(bb), *inner_pair(bv_re, bv_im), lane_sum(vv)])
    )


def second_kernel(
    me_ref, near, contact, pole_re, pole_im, rhs_ext, own, partner, other, near_side, far_side, ham, ovl, sigma,
    image_ext, half_ext, turned, chunk, edge_a, edge_b, scalars, wide, acc, mats,
    *sems,
):
    start_matrices(ham, ovl, sigma, mats, sems)
    blocks, poles = own.shape[0], own.shape[1]
    z = (pole_factor(pole_re), pole_factor(pole_im))
    spots = contact_spots(contact, me_ref[0], blocks)
    cols = len(spots)
    fill_extended(image_ext, partner, own, other, me_ref[0], near_side, far_side, cols)
    norm_b, bv_re, bv_im, vv = take_columns(gathered_sums(near_side, far_side, cols), 4)
    alpha = guarded_quotient((norm_b, jnp.zeros_like(norm_b)), (bv_re, bv_im), norm_b * vv)
    scalars[0] = norm_b
    scalars[1] = alpha[0]
    scalars[2] = alpha[1]

    def update(s):
        here = pl.ds(s, 2 * TILE)
        half = rhs_ext[here] - scale(alpha, image_ext[here])
        half_ext[here] = half
        store_wide(wide, s, 2 * TILE, half)

    over_rows(half_ext.shape[0], 2 * TILE, update)
    apply_operator(near, spots, z, wide, ham, ovl, sigma, mats, sems, acc, turned)

    def terms(s):
        b = rhs_ext[pl.ds(NYB + s, 2 * TILE)]
        h = half_ext[pl.ds(NYB + s, 2 * TILE)]
        t = turned[pl.ds(s, 2 * TILE)]
        return (*inner_terms(t, h), t * t, h * h, *inner_terms(b, h), *inner_terms(b, t))

    th_re, th_im, tt, hh, bh_re, bh_im, bt_re, bt_im = sum_rows(blocks, 2 * TILE, terms, 8, poles)
    columns = [
        *inner_pair(th_re, th_im), lane_sum(tt), lane_sum(hh),
        *inner_pair(bh_re, bh_im), *inner_pair(bt_re, bt_im),
    ]
    store_chunk(chunk, edge_a, edge_b, me_ref[0], spots, turned, pack_columns(columns))


def third_kernel(
    me_ref, near, contact, pole_re, pole_im, scalars, rhs_ext, image_ext, half_ext, own, partner, other,
    near_side, far_side, ham, ovl, sigma,
    residual_own, direction_own, residual_rem, direction_rem, iterate, image, chunk, edge_a,
    edge_b, rho_out, turned_ext, wide, acc, mats, *sems,
):
    start_matrices(ham, ovl, sigma, mats, sems)
    blocks, poles = own.shape[0], own.shape[1]
    z = (pole_factor(pole_re), pole_factor(pole_im))
    spots = contact_spots(contact, me_ref[0], blocks)
    cols = len(spots)
    fill_extended(turned_ext, partner, own, other, me_ref[0], near_side, far_side, cols)
    sums = take_columns(gathered_sums(near_side, far_side, cols), 8)
    th, tt, hh, bh, bt = (sums[0], sums[1]), sums[2], sums[3], (sums[4], sums[5]), (sums[6], sums[7])
    norm_b, alpha = scalars[0], (scalars[1], scalars[2])
    turned_sq = tt + SMALL_EPS
    omega = (th[0] / turned_sq, th[1] / turned_sq)
    minus = complex_mul(omega, bt)
    rho_next = (bh[0] - minus[0], bh[1] - minus[1])
    zeros = jnp.zeros_like(tt)
    inverse_omega = guarded_quotient((turned_sq, zeros), th, tt * hh)
    ratio = complex_mul(rho_next, complex_mul(alpha, inverse_omega))
    beta = (ratio[0] / norm_b, ratio[1] / norm_b)
    rho_out[0] = rho_next[0]
    rho_out[1] = rho_next[1]
    rho_out[2] = norm_b

    def update(s):
        half = half_ext[pl.ds(s, TILE)]
        residual = half - scale(omega, turned_ext[pl.ds(s, TILE)])
        old = rhs_ext[pl.ds(s, TILE)]
        direction = residual + scale(beta, old - scale(omega, image_ext[pl.ds(s, TILE)]))
        store_wide(wide, s, TILE, direction)
        return residual, direction

    def update_own(s):
        residual, direction = update(NYB + s)
        residual_own[pl.ds(s, TILE)] = residual
        direction_own[pl.ds(s, TILE)] = direction
        iterate[pl.ds(s, TILE)] = scale(alpha, rhs_ext[pl.ds(NYB + s, TILE)]) + scale(
            omega, half_ext[pl.ds(NYB + s, TILE)]
        )

    def update_rest(source, target):
        residual, direction = update(source)
        residual_rem[pl.ds(target, TILE)] = residual
        direction_rem[pl.ds(target, TILE)] = direction

    over_rows(blocks, TILE, update_own)
    update_rest(0, 0)
    over_rows(NYB + CONTACT, TILE, lambda s: update_rest(NYB + blocks + s, NYB + s))
    apply_operator(near, spots, z, wide, ham, ovl, sigma, mats, sems, acc, image)

    def terms(s):
        b, v = rhs_ext[pl.ds(NYB + s, 2 * TILE)], image[pl.ds(s, 2 * TILE)]
        return (*inner_terms(b, v), v * v)

    bv_re, bv_im, vv = sum_rows(blocks, 2 * TILE, terms, 3, poles)
    store_chunk(chunk, edge_a, edge_b, me_ref[0], spots, image, pack_columns([*inner_pair(bv_re, bv_im), lane_sum(vv)]))


def fourth_kernel(
    me_ref, near, contact, pole_re, pole_im, rho_in, residual_own, direction_own, residual_rem,
    direction_rem, iterate_in, own, partner, other, near_side, far_side, ham, ovl, sigma,
    half_own, turned, iterate, sums_out, contact_image, wide, acc, mats, *sems,
):
    start_matrices(ham, ovl, sigma, mats, sems)
    blocks, poles = own.shape[0], own.shape[1]
    z = (pole_factor(pole_re), pole_factor(pole_im))
    spots = contact_spots(contact, me_ref[0], blocks)
    cols = len(spots)
    place_gathered(contact_image, 0, me_ref[0], near_side, far_side, cols)
    bv_re, bv_im, vv = take_columns(gathered_sums(near_side, far_side, cols), 3)
    norm_b = rho_in[2]
    alpha = guarded_quotient((rho_in[0], rho_in[1]), (bv_re, bv_im), norm_b * vv)

    def update_own(s):
        here = pl.ds(s, TILE)
        half = residual_own[here] - scale(alpha, own[here])
        half_own[here] = half
        iterate[here] = iterate_in[here] + scale(alpha, direction_own[here])
        store_wide(wide, NYB + s, TILE, half)

    over_rows(blocks, TILE, update_own)
    for start, image in zip(halo_starts(me_ref[0], blocks), (partner, other)):
        remote = jnp.where(start == 0, 0, NYB)
        half = residual_rem[pl.ds(remote, NYB)] - scale(alpha, image[...])
        store_wide(wide, start, NYB, half)

    def update_contact(s):
        half = residual_rem[pl.ds(2 * NYB + s, TILE)] - scale(alpha, contact_image[pl.ds(s, TILE)])
        store_wide(wide, 2 * NYB + blocks + s, TILE, half)

    over_rows(CONTACT, TILE, update_contact)
    apply_operator(near, spots, z, wide, ham, ovl, sigma, mats, sems, acc, turned)

    def terms(s):
        h, t = half_own[pl.ds(s, 2 * TILE)], turned[pl.ds(s, 2 * TILE)]
        return (*inner_terms(t, h), t * t)

    th_re, th_im, tt = sum_rows(blocks, 2 * TILE, terms, 3, poles)
    sums_out[0] = pack_columns([*inner_pair(th_re, th_im), lane_sum(tt)])


def last_kernel(near_side, far_side, half_own, turned, iterate, solution_out, residual_out):
    th_re, th_im, tt = take_columns(gathered_sums(near_side, far_side, 0), 3)
    turned_sq = tt + SMALL_EPS
    omega = (th_re / turned_sq, th_im / turned_sq)

    def update(s):
        here = pl.ds(s, TILE)
        half = half_own[here]
        solution_out[here] = iterate[here] + scale(omega, half)
        residual_out[here] = half - scale(omega, turned[here])

    over_rows(half_own.shape[0], TILE, update)


def local(rhs, ham, ovl, sigma, neighbours, contact, pole_real, pole_imag):
    blocks, poles = rhs.shape[0], rhs.shape[1]
    cols = contact.shape[0]
    count = lax.axis_size("gx")
    me = lax.axis_index("gx")
    first_block = me * blocks
    near = ((neighbours - first_block + NYB) % (blocks * count)).reshape(-1)
    me_ref = jnp.reshape(me, (1,)).astype(jnp.int32)
    ext = blocks + 2 * NYB + CONTACT

    def flip(value, mask):
        return lax.ppermute(value, "gx", [(i, i ^ mask) for i in range(count)])

    def exchange(chunk, edges=None, beside=None):
        parts = [chunk] + [flip(chunk, mask) for mask in range(4, count, 4)]
        far = ()
        if edges is not None:
            other = [(i, (i + 1 if i % 2 else i - 1) % count) for i in range(count)]
            far = (lax.ppermute(edges[1], "gx", other),)
        line = jnp.stack(parts)
        extra = ()
        if beside is not None:
            after, line = lax.optimization_barrier((near, line))
            extra = (beside(after),)
        plane = jnp.concatenate([line, flip(line, 2)])
        if edges is None:
            return plane, flip(plane, 1)
        far, extra, plane = lax.optimization_barrier((far, extra, plane))
        return (*extra, flip(edges[0], 1), *far, plane, flip(plane, 1))

    def vec_shape(rows):
        return jax.ShapeDtypeStruct((rows, poles, LANES), F32)

    slabs = (ham.reshape(-1, LANES, LANES), ovl.reshape(-1, LANES, LANES), sigma)
    small = pltpu.CompilerParams(vmem_limit_bytes=8 << 20)
    large = pltpu.CompilerParams(vmem_limit_bytes=43 << 20)
    wide = pltpu.VMEM((ext, 2 * poles, LANES), BF16)
    acc = pltpu.VMEM((sigma.shape[0], TILE * 2 * poles), F32)
    held = pltpu.VMEM((sum(m.shape[0] for m in slabs), LANES, LANES), BF16)
    parts = max(2, blocks // 32)
    sems = [pltpu.SemaphoreType.DMA((p,)) for p in (parts, parts, max(1, sigma.shape[0] // 128))]
    hbm = pl.BlockSpec(memory_space=pl.ANY)
    fixed = (me_ref, near, contact, pole_real, pole_imag)
    remote = 2 * NYB + CONTACT
    rows = cols + 1

    def call(kernel, inputs, out_rows, scratch, name):
        scratch = [pltpu.VMEM((r, poles, LANES), F32) for r in scratch]
        return pl.pallas_call(
            kernel,
            in_specs=[SMEM] * 5 + [VMEM] * (len(inputs) - 5) + [hbm] * 3,
            out_specs=[VMEM] * len(out_rows),
            out_shape=[vec_shape(r) for r in out_rows],
            scratch_shapes=[*scratch, wide, acc, held, *sems],
            compiler_params=large,
            name=name,
        )(*inputs, *slabs)

    chunk, *edges = pl.pallas_call(
        prepare_kernel,
        in_specs=[SMEM, SMEM, pl.BlockSpec(memory_space=pl.ANY)],
        out_specs=[VMEM] * 3,
        out_shape=[vec_shape(rows), vec_shape(NYB), vec_shape(NYB)],
        scratch_shapes=[pltpu.SemaphoreType.DMA((cols + 2,))],
        compiler_params=small,
        name="prepare",
    )(me_ref, contact, rhs)
    def own_part(near):
        return pl.pallas_call(
            functools.partial(own_kernel, 0),
            in_specs=[SMEM] * 3 + [VMEM] + [hbm] * 2,
            out_specs=VMEM,
            out_shape=vec_shape(blocks),
            scratch_shapes=[wide, held, *([pltpu.SemaphoreType.DMA((parts,))] * 2)],
            compiler_params=pltpu.CompilerParams(vmem_limit_bytes=50 << 20),
            cost_estimate=pl.CostEstimate(
                flops=4 * ham.size * 2 * poles, bytes_accessed=4 * ham.size, transcendentals=0
            ),
            name="own",
        )(near, pole_real, pole_imag, rhs, *slabs[:2])

    rhs_ext, image, chunk, edge_a, edge_b = call(
        first_kernel, (*fixed, rhs, *exchange(chunk, edges, own_part)),
        [ext, blocks, rows, NYB, NYB], [], "first",
    )
    image_ext, half_ext, turned, chunk, edge_a, edge_b, scalars = call(
        second_kernel, (*fixed, rhs_ext, image, *exchange(chunk, (edge_a, edge_b))),
        [ext, ext, blocks, rows, NYB, NYB, 3], [], "second",
    )
    res_own, dir_own, res_rem, dir_rem, iterate, image, chunk, edge_a, edge_b, rho = call(
        third_kernel,
        (*fixed, scalars, rhs_ext, image_ext, half_ext, turned, *exchange(chunk, (edge_a, edge_b))),
        [blocks, blocks, remote, remote, blocks, blocks, rows, NYB, NYB, 3], [ext], "third",
    )
    half_own, turned, iterate, sums = call(
        fourth_kernel,
        (*fixed, rho, res_own, dir_own, res_rem, dir_rem, iterate, image,
         *exchange(chunk, (edge_a, edge_b))),
        [blocks, blocks, blocks, 1], [CONTACT], "fourth",
    )
    return tuple(
        pl.pallas_call(
            last_kernel,
            in_specs=[VMEM] * 5,
            out_specs=[VMEM] * 2,
            out_shape=[vec_shape(blocks)] * 2,
            compiler_params=small,
            name="last",
        )(*exchange(sums), half_own, turned, iterate)
    )


def solution(mesh):
    return jax.shard_map(
        local,
        mesh=mesh,
        in_specs=(
            P("gx", "grp", None),
            P("gx", None, None, None),
            P("gx", None, None, None),
            P("gx", None, None),
            P("gx", None),
            P("gx"),
            P("grp"),
            P("grp"),
        ),
        out_specs=(P("gx", "grp", None), P("gx", "grp", None)),
        check_vma=False,
    )
```

```python
import functools

import jax
import jax.numpy as jnp
from jax import lax
from jax.experimental import pallas as pl
from jax.experimental.pallas import tpu as pltpu
from jax.sharding import PartitionSpec as P

BO = 64
NYB = 16
NNZ = 5
CONTACT = 128
LANES = 2 * BO
TILE = 16
FLOOR_SHARE = 0.0625
SMALL_EPS = 1e-06
F32 = jnp.float32
BF16 = jnp.bfloat16
VMEM = pl.BlockSpec(memory_space=pltpu.VMEM)
SMEM = pl.BlockSpec(memory_space=pltpu.SMEM)


def dot_nt(left, right):
    return lax.dot_general(left, right, (((1,), (1,)), ((), ())), preferred_element_type=F32)


def swap_halves(vec):
    return pltpu.roll(vec, BO, axis=vec.ndim - 1)


def half_sign(ndim):
    lane = lax.broadcasted_iota(jnp.int32, (1,) * (ndim - 1) + (LANES,), ndim - 1)
    return jnp.where(lane < BO, -1.0, 1.0).astype(F32)


def scale(factor, vec):
    fac_re = factor[0]
    fac_im = factor[1] * half_sign(2)
    return fac_re * vec + fac_im * swap_halves(vec)


def complex_mul(a, b):
    return (a[0] * b[0] - a[1] * b[1], a[0] * b[1] + a[1] * b[0])


def guarded_quotient(num, den, bound_sq):
    top = complex_mul(num, (den[0], -den[1]))
    size = jnp.maximum(den[0] * den[0] + den[1] * den[1], FLOOR_SHARE * bound_sq)
    return (top[0] / size, top[1] / size)


def spread(column):
    return jnp.broadcast_to(column, (column.shape[0], LANES))


def pack_columns(columns):
    poles = columns[0].shape[0]
    lane = lax.broadcasted_iota(jnp.int32, (poles, LANES), 1)
    packed = jnp.zeros((poles, LANES), F32)
    for index, column in enumerate(columns):
        packed = jnp.where(lane == index, column, packed)
    return packed


def take_columns(packed, count):
    return [spread(packed[:, index : index + 1]) for index in range(count)]


def lane_sum(vec):
    return jnp.sum(vec, axis=1, keepdims=True)


def store_wide(wide, start, rows, vec):
    lane = lax.broadcasted_iota(jnp.int32, (1, 1, LANES), 2)
    front = jnp.where(lane < BO, vec, -vec)
    wide[pl.ds(start, rows)] = jnp.concatenate([front, swap_halves(vec)], axis=1).astype(BF16)


def chunk_of(partner, me, count):
    slot = jnp.bitwise_xor(partner, me)
    inner = jnp.right_shift(slot, 1)
    y_bit = jnp.bitwise_and(inner, 1)
    return jnp.bitwise_and(slot, 1), y_bit * (count // 4) + jnp.right_shift(inner, 1)


def gathered_sums(near_side, far_side, row):
    total = None
    for index in range(near_side.shape[0]):
        pair = near_side[index, row] + far_side[index, row]
        total = pair if total is None else total + pair
    return total


def place_gathered(target, offset, me, near_side, far_side, cols):
    half = near_side.shape[0]
    for index in range(half):
        y_bit, z_part = index // (half // 2), index % (half // 2)
        partner = jnp.bitwise_xor(me, 2 * y_bit + 4 * z_part)
        target[pl.ds(offset + partner * cols, cols)] = near_side[index, :cols]
        partner = jnp.bitwise_xor(partner, 1)
        target[pl.ds(offset + partner * cols, cols)] = far_side[index, :cols]


def over_rows(count, step, body):
    def run(index, carry):
        body(pl.multiple_of(index * step, step))
        return carry

    lax.fori_loop(0, count // step, run, 0)


def sum_rows(count, step, body, terms, poles):
    def run(index, carry):
        parts = body(pl.multiple_of(index * step, step))
        return tuple(c + jnp.sum(p, axis=0) for c, p in zip(carry, parts))

    zero = jnp.zeros((poles, LANES), F32)
    return lax.fori_loop(0, count // step, run, (zero,) * terms)


def contact_spots(contact, me, blocks):
    return [contact[l] - me * blocks for l in range(contact.shape[0])]


def halo_starts(me, blocks):
    odd = jnp.bitwise_and(me, 1)
    return (1 - odd) * (NYB + blocks), odd * (NYB + blocks)


def edge_start(kind, me, blocks):
    odd = jnp.bitwise_and(me, 1)
    return (1 - odd if kind == 0 else odd) * (blocks - NYB)


def fill_extended(ext, partner, own, other, me, near_side, far_side, cols):
    blocks = own.shape[0]
    partner_start, other_start = halo_starts(me, blocks)
    ext[pl.ds(partner_start, NYB)] = partner[...]
    ext[pl.ds(other_start, NYB)] = other[...]
    ext[NYB : NYB + blocks] = own[...]
    place_gathered(ext, 2 * NYB + blocks, me, near_side, far_side, cols)


def pole_factor(values):
    poles = values.shape[0]
    row = lax.broadcasted_iota(jnp.int32, (poles, LANES), 0)
    factor = jnp.zeros((poles, LANES), F32)
    for pole in range(poles):
        factor = jnp.where(row == pole, values[pole], factor)
    return factor


def combine(z, result):
    poles = z[0].shape[0]
    left = lax.broadcasted_iota(jnp.int32, (poles, LANES), 1) < BO
    top, low = result[:poles], result[poles:]
    ham_part = jnp.where(left, top, swap_halves(low))
    ovl_part = jnp.where(left, swap_halves(top), low)
    return scale(z, ovl_part) - ham_part


def ovl_base(blocks):
    return blocks * NNZ // 2


def sparse_block(mats, base, pair, index):
    half = index % 2
    return mats[base + NNZ * pair + index // 2, BO * half : BO * (half + 1)]


def sparse_group(near, z, wide, mats, blocks, image, first, count, shift=0):
    rows = 2 * image.shape[1]
    bases = (0, ovl_base(blocks))
    for pair in range(count // 2):
        b = first + 2 * pair
        vectors, matrices = [], []
        for q in range(2):
            vectors.append(jnp.concatenate([wide[near[(b + q) * NNZ + k]] for k in range(NNZ)], axis=1))
            for base in bases:
                pieces = [
                    sparse_block(mats, base, first // 2 + pair, q * NNZ + k) for k in range(NNZ)
                ]
                matrices.append(jnp.concatenate(pieces, axis=1))
        result = dot_nt(jnp.concatenate(vectors, axis=0), jnp.concatenate(matrices, axis=0))
        for q in range(2):
            image[b + q - shift] = combine(
                z, result[rows * q : rows * (q + 1), LANES * q : LANES * (q + 1)]
            )


def part_copy(source, mats, base, sem, part):
    size = source.shape[0] // sem.shape[0]
    return pltpu.make_async_copy(
        source.at[pl.ds(part * size, size)],
        mats.at[pl.ds(base + part * size, size)],
        sem.at[part],
    )


def start_sparse(ham, ovl, mats, sems):
    base = ovl_base(2 * ham.shape[0] // NNZ)
    for part in range(sems[0].shape[0]):
        part_copy(ham, mats, 0, sems[0], part).start()
        part_copy(ovl, mats, base, sems[1], part).start()


def start_sigma(sigma, mats, sem):
    base = mats.shape[0] - sigma.shape[0]
    for part in range(sem.shape[0]):
        part_copy(sigma, mats, base, sem, part).start()


def start_matrices(ham, ovl, sigma, mats, sems):
    start_sparse(ham, ovl, mats, sems)
    start_sigma(sigma, mats, sems[2])


def sparse_part(near, z, wide, ham, ovl, mats, sems, image):
    parts = sems[0].shape[0]
    blocks = image.shape[0]
    size = blocks // parts

    def step(part, carry):
        part_copy(ham, mats, 0, sems[0], part).wait()
        part_copy(ovl, mats, ovl_base(blocks), sems[1], part).wait()
        sparse_group(near, z, wide, mats, blocks, image, part * size, size)
        return carry

    lax.fori_loop(0, parts, step, 0)


def edge_part(near, z, wide, mats, image):
    blocks = image.shape[0]
    for first, slot in ((0, 2), (blocks - NYB, 1)):

        def step(group, carry, first=first, slot=slot):
            for index in range(4):
                pair = first // 2 + 4 * group + index
                for q in range(2):
                    b = 2 * pair + q
                    pieces = [
                        sparse_block(mats, base, pair, q * NNZ + slot)
                        for base in (0, ovl_base(blocks))
                    ]
                    product = dot_nt(wide[near[b * NNZ + slot]], jnp.concatenate(pieces, axis=0))
                    image[b] = image[b] + combine(z, product)
            return carry

        lax.fori_loop(0, NYB // 8, step, 0)


def contact_part(spots, wide, sigma, mats, sem, acc, image):
    blocks, poles = image.shape[0], image.shape[1]
    cols = len(spots)
    first_contact = blocks + 2 * NYB
    base = blocks * NNZ
    group_rows = sigma.shape[0] // sem.shape[0]
    width = TILE * 2 * poles
    row_t = lax.broadcasted_iota(jnp.int32, (TILE, width), 0)
    col_t = lax.broadcasted_iota(jnp.int32, (TILE, width), 1) // (2 * poles)
    keep = (row_t == col_t)[None]

    def step(group, carry):
        part_copy(sigma, mats, base, sem, group).wait()
        start = base + group * group_rows
        total = None
        for pair in range(CONTACT // (2 * TILE)):
            slabs, vectors = [], []
            for side in range(2):
                first = (2 * pair + side) * TILE
                slab = mats[pl.ds(start, group_rows), first : first + TILE]
                slabs.append(slab.reshape(group_rows * TILE, LANES))
                vectors.append(
                    wide[first_contact + first : first_contact + first + TILE].reshape(width, LANES)
                )
            part = dot_nt(jnp.concatenate(slabs, axis=1), jnp.concatenate(vectors, axis=1))
            total = part if total is None else total + part
        kept = jnp.where(keep, total.reshape(group_rows, TILE, width), 0.0)
        acc[pl.ds(pl.multiple_of(group * group_rows, group_rows), group_rows)] = jnp.sum(kept, axis=1)
        return carry

    lax.fori_loop(0, sem.shape[0], step, 0)
    fold_row = lax.broadcasted_iota(jnp.int32, (2 * poles, width), 0)
    fold_col = lax.broadcasted_iota(jnp.int32, (2 * poles, width), 1) % (2 * poles)
    fold = jnp.where(fold_row == fold_col, 1.0, 0.0).astype(BF16)
    rest = acc[...]
    folded = None
    for _ in range(2):
        piece = rest.astype(BF16)
        part = dot_nt(fold, piece)
        folded = part if folded is None else folded + part
        rest = rest - piece.astype(F32)
    for l in range(cols):
        column = slice(BO * l, BO * (l + 1))
        product = jnp.concatenate([folded[:poles, column], folded[poles:, column]], axis=1)
        spot = spots[l]
        image[spot] = image[spot] - product


def apply_operator(near, spots, z, wide, ham, ovl, sigma, mats, sems, acc, image):
    sparse_part(near, z, wide, ham, ovl, mats, sems, image)
    contact_part(spots, wide, sigma, mats, sems[2], acc, image)


def store_chunk(chunk, edge_a, edge_b, me, spots, image, sums):
    cols = len(spots)
    blocks = image.shape[0]
    edge_a[...] = image[pl.ds(edge_start(0, me, blocks), NYB)]
    edge_b[...] = image[pl.ds(edge_start(1, me, blocks), NYB)]
    for l in range(cols):
        chunk[l] = image[spots[l]]
    chunk[cols] = sums


def inner_terms(a, c):
    return a * c, a * swap_halves(c)


def inner_pair(re_acc, im_acc):
    return lane_sum(re_acc), lane_sum(im_acc * -half_sign(2))


def prepare_kernel(me_ref, contact, rhs, chunk, edge_a, edge_b, sem):
    blocks, poles = rhs.shape[0], rhs.shape[1]
    spots = contact_spots(contact, me_ref[0], blocks)
    cols = len(spots)
    copies = [pltpu.make_async_copy(rhs.at[spots[l]], chunk.at[l], sem.at[l]) for l in range(cols)]
    for kind, edge in enumerate((edge_a, edge_b)):
        here = pl.ds(edge_start(kind, me_ref[0], blocks), NYB)
        copies.append(pltpu.make_async_copy(rhs.at[here], edge, sem.at[cols + kind]))
    for copy in copies:
        copy.start()
    chunk[cols] = jnp.zeros((poles, LANES), F32)
    for copy in copies:
        copy.wait()


def own_kernel(first, near, pole_re, pole_im, own, ham, ovl, image, wide, mats, *sems):
    z = (pole_factor(pole_re), pole_factor(pole_im))
    blocks = own.shape[0]
    parts = sems[0].shape[0]
    size = image.shape[0] // parts
    slabs = size * NNZ // 2
    start = first * NNZ // 2

    def copies(part):
        for source, base, sem in ((ham, 0, sems[0]), (ovl, ovl_base(blocks), sems[1])):
            yield pltpu.make_async_copy(
                source.at[pl.ds(start + part * slabs, slabs)],
                mats.at[pl.ds(base + start + part * slabs, slabs)],
                sem.at[part],
            )

    for part in range(parts):
        for copy in copies(part):
            copy.start()
    wide[0:NYB] = jnp.zeros((NYB, *wide.shape[1:]), BF16)
    wide[NYB + blocks : 2 * NYB + blocks] = jnp.zeros((NYB, *wide.shape[1:]), BF16)
    low = max(0, first - NYB)
    needed = min(blocks, first + image.shape[0] + NYB) - low
    over_rows(
        needed, TILE,
        lambda s: store_wide(wide, NYB + low + s, TILE, own[pl.ds(low + s, TILE)]),
    )

    def step(part, carry):
        for copy in copies(part):
            copy.wait()
        sparse_group(
            near, z, wide, mats, blocks, image, first + part * size, size, shift=first
        )
        return carry

    lax.fori_loop(0, parts, step, 0)


def first_kernel(
    me_ref, near, contact, pole_re, pole_im, own, image_in, partner, other, near_side, far_side, ham, ovl, sigma,
    rhs_ext, image, chunk, edge_a, edge_b, wide, acc, mats, *sems,
):
    blocks, poles = own.shape[0], own.shape[1]
    z = (pole_factor(pole_re), pole_factor(pole_im))
    spots = contact_spots(contact, me_ref[0], blocks)
    edge_slabs = NYB * NNZ // 2
    edges = []
    for source, base, sem in ((ham, 0, sems[0]), (ovl, ovl_base(blocks), sems[1])):
        for side, start in enumerate((0, (blocks - NYB) * NNZ // 2)):
            edges.append(
                pltpu.make_async_copy(
                    source.at[pl.ds(start, edge_slabs)],
                    mats.at[pl.ds(base + start, edge_slabs)],
                    sem.at[side],
                )
            )
    for copy in edges:
        copy.start()
    start_sigma(sigma, mats, sems[2])
    fill_extended(rhs_ext, partner, own, other, me_ref[0], near_side, far_side, len(spots))
    store_wide(wide, 0, NYB, rhs_ext[0:NYB])
    over_rows(
        NYB + CONTACT, TILE,
        lambda s: store_wide(wide, NYB + blocks + s, TILE, rhs_ext[pl.ds(NYB + blocks + s, TILE)]),
    )
    image[...] = image_in[...]
    for copy in edges:
        copy.wait()
    edge_part(near, z, wide, mats, image)
    contact_part(spots, wide, sigma, mats, sems[2], acc, image)

    def terms(s):
        b, v = own[pl.ds(s, 2 * TILE)], image[pl.ds(s, 2 * TILE)]
        return (b * b, *inner_terms(b, v), v * v)

    bb, bv_re, bv_im, vv = sum_rows(blocks, 2 * TILE, terms, 4, poles)
    store_chunk(
        chunk, edge_a, edge_b, me_ref[0], spots, image, pack_columns([lane_sum(bb), *inner_pair(bv_re, bv_im), lane_sum(vv)])
    )


def second_kernel(
    me_ref, near, contact, pole_re, pole_im, rhs_ext, own, partner, other, near_side, far_side, ham, ovl, sigma,
    image_ext, half_ext, turned, chunk, edge_a, edge_b, scalars, wide, acc, mats,
    *sems,
):
    start_matrices(ham, ovl, sigma, mats, sems)
    blocks, poles = own.shape[0], own.shape[1]
    z = (pole_factor(pole_re), pole_factor(pole_im))
    spots = contact_spots(contact, me_ref[0], blocks)
    cols = len(spots)
    fill_extended(image_ext, partner, own, other, me_ref[0], near_side, far_side, cols)
    norm_b, bv_re, bv_im, vv = take_columns(gathered_sums(near_side, far_side, cols), 4)
    alpha = guarded_quotient((norm_b, jnp.zeros_like(norm_b)), (bv_re, bv_im), norm_b * vv)
    scalars[0] = norm_b
    scalars[1] = alpha[0]
    scalars[2] = alpha[1]

    def update(s):
        here = pl.ds(s, 2 * TILE)
        half = rhs_ext[here] - scale(alpha, image_ext[here])
        half_ext[here] = half
        store_wide(wide, s, 2 * TILE, half)

    over_rows(half_ext.shape[0], 2 * TILE, update)
    apply_operator(near, spots, z, wide, ham, ovl, sigma, mats, sems, acc, turned)

    def terms(s):
        b = rhs_ext[pl.ds(NYB + s, 2 * TILE)]
        h = half_ext[pl.ds(NYB + s, 2 * TILE)]
        t = turned[pl.ds(s, 2 * TILE)]
        return (*inner_terms(t, h), t * t, h * h, *inner_terms(b, h), *inner_terms(b, t))

    th_re, th_im, tt, hh, bh_re, bh_im, bt_re, bt_im = sum_rows(blocks, 2 * TILE, terms, 8, poles)
    columns = [
        *inner_pair(th_re, th_im), lane_sum(tt), lane_sum(hh),
        *inner_pair(bh_re, bh_im), *inner_pair(bt_re, bt_im),
    ]
    store_chunk(chunk, edge_a, edge_b, me_ref[0], spots, turned, pack_columns(columns))


def third_kernel(
    me_ref, near, contact, pole_re, pole_im, scalars, rhs_ext, image_ext, half_ext, own, partner, other,
    near_side, far_side, ham, ovl, sigma,
    residual_own, direction_own, residual_rem, direction_rem, iterate, image, chunk, edge_a,
    edge_b, rho_out, turned_ext, wide, acc, mats, *sems,
):
    start_matrices(ham, ovl, sigma, mats, sems)
    blocks, poles = own.shape[0], own.shape[1]
    z = (pole_factor(pole_re), pole_factor(pole_im))
    spots = contact_spots(contact, me_ref[0], blocks)
    cols = len(spots)
    fill_extended(turned_ext, partner, own, other, me_ref[0], near_side, far_side, cols)
    sums = take_columns(gathered_sums(near_side, far_side, cols), 8)
    th, tt, hh, bh, bt = (sums[0], sums[1]), sums[2], sums[3], (sums[4], sums[5]), (sums[6], sums[7])
    norm_b, alpha = scalars[0], (scalars[1], scalars[2])
    turned_sq = tt + SMALL_EPS
    omega = (th[0] / turned_sq, th[1] / turned_sq)
    minus = complex_mul(omega, bt)
    rho_next = (bh[0] - minus[0], bh[1] - minus[1])
    zeros = jnp.zeros_like(tt)
    inverse_omega = guarded_quotient((turned_sq, zeros), th, tt * hh)
    ratio = complex_mul(rho_next, complex_mul(alpha, inverse_omega))
    beta = (ratio[0] / norm_b, ratio[1] / norm_b)
    rho_out[0] = rho_next[0]
    rho_out[1] = rho_next[1]
    rho_out[2] = norm_b

    def update(s, size):
        here = pl.ds(s, size)
        half = half_ext[here]
        residual = half - scale(omega, turned_ext[here])
        old = rhs_ext[here]
        direction = residual + scale(beta, old - scale(omega, image_ext[here]))
        store_wide(wide, s, size, direction)
        return residual, direction

    def update_own(s):
        residual, direction = update(NYB + s, 2 * TILE)
        residual_own[pl.ds(s, 2 * TILE)] = residual
        direction_own[pl.ds(s, 2 * TILE)] = direction
        here = pl.ds(NYB + s, 2 * TILE)
        iterate[pl.ds(s, 2 * TILE)] = scale(alpha, rhs_ext[here]) + scale(omega, half_ext[here])

    def update_rest(source, target, size):
        residual, direction = update(source, size)
        residual_rem[pl.ds(target, size)] = residual
        direction_rem[pl.ds(target, size)] = direction

    over_rows(blocks, 2 * TILE, update_own)
    update_rest(0, 0, NYB)
    update_rest(NYB + blocks, NYB, NYB)
    over_rows(CONTACT, 2 * TILE, lambda s: update_rest(2 * NYB + blocks + s, 2 * NYB + s, 2 * TILE))
    apply_operator(near, spots, z, wide, ham, ovl, sigma, mats, sems, acc, image)

    def terms(s):
        b, v = rhs_ext[pl.ds(NYB + s, 2 * TILE)], image[pl.ds(s, 2 * TILE)]
        return (*inner_terms(b, v), v * v)

    bv_re, bv_im, vv = sum_rows(blocks, 2 * TILE, terms, 3, poles)
    store_chunk(chunk, edge_a, edge_b, me_ref[0], spots, image, pack_columns([*inner_pair(bv_re, bv_im), lane_sum(vv)]))


def fourth_kernel(
    me_ref, near, contact, pole_re, pole_im, rho_in, residual_own, direction_own, residual_rem,
    direction_rem, iterate_in, own, partner, other, near_side, far_side, ham, ovl, sigma,
    half_own, turned, iterate, sums_out, contact_image, wide, acc, mats, *sems,
):
    start_matrices(ham, ovl, sigma, mats, sems)
    blocks, poles = own.shape[0], own.shape[1]
    z = (pole_factor(pole_re), pole_factor(pole_im))
    spots = contact_spots(contact, me_ref[0], blocks)
    cols = len(spots)
    place_gathered(contact_image, 0, me_ref[0], near_side, far_side, cols)
    bv_re, bv_im, vv = take_columns(gathered_sums(near_side, far_side, cols), 3)
    norm_b = rho_in[2]
    alpha = guarded_quotient((rho_in[0], rho_in[1]), (bv_re, bv_im), norm_b * vv)

    def update_own(s):
        here = pl.ds(s, 2 * TILE)
        half = residual_own[here] - scale(alpha, own[here])
        half_own[here] = half
        iterate[here] = iterate_in[here] + scale(alpha, direction_own[here])
        store_wide(wide, NYB + s, 2 * TILE, half)

    over_rows(blocks, 2 * TILE, update_own)
    for start, image in zip(halo_starts(me_ref[0], blocks), (partner, other)):
        remote = jnp.where(start == 0, 0, NYB)
        half = residual_rem[pl.ds(remote, NYB)] - scale(alpha, image[...])
        store_wide(wide, start, NYB, half)

    def update_contact(s):
        here = pl.ds(2 * NYB + s, 2 * TILE)
        half = residual_rem[here] - scale(alpha, contact_image[pl.ds(s, 2 * TILE)])
        store_wide(wide, 2 * NYB + blocks + s, 2 * TILE, half)

    over_rows(CONTACT, 2 * TILE, update_contact)
    apply_operator(near, spots, z, wide, ham, ovl, sigma, mats, sems, acc, turned)

    def terms(s):
        h, t = half_own[pl.ds(s, 2 * TILE)], turned[pl.ds(s, 2 * TILE)]
        return (*inner_terms(t, h), t * t)

    th_re, th_im, tt = sum_rows(blocks, 2 * TILE, terms, 3, poles)
    sums_out[0] = pack_columns([*inner_pair(th_re, th_im), lane_sum(tt)])


def last_kernel(near_side, far_side, half_own, turned, iterate, solution_out, residual_out):
    th_re, th_im, tt = take_columns(gathered_sums(near_side, far_side, 0), 3)
    turned_sq = tt + SMALL_EPS
    omega = (th_re / turned_sq, th_im / turned_sq)

    def update(s):
        here = pl.ds(s, 2 * TILE)
        half = half_own[here]
        solution_out[here] = iterate[here] + scale(omega, half)
        residual_out[here] = half - scale(omega, turned[here])

    over_rows(half_own.shape[0], 2 * TILE, update)


def local(rhs, ham, ovl, sigma, neighbours, contact, pole_real, pole_imag):
    blocks, poles = rhs.shape[0], rhs.shape[1]
    cols = contact.shape[0]
    count = lax.axis_size("gx")
    me = lax.axis_index("gx")
    first_block = me * blocks
    near = ((neighbours - first_block + NYB) % (blocks * count)).reshape(-1)
    me_ref = jnp.reshape(me, (1,)).astype(jnp.int32)
    ext = blocks + 2 * NYB + CONTACT

    def flip(value, mask):
        return lax.ppermute(value, "gx", [(i, i ^ mask) for i in range(count)])

    def exchange(chunk, edges=None, beside=None):
        parts = [chunk] + [flip(chunk, mask) for mask in range(4, count, 4)]
        far = ()
        if edges is not None:
            other = [(i, (i + 1 if i % 2 else i - 1) % count) for i in range(count)]
            far = (lax.ppermute(edges[1], "gx", other),)
        line = jnp.stack(parts)
        extra = ()
        if beside is not None:
            after, line = lax.optimization_barrier((near, line))
            extra = (beside(after),)
        plane = jnp.concatenate([line, flip(line, 2)])
        if edges is None:
            return plane, flip(plane, 1)
        far, extra, plane = lax.optimization_barrier((far, extra, plane))
        return (*extra, flip(edges[0], 1), *far, plane, flip(plane, 1))

    def vec_shape(rows):
        return jax.ShapeDtypeStruct((rows, poles, LANES), F32)

    slabs = (ham.reshape(-1, LANES, LANES), ovl.reshape(-1, LANES, LANES), sigma)
    small = pltpu.CompilerParams(vmem_limit_bytes=8 << 20)
    large = pltpu.CompilerParams(vmem_limit_bytes=43 << 20)
    wide = pltpu.VMEM((ext, 2 * poles, LANES), BF16)
    acc = pltpu.VMEM((sigma.shape[0], TILE * 2 * poles), F32)
    held = pltpu.VMEM((sum(m.shape[0] for m in slabs), LANES, LANES), BF16)
    parts = max(2, blocks // 32)
    sems = [pltpu.SemaphoreType.DMA((p,)) for p in (parts, parts, max(1, sigma.shape[0] // 128))]
    hbm = pl.BlockSpec(memory_space=pl.ANY)
    fixed = (me_ref, near, contact, pole_real, pole_imag)
    remote = 2 * NYB + CONTACT
    rows = cols + 1

    def call(kernel, inputs, out_rows, scratch, name):
        scratch = [pltpu.VMEM((r, poles, LANES), F32) for r in scratch]
        return pl.pallas_call(
            kernel,
            in_specs=[SMEM] * 5 + [VMEM] * (len(inputs) - 5) + [hbm] * 3,
            out_specs=[VMEM] * len(out_rows),
            out_shape=[vec_shape(r) for r in out_rows],
            scratch_shapes=[*scratch, wide, acc, held, *sems],
            compiler_params=large,
            name=name,
        )(*inputs, *slabs)

    chunk, *edges = pl.pallas_call(
        prepare_kernel,
        in_specs=[SMEM, SMEM, pl.BlockSpec(memory_space=pl.ANY)],
        out_specs=[VMEM] * 3,
        out_shape=[vec_shape(rows), vec_shape(NYB), vec_shape(NYB)],
        scratch_shapes=[pltpu.SemaphoreType.DMA((cols + 2,))],
        compiler_params=small,
        name="prepare",
    )(me_ref, contact, rhs)
    def own_part(near):
        return pl.pallas_call(
            functools.partial(own_kernel, 0),
            in_specs=[SMEM] * 3 + [VMEM] + [hbm] * 2,
            out_specs=VMEM,
            out_shape=vec_shape(blocks),
            scratch_shapes=[wide, held, *([pltpu.SemaphoreType.DMA((parts,))] * 2)],
            compiler_params=pltpu.CompilerParams(vmem_limit_bytes=50 << 20),
            cost_estimate=pl.CostEstimate(
                flops=4 * ham.size * 2 * poles, bytes_accessed=4 * ham.size, transcendentals=0
            ),
            name="own",
        )(near, pole_real, pole_imag, rhs, *slabs[:2])

    rhs_ext, image, chunk, edge_a, edge_b = call(
        first_kernel, (*fixed, rhs, *exchange(chunk, edges, own_part)),
        [ext, blocks, rows, NYB, NYB], [], "first",
    )
    image_ext, half_ext, turned, chunk, edge_a, edge_b, scalars = call(
        second_kernel, (*fixed, rhs_ext, image, *exchange(chunk, (edge_a, edge_b))),
        [ext, ext, blocks, rows, NYB, NYB, 3], [], "second",
    )
    res_own, dir_own, res_rem, dir_rem, iterate, image, chunk, edge_a, edge_b, rho = call(
        third_kernel,
        (*fixed, scalars, rhs_ext, image_ext, half_ext, turned, *exchange(chunk, (edge_a, edge_b))),
        [blocks, blocks, remote, remote, blocks, blocks, rows, NYB, NYB, 3], [ext], "third",
    )
    half_own, turned, iterate, sums = call(
        fourth_kernel,
        (*fixed, rho, res_own, dir_own, res_rem, dir_rem, iterate, image,
         *exchange(chunk, (edge_a, edge_b))),
        [blocks, blocks, blocks, 1], [CONTACT], "fourth",
    )
    return tuple(
        pl.pallas_call(
            last_kernel,
            in_specs=[VMEM] * 5,
            out_specs=[VMEM] * 2,
            out_shape=[vec_shape(blocks)] * 2,
            compiler_params=small,
            name="last",
        )(*exchange(sums), half_own, turned, iterate)
    )


def solution(mesh):
    return jax.shard_map(
        local,
        mesh=mesh,
        in_specs=(
            P("gx", "grp", None),
            P("gx", None, None, None),
            P("gx", None, None, None),
            P("gx", None, None),
            P("gx", None),
            P("gx"),
            P("grp"),
            P("grp"),
        ),
        out_specs=(P("gx", "grp", None), P("gx", "grp", None)),
        check_vma=False,
    )
```

```python
import functools

import jax
import jax.numpy as jnp
from jax import lax
from jax.experimental import pallas as pl
from jax.experimental.pallas import tpu as pltpu
from jax.sharding import PartitionSpec as P

BO = 64
NYB = 16
NNZ = 5
CONTACT = 128
LANES = 2 * BO
TILE = 16
FLOOR_SHARE = 0.0625
SMALL_EPS = 1e-06
F32 = jnp.float32
BF16 = jnp.bfloat16
VMEM = pl.BlockSpec(memory_space=pltpu.VMEM)
SMEM = pl.BlockSpec(memory_space=pltpu.SMEM)


def dot_nt(left, right):
    return lax.dot_general(left, right, (((1,), (1,)), ((), ())), preferred_element_type=F32)


def swap_halves(vec):
    return pltpu.roll(vec, BO, axis=vec.ndim - 1)


def half_sign(ndim):
    lane = lax.broadcasted_iota(jnp.int32, (1,) * (ndim - 1) + (LANES,), ndim - 1)
    return jnp.where(lane < BO, -1.0, 1.0).astype(F32)


def scale(factor, vec):
    fac_re = factor[0]
    fac_im = factor[1] * half_sign(2)
    return fac_re * vec + fac_im * swap_halves(vec)


def complex_mul(a, b):
    return (a[0] * b[0] - a[1] * b[1], a[0] * b[1] + a[1] * b[0])


def guarded_quotient(num, den, bound_sq):
    top = complex_mul(num, (den[0], -den[1]))
    size = jnp.maximum(den[0] * den[0] + den[1] * den[1], FLOOR_SHARE * bound_sq)
    return (top[0] / size, top[1] / size)


def spread(column):
    return jnp.broadcast_to(column, (column.shape[0], LANES))


def pack_columns(columns):
    poles = columns[0].shape[0]
    lane = lax.broadcasted_iota(jnp.int32, (poles, LANES), 1)
    packed = jnp.zeros((poles, LANES), F32)
    for index, column in enumerate(columns):
        packed = jnp.where(lane == index, column, packed)
    return packed


def take_columns(packed, count):
    return [spread(packed[:, index : index + 1]) for index in range(count)]


def lane_sum(vec):
    return jnp.sum(vec, axis=1, keepdims=True)


def store_wide(wide, start, rows, vec):
    lane = lax.broadcasted_iota(jnp.int32, (1, 1, LANES), 2)
    front = jnp.where(lane < BO, vec, -vec)
    wide[pl.ds(start, rows)] = jnp.concatenate([front, swap_halves(vec)], axis=1).astype(BF16)


def chunk_of(partner, me, count):
    slot = jnp.bitwise_xor(partner, me)
    inner = jnp.right_shift(slot, 1)
    y_bit = jnp.bitwise_and(inner, 1)
    return jnp.bitwise_and(slot, 1), y_bit * (count // 4) + jnp.right_shift(inner, 1)


def gathered_sums(near_side, far_side, row):
    total = None
    for index in range(near_side.shape[0]):
        pair = near_side[index, row] + far_side[index, row]
        total = pair if total is None else total + pair
    return total


def place_gathered(target, offset, me, near_side, far_side, cols):
    half = near_side.shape[0]
    for index in range(half):
        y_bit, z_part = index // (half // 2), index % (half // 2)
        partner = jnp.bitwise_xor(me, 2 * y_bit + 4 * z_part)
        target[pl.ds(offset + partner * cols, cols)] = near_side[index, :cols]
        partner = jnp.bitwise_xor(partner, 1)
        target[pl.ds(offset + partner * cols, cols)] = far_side[index, :cols]


def over_rows(count, step, body):
    def run(index, carry):
        body(pl.multiple_of(index * step, step))
        return carry

    lax.fori_loop(0, count // step, run, 0)


def sum_step(blocks):
    return min(4 * TILE, blocks)


def sum_rows(count, step, body, terms, poles):
    def run(index, carry):
        parts = body(pl.multiple_of(index * step, step))
        return tuple(c + jnp.sum(p, axis=0) for c, p in zip(carry, parts))

    zero = jnp.zeros((poles, LANES), F32)
    return lax.fori_loop(0, count // step, run, (zero,) * terms)


def contact_spots(contact, me, blocks):
    return [contact[l] - me * blocks for l in range(contact.shape[0])]


def halo_starts(me, blocks):
    odd = jnp.bitwise_and(me, 1)
    return (1 - odd) * (NYB + blocks), odd * (NYB + blocks)


def edge_start(kind, me, blocks):
    odd = jnp.bitwise_and(me, 1)
    return (1 - odd if kind == 0 else odd) * (blocks - NYB)


def fill_extended(ext, partner, own, other, me, near_side, far_side, cols):
    blocks = own.shape[0]
    partner_start, other_start = halo_starts(me, blocks)
    ext[pl.ds(partner_start, NYB)] = partner[...]
    ext[pl.ds(other_start, NYB)] = other[...]
    ext[NYB : NYB + blocks] = own[...]
    place_gathered(ext, 2 * NYB + blocks, me, near_side, far_side, cols)


def pole_factor(values):
    poles = values.shape[0]
    row = lax.broadcasted_iota(jnp.int32, (poles, LANES), 0)
    factor = jnp.zeros((poles, LANES), F32)
    for pole in range(poles):
        factor = jnp.where(row == pole, values[pole], factor)
    return factor


def combine(z, result):
    poles = z[0].shape[0]
    left = lax.broadcasted_iota(jnp.int32, (poles, LANES), 1) < BO
    top, low = result[:poles], result[poles:]
    ham_part = jnp.where(left, top, swap_halves(low))
    ovl_part = jnp.where(left, swap_halves(top), low)
    return scale(z, ovl_part) - ham_part


def ovl_base(blocks):
    return blocks * NNZ // 2


def sparse_block(mats, base, pair, index):
    half = index % 2
    return mats[base + NNZ * pair + index // 2, BO * half : BO * (half + 1)]


def sparse_group(near, z, wide, mats, blocks, image, first, count, shift=0):
    rows = 2 * image.shape[1]
    bases = (0, ovl_base(blocks))
    for pair in range(count // 2):
        b = first + 2 * pair
        vectors, matrices = [], []
        for q in range(2):
            vectors.append(jnp.concatenate([wide[near[(b + q) * NNZ + k]] for k in range(NNZ)], axis=1))
            for base in bases:
                pieces = [
                    sparse_block(mats, base, first // 2 + pair, q * NNZ + k) for k in range(NNZ)
                ]
                matrices.append(jnp.concatenate(pieces, axis=1))
        result = dot_nt(jnp.concatenate(vectors, axis=0), jnp.concatenate(matrices, axis=0))
        for q in range(2):
            image[b + q - shift] = combine(
                z, result[rows * q : rows * (q + 1), LANES * q : LANES * (q + 1)]
            )


def part_copy(source, mats, base, sem, part):
    size = source.shape[0] // sem.shape[0]
    return pltpu.make_async_copy(
        source.at[pl.ds(part * size, size)],
        mats.at[pl.ds(base + part * size, size)],
        sem.at[part],
    )


def start_sparse(ham, ovl, mats, sems):
    base = ovl_base(2 * ham.shape[0] // NNZ)
    for part in range(sems[0].shape[0]):
        part_copy(ham, mats, 0, sems[0], part).start()
        part_copy(ovl, mats, base, sems[1], part).start()


def start_sigma(sigma, mats, sem):
    base = mats.shape[0] - sigma.shape[0]
    for part in range(sem.shape[0]):
        part_copy(sigma, mats, base, sem, part).start()


def start_matrices(ham, ovl, sigma, mats, sems):
    start_sparse(ham, ovl, mats, sems)
    start_sigma(sigma, mats, sems[2])


def sparse_part(near, z, wide, ham, ovl, mats, sems, image):
    parts = sems[0].shape[0]
    blocks = image.shape[0]
    size = blocks // parts

    def step(part, carry):
        part_copy(ham, mats, 0, sems[0], part).wait()
        part_copy(ovl, mats, ovl_base(blocks), sems[1], part).wait()
        sparse_group(near, z, wide, mats, blocks, image, part * size, size)
        return carry

    lax.fori_loop(0, parts, step, 0)


def edge_part(near, z, wide, mats, image):
    blocks = image.shape[0]
    for first, slot in ((0, 2), (blocks - NYB, 1)):

        def step(group, carry, first=first, slot=slot):
            for index in range(8):
                pair = first // 2 + 8 * group + index
                for q in range(2):
                    b = 2 * pair + q
                    pieces = [
                        sparse_block(mats, base, pair, q * NNZ + slot)
                        for base in (0, ovl_base(blocks))
                    ]
                    product = dot_nt(wide[near[b * NNZ + slot]], jnp.concatenate(pieces, axis=0))
                    image[b] = image[b] + combine(z, product)
            return carry

        lax.fori_loop(0, NYB // 16, step, 0)


def contact_part(spots, wide, sigma, mats, sem, acc, image):
    blocks, poles = image.shape[0], image.shape[1]
    cols = len(spots)
    first_contact = blocks + 2 * NYB
    base = blocks * NNZ
    group_rows = sigma.shape[0] // sem.shape[0]
    width = TILE * 2 * poles
    row_t = lax.broadcasted_iota(jnp.int32, (TILE, width), 0)
    col_t = lax.broadcasted_iota(jnp.int32, (TILE, width), 1) // (2 * poles)
    keep = (row_t == col_t)[None]

    def step(group, carry):
        part_copy(sigma, mats, base, sem, group).wait()
        start = base + group * group_rows
        total = None
        for pair in range(CONTACT // (2 * TILE)):
            slabs, vectors = [], []
            for side in range(2):
                first = (2 * pair + side) * TILE
                slab = mats[pl.ds(start, group_rows), first : first + TILE]
                slabs.append(slab.reshape(group_rows * TILE, LANES))
                vectors.append(
                    wide[first_contact + first : first_contact + first + TILE].reshape(width, LANES)
                )
            part = dot_nt(jnp.concatenate(slabs, axis=1), jnp.concatenate(vectors, axis=1))
            total = part if total is None else total + part
        kept = jnp.where(keep, total.reshape(group_rows, TILE, width), 0.0)
        acc[pl.ds(pl.multiple_of(group * group_rows, group_rows), group_rows)] = jnp.sum(kept, axis=1)
        return carry

    lax.fori_loop(0, sem.shape[0], step, 0)
    fold_row = lax.broadcasted_iota(jnp.int32, (2 * poles, width), 0)
    fold_col = lax.broadcasted_iota(jnp.int32, (2 * poles, width), 1) % (2 * poles)
    fold = jnp.where(fold_row == fold_col, 1.0, 0.0).astype(BF16)
    rest = acc[...]
    folded = None
    for _ in range(2):
        piece = rest.astype(BF16)
        part = dot_nt(fold, piece)
        folded = part if folded is None else folded + part
        rest = rest - piece.astype(F32)
    for l in range(cols):
        column = slice(BO * l, BO * (l + 1))
        product = jnp.concatenate([folded[:poles, column], folded[poles:, column]], axis=1)
        spot = spots[l]
        image[spot] = image[spot] - product


def apply_operator(near, spots, z, wide, ham, ovl, sigma, mats, sems, acc, image):
    sparse_part(near, z, wide, ham, ovl, mats, sems, image)
    contact_part(spots, wide, sigma, mats, sems[2], acc, image)


def store_chunk(chunk, edge_a, edge_b, me, spots, image, sums):
    cols = len(spots)
    blocks = image.shape[0]
    edge_a[...] = image[pl.ds(edge_start(0, me, blocks), NYB)]
    edge_b[...] = image[pl.ds(edge_start(1, me, blocks), NYB)]
    for l in range(cols):
        chunk[l] = image[spots[l]]
    chunk[cols] = sums


def inner_terms(a, c):
    return a * c, a * swap_halves(c)


def inner_pair(re_acc, im_acc):
    return lane_sum(re_acc), lane_sum(im_acc * -half_sign(2))


def prepare_kernel(me_ref, contact, rhs, chunk, edge_a, edge_b, sem):
    blocks, poles = rhs.shape[0], rhs.shape[1]
    spots = contact_spots(contact, me_ref[0], blocks)
    cols = len(spots)
    copies = [pltpu.make_async_copy(rhs.at[spots[l]], chunk.at[l], sem.at[l]) for l in range(cols)]
    for kind, edge in enumerate((edge_a, edge_b)):
        here = pl.ds(edge_start(kind, me_ref[0], blocks), NYB)
        copies.append(pltpu.make_async_copy(rhs.at[here], edge, sem.at[cols + kind]))
    for copy in copies:
        copy.start()
    chunk[cols] = jnp.zeros((poles, LANES), F32)
    for copy in copies:
        copy.wait()


def own_kernel(first, near, pole_re, pole_im, own, ham, ovl, image, wide, mats, *sems):
    z = (pole_factor(pole_re), pole_factor(pole_im))
    blocks = own.shape[0]
    parts = sems[0].shape[0]
    size = image.shape[0] // parts
    slabs = size * NNZ // 2
    start = first * NNZ // 2

    def copies(part):
        for source, base, sem in ((ham, 0, sems[0]), (ovl, ovl_base(blocks), sems[1])):
            yield pltpu.make_async_copy(
                source.at[pl.ds(start + part * slabs, slabs)],
                mats.at[pl.ds(base + start + part * slabs, slabs)],
                sem.at[part],
            )

    for part in range(parts):
        for copy in copies(part):
            copy.start()
    wide[0:NYB] = jnp.zeros((NYB, *wide.shape[1:]), BF16)
    wide[NYB + blocks : 2 * NYB + blocks] = jnp.zeros((NYB, *wide.shape[1:]), BF16)
    low = max(0, first - NYB)
    needed = min(blocks, first + image.shape[0] + NYB) - low
    over_rows(
        needed, TILE,
        lambda s: store_wide(wide, NYB + low + s, TILE, own[pl.ds(low + s, TILE)]),
    )

    def step(part, carry):
        for copy in copies(part):
            copy.wait()
        sparse_group(
            near, z, wide, mats, blocks, image, first + part * size, size, shift=first
        )
        return carry

    lax.fori_loop(0, parts, step, 0)


def first_kernel(
    me_ref, near, contact, pole_re, pole_im, own, image_in, partner, other, near_side, far_side, ham, ovl, sigma,
    rhs_ext, image, chunk, edge_a, edge_b, wide, acc, mats, *sems,
):
    blocks, poles = own.shape[0], own.shape[1]
    z = (pole_factor(pole_re), pole_factor(pole_im))
    spots = contact_spots(contact, me_ref[0], blocks)
    edge_slabs = NYB * NNZ // 2
    edges = []
    for source, base, sem in ((ham, 0, sems[0]), (ovl, ovl_base(blocks), sems[1])):
        for side, start in enumerate((0, (blocks - NYB) * NNZ // 2)):
            edges.append(
                pltpu.make_async_copy(
                    source.at[pl.ds(start, edge_slabs)],
                    mats.at[pl.ds(base + start, edge_slabs)],
                    sem.at[side],
                )
            )
    for copy in edges:
        copy.start()
    start_sigma(sigma, mats, sems[2])
    fill_extended(rhs_ext, partner, own, other, me_ref[0], near_side, far_side, len(spots))
    store_wide(wide, 0, NYB, rhs_ext[0:NYB])
    over_rows(
        NYB + CONTACT, TILE,
        lambda s: store_wide(wide, NYB + blocks + s, TILE, rhs_ext[pl.ds(NYB + blocks + s, TILE)]),
    )
    image[...] = image_in[...]
    for copy in edges:
        copy.wait()
    edge_part(near, z, wide, mats, image)
    contact_part(spots, wide, sigma, mats, sems[2], acc, image)

    def terms(s):
        b, v = own[pl.ds(s, sum_step(blocks))], image[pl.ds(s, sum_step(blocks))]
        return (b * b, *inner_terms(b, v), v * v)

    bb, bv_re, bv_im, vv = sum_rows(blocks, sum_step(blocks), terms, 4, poles)
    store_chunk(
        chunk, edge_a, edge_b, me_ref[0], spots, image, pack_columns([lane_sum(bb), *inner_pair(bv_re, bv_im), lane_sum(vv)])
    )


def second_kernel(
    me_ref, near, contact, pole_re, pole_im, rhs_ext, own, partner, other, near_side, far_side, ham, ovl, sigma,
    image_ext, half_ext, turned, chunk, edge_a, edge_b, scalars, wide, acc, mats,
    *sems,
):
    start_matrices(ham, ovl, sigma, mats, sems)
    blocks, poles = own.shape[0], own.shape[1]
    z = (pole_factor(pole_re), pole_factor(pole_im))
    spots = contact_spots(contact, me_ref[0], blocks)
    cols = len(spots)
    fill_extended(image_ext, partner, own, other, me_ref[0], near_side, far_side, cols)
    norm_b, bv_re, bv_im, vv = take_columns(gathered_sums(near_side, far_side, cols), 4)
    alpha = guarded_quotient((norm_b, jnp.zeros_like(norm_b)), (bv_re, bv_im), norm_b * vv)
    scalars[0] = norm_b
    scalars[1] = alpha[0]
    scalars[2] = alpha[1]

    def update(s):
        here = pl.ds(s, 2 * TILE)
        half = rhs_ext[here] - scale(alpha, image_ext[here])
        half_ext[here] = half
        store_wide(wide, s, 2 * TILE, half)

    over_rows(half_ext.shape[0], 2 * TILE, update)
    apply_operator(near, spots, z, wide, ham, ovl, sigma, mats, sems, acc, turned)

    def terms(s):
        b = rhs_ext[pl.ds(NYB + s, sum_step(blocks))]
        h = half_ext[pl.ds(NYB + s, sum_step(blocks))]
        t = turned[pl.ds(s, sum_step(blocks))]
        return (*inner_terms(t, h), t * t, h * h, *inner_terms(b, h), *inner_terms(b, t))

    th_re, th_im, tt, hh, bh_re, bh_im, bt_re, bt_im = sum_rows(blocks, sum_step(blocks), terms, 8, poles)
    columns = [
        *inner_pair(th_re, th_im), lane_sum(tt), lane_sum(hh),
        *inner_pair(bh_re, bh_im), *inner_pair(bt_re, bt_im),
    ]
    store_chunk(chunk, edge_a, edge_b, me_ref[0], spots, turned, pack_columns(columns))


def third_kernel(
    me_ref, near, contact, pole_re, pole_im, scalars, rhs_ext, image_ext, half_ext, own, partner, other,
    near_side, far_side, ham, ovl, sigma,
    residual_own, direction_own, residual_rem, direction_rem, iterate, image, chunk, edge_a,
    edge_b, rho_out, turned_ext, wide, acc, mats, *sems,
):
    start_matrices(ham, ovl, sigma, mats, sems)
    blocks, poles = own.shape[0], own.shape[1]
    z = (pole_factor(pole_re), pole_factor(pole_im))
    spots = contact_spots(contact, me_ref[0], blocks)
    cols = len(spots)
    fill_extended(turned_ext, partner, own, other, me_ref[0], near_side, far_side, cols)
    sums = take_columns(gathered_sums(near_side, far_side, cols), 8)
    th, tt, hh, bh, bt = (sums[0], sums[1]), sums[2], sums[3], (sums[4], sums[5]), (sums[6], sums[7])
    norm_b, alpha = scalars[0], (scalars[1], scalars[2])
    turned_sq = tt + SMALL_EPS
    omega = (th[0] / turned_sq, th[1] / turned_sq)
    minus = complex_mul(omega, bt)
    rho_next = (bh[0] - minus[0], bh[1] - minus[1])
    zeros = jnp.zeros_like(tt)
    inverse_omega = guarded_quotient((turned_sq, zeros), th, tt * hh)
    ratio = complex_mul(rho_next, complex_mul(alpha, inverse_omega))
    beta = (ratio[0] / norm_b, ratio[1] / norm_b)
    rho_out[0] = rho_next[0]
    rho_out[1] = rho_next[1]
    rho_out[2] = norm_b

    def update(s, size):
        here = pl.ds(s, size)
        half = half_ext[here]
        residual = half - scale(omega, turned_ext[here])
        old = rhs_ext[here]
        direction = residual + scale(beta, old - scale(omega, image_ext[here]))
        store_wide(wide, s, size, direction)
        return residual, direction

    def update_own(s):
        residual, direction = update(NYB + s, 2 * TILE)
        residual_own[pl.ds(s, 2 * TILE)] = residual
        direction_own[pl.ds(s, 2 * TILE)] = direction
        here = pl.ds(NYB + s, 2 * TILE)
        iterate[pl.ds(s, 2 * TILE)] = scale(alpha, rhs_ext[here]) + scale(omega, half_ext[here])

    def update_rest(source, target, size):
        residual, direction = update(source, size)
        residual_rem[pl.ds(target, size)] = residual
        direction_rem[pl.ds(target, size)] = direction

    over_rows(blocks, 2 * TILE, update_own)
    update_rest(0, 0, NYB)
    update_rest(NYB + blocks, NYB, NYB)
    over_rows(CONTACT, 2 * TILE, lambda s: update_rest(2 * NYB + blocks + s, 2 * NYB + s, 2 * TILE))
    apply_operator(near, spots, z, wide, ham, ovl, sigma, mats, sems, acc, image)

    def terms(s):
        b, v = rhs_ext[pl.ds(NYB + s, sum_step(blocks))], image[pl.ds(s, sum_step(blocks))]
        return (*inner_terms(b, v), v * v)

    bv_re, bv_im, vv = sum_rows(blocks, sum_step(blocks), terms, 3, poles)
    store_chunk(chunk, edge_a, edge_b, me_ref[0], spots, image, pack_columns([*inner_pair(bv_re, bv_im), lane_sum(vv)]))


def fourth_kernel(
    me_ref, near, contact, pole_re, pole_im, rho_in, residual_own, direction_own, residual_rem,
    direction_rem, iterate_in, own, partner, other, near_side, far_side, ham, ovl, sigma,
    half_own, turned, iterate, sums_out, contact_image, wide, acc, mats, *sems,
):
    start_matrices(ham, ovl, sigma, mats, sems)
    blocks, poles = own.shape[0], own.shape[1]
    z = (pole_factor(pole_re), pole_factor(pole_im))
    spots = contact_spots(contact, me_ref[0], blocks)
    cols = len(spots)
    place_gathered(contact_image, 0, me_ref[0], near_side, far_side, cols)
    bv_re, bv_im, vv = take_columns(gathered_sums(near_side, far_side, cols), 3)
    norm_b = rho_in[2]
    alpha = guarded_quotient((rho_in[0], rho_in[1]), (bv_re, bv_im), norm_b * vv)

    def update_own(s):
        here = pl.ds(s, 2 * TILE)
        half = residual_own[here] - scale(alpha, own[here])
        half_own[here] = half
        iterate[here] = iterate_in[here] + scale(alpha, direction_own[here])
        store_wide(wide, NYB + s, 2 * TILE, half)

    over_rows(blocks, 2 * TILE, update_own)
    for start, image in zip(halo_starts(me_ref[0], blocks), (partner, other)):
        remote = jnp.where(start == 0, 0, NYB)
        half = residual_rem[pl.ds(remote, NYB)] - scale(alpha, image[...])
        store_wide(wide, start, NYB, half)

    def update_contact(s):
        here = pl.ds(2 * NYB + s, 2 * TILE)
        half = residual_rem[here] - scale(alpha, contact_image[pl.ds(s, 2 * TILE)])
        store_wide(wide, 2 * NYB + blocks + s, 2 * TILE, half)

    over_rows(CONTACT, 2 * TILE, update_contact)
    apply_operator(near, spots, z, wide, ham, ovl, sigma, mats, sems, acc, turned)

    def terms(s):
        h, t = half_own[pl.ds(s, sum_step(blocks))], turned[pl.ds(s, sum_step(blocks))]
        return (*inner_terms(t, h), t * t)

    th_re, th_im, tt = sum_rows(blocks, sum_step(blocks), terms, 3, poles)
    sums_out[0] = pack_columns([*inner_pair(th_re, th_im), lane_sum(tt)])


def last_kernel(near_side, far_side, half_own, turned, iterate, solution_out, residual_out):
    th_re, th_im, tt = take_columns(gathered_sums(near_side, far_side, 0), 3)
    turned_sq = tt + SMALL_EPS
    omega = (th_re / turned_sq, th_im / turned_sq)

    def update(s):
        here = pl.ds(s, 2 * TILE)
        half = half_own[here]
        solution_out[here] = iterate[here] + scale(omega, half)
        residual_out[here] = half - scale(omega, turned[here])

    over_rows(half_own.shape[0], 2 * TILE, update)


def local(rhs, ham, ovl, sigma, neighbours, contact, pole_real, pole_imag):
    blocks, poles = rhs.shape[0], rhs.shape[1]
    cols = contact.shape[0]
    count = lax.axis_size("gx")
    me = lax.axis_index("gx")
    first_block = me * blocks
    near = ((neighbours - first_block + NYB) % (blocks * count)).reshape(-1)
    me_ref = jnp.reshape(me, (1,)).astype(jnp.int32)
    ext = blocks + 2 * NYB + CONTACT

    def flip(value, mask):
        return lax.ppermute(value, "gx", [(i, i ^ mask) for i in range(count)])

    def exchange(chunk, edges=None, beside=None):
        parts = [chunk] + [flip(chunk, mask) for mask in range(4, count, 4)]
        far = ()
        if edges is not None:
            other = [(i, (i + 1 if i % 2 else i - 1) % count) for i in range(count)]
            far = (lax.ppermute(edges[1], "gx", other),)
        line = jnp.stack(parts)
        extra = ()
        if beside is not None:
            after, line = lax.optimization_barrier((near, line))
            extra = (beside(after),)
        plane = jnp.concatenate([line, flip(line, 2)])
        if edges is None:
            return plane, flip(plane, 1)
        far, extra, plane = lax.optimization_barrier((far, extra, plane))
        return (*extra, flip(edges[0], 1), *far, plane, flip(plane, 1))

    def vec_shape(rows):
        return jax.ShapeDtypeStruct((rows, poles, LANES), F32)

    slabs = (ham.reshape(-1, LANES, LANES), ovl.reshape(-1, LANES, LANES), sigma)
    small = pltpu.CompilerParams(vmem_limit_bytes=8 << 20)
    large = pltpu.CompilerParams(vmem_limit_bytes=43 << 20)
    wide = pltpu.VMEM((ext, 2 * poles, LANES), BF16)
    acc = pltpu.VMEM((sigma.shape[0], TILE * 2 * poles), F32)
    held = pltpu.VMEM((sum(m.shape[0] for m in slabs), LANES, LANES), BF16)
    parts = max(2, blocks // 32)
    sems = [pltpu.SemaphoreType.DMA((p,)) for p in (parts, parts, max(1, sigma.shape[0] // 128))]
    hbm = pl.BlockSpec(memory_space=pl.ANY)
    fixed = (me_ref, near, contact, pole_real, pole_imag)
    remote = 2 * NYB + CONTACT
    rows = cols + 1

    def call(kernel, inputs, out_rows, scratch, name):
        scratch = [pltpu.VMEM((r, poles, LANES), F32) for r in scratch]
        return pl.pallas_call(
            kernel,
            in_specs=[SMEM] * 5 + [VMEM] * (len(inputs) - 5) + [hbm] * 3,
            out_specs=[VMEM] * len(out_rows),
            out_shape=[vec_shape(r) for r in out_rows],
            scratch_shapes=[*scratch, wide, acc, held, *sems],
            compiler_params=large,
            name=name,
        )(*inputs, *slabs)

    chunk, *edges = pl.pallas_call(
        prepare_kernel,
        in_specs=[SMEM, SMEM, pl.BlockSpec(memory_space=pl.ANY)],
        out_specs=[VMEM] * 3,
        out_shape=[vec_shape(rows), vec_shape(NYB), vec_shape(NYB)],
        scratch_shapes=[pltpu.SemaphoreType.DMA((cols + 2,))],
        compiler_params=small,
        name="prepare",
    )(me_ref, contact, rhs)
    def own_part(near):
        return pl.pallas_call(
            functools.partial(own_kernel, 0),
            in_specs=[SMEM] * 3 + [VMEM] + [hbm] * 2,
            out_specs=VMEM,
            out_shape=vec_shape(blocks),
            scratch_shapes=[wide, held, *([pltpu.SemaphoreType.DMA((parts,))] * 2)],
            compiler_params=pltpu.CompilerParams(vmem_limit_bytes=50 << 20),
            cost_estimate=pl.CostEstimate(
                flops=4 * ham.size * 2 * poles, bytes_accessed=4 * ham.size, transcendentals=0
            ),
            name="own",
        )(near, pole_real, pole_imag, rhs, *slabs[:2])

    rhs_ext, image, chunk, edge_a, edge_b = call(
        first_kernel, (*fixed, rhs, *exchange(chunk, edges, own_part)),
        [ext, blocks, rows, NYB, NYB], [], "first",
    )
    image_ext, half_ext, turned, chunk, edge_a, edge_b, scalars = call(
        second_kernel, (*fixed, rhs_ext, image, *exchange(chunk, (edge_a, edge_b))),
        [ext, ext, blocks, rows, NYB, NYB, 3], [], "second",
    )
    res_own, dir_own, res_rem, dir_rem, iterate, image, chunk, edge_a, edge_b, rho = call(
        third_kernel,
        (*fixed, scalars, rhs_ext, image_ext, half_ext, turned, *exchange(chunk, (edge_a, edge_b))),
        [blocks, blocks, remote, remote, blocks, blocks, rows, NYB, NYB, 3], [ext], "third",
    )
    half_own, turned, iterate, sums = call(
        fourth_kernel,
        (*fixed, rho, res_own, dir_own, res_rem, dir_rem, iterate, image,
         *exchange(chunk, (edge_a, edge_b))),
        [blocks, blocks, blocks, 1], [CONTACT], "fourth",
    )
    return tuple(
        pl.pallas_call(
            last_kernel,
            in_specs=[VMEM] * 5,
            out_specs=[VMEM] * 2,
            out_shape=[vec_shape(blocks)] * 2,
            compiler_params=small,
            name="last",
        )(*exchange(sums), half_own, turned, iterate)
    )


def solution(mesh):
    return jax.shard_map(
        local,
        mesh=mesh,
        in_specs=(
            P("gx", "grp", None),
            P("gx", None, None, None),
            P("gx", None, None, None),
            P("gx", None, None),
            P("gx", None),
            P("gx"),
            P("grp"),
            P("grp"),
        ),
        out_specs=(P("gx", "grp", None), P("gx", "grp", None)),
        check_vma=False,
    )
```

```python
import functools

import jax
import jax.numpy as jnp
from jax import lax
from jax.experimental import pallas as pl
from jax.experimental.pallas import tpu as pltpu
from jax.sharding import PartitionSpec as P

BO = 64
NYB = 16
NNZ = 5
CONTACT = 128
LANES = 2 * BO
TILE = 16
FLOOR_SHARE = 0.0625
SMALL_EPS = 1e-06
F32 = jnp.float32
BF16 = jnp.bfloat16
VMEM = pl.BlockSpec(memory_space=pltpu.VMEM)
SMEM = pl.BlockSpec(memory_space=pltpu.SMEM)


def dot_nt(left, right):
    return lax.dot_general(left, right, (((1,), (1,)), ((), ())), preferred_element_type=F32)


def swap_halves(vec):
    return pltpu.roll(vec, BO, axis=vec.ndim - 1)


def half_sign(ndim):
    lane = lax.broadcasted_iota(jnp.int32, (1,) * (ndim - 1) + (LANES,), ndim - 1)
    return jnp.where(lane < BO, -1.0, 1.0).astype(F32)


def scale(factor, vec):
    fac_re = factor[0]
    fac_im = factor[1] * half_sign(2)
    return fac_re * vec + fac_im * swap_halves(vec)


def complex_mul(a, b):
    return (a[0] * b[0] - a[1] * b[1], a[0] * b[1] + a[1] * b[0])


def guarded_quotient(num, den, bound_sq):
    top = complex_mul(num, (den[0], -den[1]))
    size = jnp.maximum(den[0] * den[0] + den[1] * den[1], FLOOR_SHARE * bound_sq)
    return (top[0] / size, top[1] / size)


def spread(column):
    return jnp.broadcast_to(column, (column.shape[0], LANES))


def pack_columns(columns):
    poles = columns[0].shape[0]
    lane = lax.broadcasted_iota(jnp.int32, (poles, LANES), 1)
    packed = jnp.zeros((poles, LANES), F32)
    for index, column in enumerate(columns):
        packed = jnp.where(lane == index, column, packed)
    return packed


def take_columns(packed, count):
    return [spread(packed[:, index : index + 1]) for index in range(count)]


def lane_sum(vec):
    return jnp.sum(vec, axis=1, keepdims=True)


def store_wide(wide, start, rows, vec):
    lane = lax.broadcasted_iota(jnp.int32, (1, 1, LANES), 2)
    front = jnp.where(lane < BO, vec, -vec)
    wide[pl.ds(start, rows)] = jnp.concatenate([front, swap_halves(vec)], axis=1).astype(BF16)


def chunk_of(partner, me, count):
    slot = jnp.bitwise_xor(partner, me)
    inner = jnp.right_shift(slot, 1)
    y_bit = jnp.bitwise_and(inner, 1)
    return jnp.bitwise_and(slot, 1), y_bit * (count // 4) + jnp.right_shift(inner, 1)


def gathered_sums(near_side, far_side, row):
    total = None
    for index in range(near_side.shape[0]):
        pair = near_side[index, row] + far_side[index, row]
        total = pair if total is None else total + pair
    return total


def place_gathered(target, offset, me, near_side, far_side, cols):
    half = near_side.shape[0]
    for index in range(half):
        y_bit, z_part = index // (half // 2), index % (half // 2)
        partner = jnp.bitwise_xor(me, 2 * y_bit + 4 * z_part)
        target[pl.ds(offset + partner * cols, cols)] = near_side[index, :cols]
        partner = jnp.bitwise_xor(partner, 1)
        target[pl.ds(offset + partner * cols, cols)] = far_side[index, :cols]


def over_rows(count, step, body):
    def run(index, carry):
        body(pl.multiple_of(index * step, step))
        return carry

    lax.fori_loop(0, count // step, run, 0)


def sum_step(blocks):
    return min(4 * TILE, blocks)


def sum_rows(count, step, body, terms, poles):
    def run(index, carry):
        parts = body(pl.multiple_of(index * step, step))
        return tuple(c + jnp.sum(p, axis=0) for c, p in zip(carry, parts))

    zero = jnp.zeros((poles, LANES), F32)
    return lax.fori_loop(0, count // step, run, (zero,) * terms)


def contact_spots(contact, me, blocks):
    return [contact[l] - me * blocks for l in range(contact.shape[0])]


def halo_starts(me, blocks):
    odd = jnp.bitwise_and(me, 1)
    return (1 - odd) * (NYB + blocks), odd * (NYB + blocks)


def edge_start(kind, me, blocks):
    odd = jnp.bitwise_and(me, 1)
    return (1 - odd if kind == 0 else odd) * (blocks - NYB)


def fill_extended(ext, partner, own, other, me, near_side, far_side, cols):
    blocks = own.shape[0]
    partner_start, other_start = halo_starts(me, blocks)
    ext[pl.ds(partner_start, NYB)] = partner[...]
    ext[pl.ds(other_start, NYB)] = other[...]
    ext[NYB : NYB + blocks] = own[...]
    place_gathered(ext, 2 * NYB + blocks, me, near_side, far_side, cols)


def pole_factor(values, part):
    poles = values.shape[0] // 2
    row = lax.broadcasted_iota(jnp.int32, (poles, LANES), 0)
    factor = jnp.zeros((poles, LANES), F32)
    for pole in range(poles):
        factor = jnp.where(row == pole, values[part * poles + pole], factor)
    return factor


def combine(z, result):
    poles = z[0].shape[0]
    left = lax.broadcasted_iota(jnp.int32, (poles, LANES), 1) < BO
    top, low = result[:poles], result[poles:]
    ham_part = jnp.where(left, top, swap_halves(low))
    ovl_part = jnp.where(left, swap_halves(top), low)
    return scale(z, ovl_part) - ham_part


def ovl_base(blocks):
    return blocks * NNZ // 2


def sparse_block(mats, base, pair, index):
    half = index % 2
    return mats[base + NNZ * pair + index // 2, BO * half : BO * (half + 1)]


def sparse_group(near, z, wide, mats, blocks, image, first, count, shift=0):
    rows = 2 * image.shape[1]
    bases = (0, ovl_base(blocks))
    for pair in range(count // 2):
        b = first + 2 * pair
        vectors, matrices = [], []
        for q in range(2):
            vectors.append(jnp.concatenate([wide[near[(b + q) * NNZ + k]] for k in range(NNZ)], axis=1))
            for base in bases:
                pieces = [
                    sparse_block(mats, base, first // 2 + pair, q * NNZ + k) for k in range(NNZ)
                ]
                matrices.append(jnp.concatenate(pieces, axis=1))
        result = dot_nt(jnp.concatenate(vectors, axis=0), jnp.concatenate(matrices, axis=0))
        for q in range(2):
            image[b + q - shift] = combine(
                z, result[rows * q : rows * (q + 1), LANES * q : LANES * (q + 1)]
            )


def part_copy(source, mats, base, sem, part):
    size = source.shape[0] // sem.shape[0]
    return pltpu.make_async_copy(
        source.at[pl.ds(part * size, size)],
        mats.at[pl.ds(base + part * size, size)],
        sem.at[part],
    )


def start_sparse(ham, ovl, mats, sems):
    base = ovl_base(2 * ham.shape[0] // NNZ)
    for part in range(sems[0].shape[0]):
        part_copy(ham, mats, 0, sems[0], part).start()
        part_copy(ovl, mats, base, sems[1], part).start()


def start_sigma(sigma, mats, sem):
    base = mats.shape[0] - sigma.shape[0]
    for part in range(sem.shape[0]):
        part_copy(sigma, mats, base, sem, part).start()


def start_matrices(ham, ovl, sigma, mats, sems):
    start_sparse(ham, ovl, mats, sems)
    start_sigma(sigma, mats, sems[2])


def sparse_part(near, z, wide, ham, ovl, mats, sems, image):
    parts = sems[0].shape[0]
    blocks = image.shape[0]
    size = blocks // parts

    def step(part, carry):
        part_copy(ham, mats, 0, sems[0], part).wait()
        part_copy(ovl, mats, ovl_base(blocks), sems[1], part).wait()
        sparse_group(near, z, wide, mats, blocks, image, part * size, size)
        return carry

    lax.fori_loop(0, parts, step, 0)


def edge_part(near, z, wide, mats, image):
    blocks = image.shape[0]
    for first, slot in ((0, 2), (blocks - NYB, 1)):

        def step(group, carry, first=first, slot=slot):
            for index in range(8):
                pair = first // 2 + 8 * group + index
                for q in range(2):
                    b = 2 * pair + q
                    pieces = [
                        sparse_block(mats, base, pair, q * NNZ + slot)
                        for base in (0, ovl_base(blocks))
                    ]
                    product = dot_nt(wide[near[b * NNZ + slot]], jnp.concatenate(pieces, axis=0))
                    image[b] = image[b] + combine(z, product)
            return carry

        lax.fori_loop(0, NYB // 16, step, 0)


def contact_part(spots, wide, sigma, mats, sem, acc, image):
    blocks, poles = image.shape[0], image.shape[1]
    cols = len(spots)
    first_contact = blocks + 2 * NYB
    base = blocks * NNZ
    group_rows = sigma.shape[0] // sem.shape[0]
    width = TILE * 2 * poles
    row_t = lax.broadcasted_iota(jnp.int32, (TILE, width), 0)
    col_t = lax.broadcasted_iota(jnp.int32, (TILE, width), 1) // (2 * poles)
    keep = (row_t == col_t)[None]

    def step(group, carry):
        part_copy(sigma, mats, base, sem, group).wait()
        start = base + group * group_rows
        total = None
        for pair in range(CONTACT // (2 * TILE)):
            slabs, vectors = [], []
            for side in range(2):
                first = (2 * pair + side) * TILE
                slab = mats[pl.ds(start, group_rows), first : first + TILE]
                slabs.append(slab.reshape(group_rows * TILE, LANES))
                vectors.append(
                    wide[first_contact + first : first_contact + first + TILE].reshape(width, LANES)
                )
            part = dot_nt(jnp.concatenate(slabs, axis=1), jnp.concatenate(vectors, axis=1))
            total = part if total is None else total + part
        kept = jnp.where(keep, total.reshape(group_rows, TILE, width), 0.0)
        acc[pl.ds(pl.multiple_of(group * group_rows, group_rows), group_rows)] = jnp.sum(kept, axis=1)
        return carry

    lax.fori_loop(0, sem.shape[0], step, 0)
    fold_row = lax.broadcasted_iota(jnp.int32, (2 * poles, width), 0)
    fold_col = lax.broadcasted_iota(jnp.int32, (2 * poles, width), 1) % (2 * poles)
    fold = jnp.where(fold_row == fold_col, 1.0, 0.0).astype(BF16)
    rest = acc[...]
    folded = None
    for _ in range(2):
        piece = rest.astype(BF16)
        part = dot_nt(fold, piece)
        folded = part if folded is None else folded + part
        rest = rest - piece.astype(F32)
    for l in range(cols):
        column = slice(BO * l, BO * (l + 1))
        product = jnp.concatenate([folded[:poles, column], folded[poles:, column]], axis=1)
        spot = spots[l]
        image[spot] = image[spot] - product


def apply_operator(near, spots, z, wide, ham, ovl, sigma, mats, sems, acc, image):
    sparse_part(near, z, wide, ham, ovl, mats, sems, image)
    contact_part(spots, wide, sigma, mats, sems[2], acc, image)


def store_chunk(chunk, edge_a, edge_b, me, spots, image, sums):
    cols = len(spots)
    blocks = image.shape[0]
    edge_a[...] = image[pl.ds(edge_start(0, me, blocks), NYB)]
    edge_b[...] = image[pl.ds(edge_start(1, me, blocks), NYB)]
    for l in range(cols):
        chunk[l] = image[spots[l]]
    chunk[cols] = sums


def inner_terms(a, c):
    return a * c, a * swap_halves(c)


def inner_pair(re_acc, im_acc):
    return lane_sum(re_acc), lane_sum(im_acc * -half_sign(2))


def prepare_kernel(me_ref, contact, rhs, chunk, edge_a, edge_b, sem):
    blocks, poles = rhs.shape[0], rhs.shape[1]
    spots = contact_spots(contact, me_ref[0], blocks)
    cols = len(spots)
    copies = [pltpu.make_async_copy(rhs.at[spots[l]], chunk.at[l], sem.at[l]) for l in range(cols)]
    for kind, edge in enumerate((edge_a, edge_b)):
        here = pl.ds(edge_start(kind, me_ref[0], blocks), NYB)
        copies.append(pltpu.make_async_copy(rhs.at[here], edge, sem.at[cols + kind]))
    for copy in copies:
        copy.start()
    chunk[cols] = jnp.zeros((poles, LANES), F32)
    for copy in copies:
        copy.wait()


def own_kernel(first, near, pole_ref, own, ham, ovl, image, wide, mats, *sems):
    z = (pole_factor(pole_ref, 0), pole_factor(pole_ref, 1))
    blocks = own.shape[0]
    parts = sems[0].shape[0]
    size = image.shape[0] // parts
    slabs = size * NNZ // 2
    start = first * NNZ // 2

    def copies(part):
        for source, base, sem in ((ham, 0, sems[0]), (ovl, ovl_base(blocks), sems[1])):
            yield pltpu.make_async_copy(
                source.at[pl.ds(start + part * slabs, slabs)],
                mats.at[pl.ds(base + start + part * slabs, slabs)],
                sem.at[part],
            )

    for part in range(parts):
        for copy in copies(part):
            copy.start()
    wide[0:NYB] = jnp.zeros((NYB, *wide.shape[1:]), BF16)
    wide[NYB + blocks : 2 * NYB + blocks] = jnp.zeros((NYB, *wide.shape[1:]), BF16)
    low = max(0, first - NYB)
    needed = min(blocks, first + image.shape[0] + NYB) - low
    over_rows(
        needed, TILE,
        lambda s: store_wide(wide, NYB + low + s, TILE, own[pl.ds(low + s, TILE)]),
    )

    def step(part, carry):
        for copy in copies(part):
            copy.wait()
        sparse_group(
            near, z, wide, mats, blocks, image, first + part * size, size, shift=first
        )
        return carry

    lax.fori_loop(0, parts, step, 0)


def first_kernel(
    me_ref, near, contact, pole_ref, own, image_in, partner, other, near_side, far_side, ham, ovl, sigma,
    rhs_ext, image, chunk, edge_a, edge_b, wide, acc, mats, *sems,
):
    blocks, poles = own.shape[0], own.shape[1]
    z = (pole_factor(pole_ref, 0), pole_factor(pole_ref, 1))
    spots = contact_spots(contact, me_ref[0], blocks)
    edge_slabs = NYB * NNZ // 2
    edges = []
    for source, base, sem in ((ham, 0, sems[0]), (ovl, ovl_base(blocks), sems[1])):
        for side, start in enumerate((0, (blocks - NYB) * NNZ // 2)):
            edges.append(
                pltpu.make_async_copy(
                    source.at[pl.ds(start, edge_slabs)],
                    mats.at[pl.ds(base + start, edge_slabs)],
                    sem.at[side],
                )
            )
    for copy in edges:
        copy.start()
    start_sigma(sigma, mats, sems[2])
    fill_extended(rhs_ext, partner, own, other, me_ref[0], near_side, far_side, len(spots))
    store_wide(wide, 0, NYB, rhs_ext[0:NYB])
    over_rows(
        NYB + CONTACT, TILE,
        lambda s: store_wide(wide, NYB + blocks + s, TILE, rhs_ext[pl.ds(NYB + blocks + s, TILE)]),
    )
    image[...] = image_in[...]
    for copy in edges:
        copy.wait()
    edge_part(near, z, wide, mats, image)
    contact_part(spots, wide, sigma, mats, sems[2], acc, image)

    def terms(s):
        b, v = own[pl.ds(s, sum_step(blocks))], image[pl.ds(s, sum_step(blocks))]
        return (b * b, *inner_terms(b, v), v * v)

    bb, bv_re, bv_im, vv = sum_rows(blocks, sum_step(blocks), terms, 4, poles)
    store_chunk(
        chunk, edge_a, edge_b, me_ref[0], spots, image, pack_columns([lane_sum(bb), *inner_pair(bv_re, bv_im), lane_sum(vv)])
    )


def second_kernel(
    me_ref, near, contact, pole_ref, rhs_ext, own, partner, other, near_side, far_side, ham, ovl, sigma,
    image_ext, half_ext, turned, chunk, edge_a, edge_b, scalars, wide, acc, mats,
    *sems,
):
    start_matrices(ham, ovl, sigma, mats, sems)
    blocks, poles = own.shape[0], own.shape[1]
    z = (pole_factor(pole_ref, 0), pole_factor(pole_ref, 1))
    spots = contact_spots(contact, me_ref[0], blocks)
    cols = len(spots)
    fill_extended(image_ext, partner, own, other, me_ref[0], near_side, far_side, cols)
    norm_b, bv_re, bv_im, vv = take_columns(gathered_sums(near_side, far_side, cols), 4)
    alpha = guarded_quotient((norm_b, jnp.zeros_like(norm_b)), (bv_re, bv_im), norm_b * vv)
    scalars[0] = norm_b
    scalars[1] = alpha[0]
    scalars[2] = alpha[1]

    def update(s):
        here = pl.ds(s, 2 * TILE)
        half = rhs_ext[here] - scale(alpha, image_ext[here])
        half_ext[here] = half
        store_wide(wide, s, 2 * TILE, half)

    over_rows(half_ext.shape[0], 2 * TILE, update)
    apply_operator(near, spots, z, wide, ham, ovl, sigma, mats, sems, acc, turned)

    def terms(s):
        b = rhs_ext[pl.ds(NYB + s, sum_step(blocks))]
        h = half_ext[pl.ds(NYB + s, sum_step(blocks))]
        t = turned[pl.ds(s, sum_step(blocks))]
        return (*inner_terms(t, h), t * t, h * h, *inner_terms(b, h), *inner_terms(b, t))

    th_re, th_im, tt, hh, bh_re, bh_im, bt_re, bt_im = sum_rows(blocks, sum_step(blocks), terms, 8, poles)
    columns = [
        *inner_pair(th_re, th_im), lane_sum(tt), lane_sum(hh),
        *inner_pair(bh_re, bh_im), *inner_pair(bt_re, bt_im),
    ]
    store_chunk(chunk, edge_a, edge_b, me_ref[0], spots, turned, pack_columns(columns))


def third_kernel(
    me_ref, near, contact, pole_ref, scalars, rhs_ext, image_ext, half_ext, own, partner, other,
    near_side, far_side, ham, ovl, sigma,
    residual_own, direction_own, residual_rem, direction_rem, iterate, image, chunk, edge_a,
    edge_b, rho_out, turned_ext, wide, acc, mats, *sems,
):
    start_matrices(ham, ovl, sigma, mats, sems)
    blocks, poles = own.shape[0], own.shape[1]
    z = (pole_factor(pole_ref, 0), pole_factor(pole_ref, 1))
    spots = contact_spots(contact, me_ref[0], blocks)
    cols = len(spots)
    fill_extended(turned_ext, partner, own, other, me_ref[0], near_side, far_side, cols)
    sums = take_columns(gathered_sums(near_side, far_side, cols), 8)
    th, tt, hh, bh, bt = (sums[0], sums[1]), sums[2], sums[3], (sums[4], sums[5]), (sums[6], sums[7])
    norm_b, alpha = scalars[0], (scalars[1], scalars[2])
    turned_sq = tt + SMALL_EPS
    omega = (th[0] / turned_sq, th[1] / turned_sq)
    minus = complex_mul(omega, bt)
    rho_next = (bh[0] - minus[0], bh[1] - minus[1])
    zeros = jnp.zeros_like(tt)
    inverse_omega = guarded_quotient((turned_sq, zeros), th, tt * hh)
    ratio = complex_mul(rho_next, complex_mul(alpha, inverse_omega))
    beta = (ratio[0] / norm_b, ratio[1] / norm_b)
    rho_out[0] = rho_next[0]
    rho_out[1] = rho_next[1]
    rho_out[2] = norm_b

    def update(s, size):
        here = pl.ds(s, size)
        half = half_ext[here]
        residual = half - scale(omega, turned_ext[here])
        old = rhs_ext[here]
        direction = residual + scale(beta, old - scale(omega, image_ext[here]))
        store_wide(wide, s, size, direction)
        return residual, direction

    def update_own(s):
        residual, direction = update(NYB + s, 2 * TILE)
        residual_own[pl.ds(s, 2 * TILE)] = residual
        direction_own[pl.ds(s, 2 * TILE)] = direction
        here = pl.ds(NYB + s, 2 * TILE)
        iterate[pl.ds(s, 2 * TILE)] = scale(alpha, rhs_ext[here]) + scale(omega, half_ext[here])

    def update_rest(source, target, size):
        residual, direction = update(source, size)
        residual_rem[pl.ds(target, size)] = residual
        direction_rem[pl.ds(target, size)] = direction

    over_rows(blocks, 2 * TILE, update_own)
    update_rest(0, 0, NYB)
    update_rest(NYB + blocks, NYB, NYB)
    over_rows(CONTACT, 2 * TILE, lambda s: update_rest(2 * NYB + blocks + s, 2 * NYB + s, 2 * TILE))
    apply_operator(near, spots, z, wide, ham, ovl, sigma, mats, sems, acc, image)

    def terms(s):
        b, v = rhs_ext[pl.ds(NYB + s, sum_step(blocks))], image[pl.ds(s, sum_step(blocks))]
        return (*inner_terms(b, v), v * v)

    bv_re, bv_im, vv = sum_rows(blocks, sum_step(blocks), terms, 3, poles)
    store_chunk(chunk, edge_a, edge_b, me_ref[0], spots, image, pack_columns([*inner_pair(bv_re, bv_im), lane_sum(vv)]))


def fourth_kernel(
    me_ref, near, contact, pole_ref, rho_in, residual_own, direction_own, residual_rem,
    direction_rem, iterate_in, own, partner, other, near_side, far_side, ham, ovl, sigma,
    half_own, turned, iterate, sums_out, contact_image, wide, acc, mats, *sems,
):
    start_matrices(ham, ovl, sigma, mats, sems)
    blocks, poles = own.shape[0], own.shape[1]
    z = (pole_factor(pole_ref, 0), pole_factor(pole_ref, 1))
    spots = contact_spots(contact, me_ref[0], blocks)
    cols = len(spots)
    place_gathered(contact_image, 0, me_ref[0], near_side, far_side, cols)
    bv_re, bv_im, vv = take_columns(gathered_sums(near_side, far_side, cols), 3)
    norm_b = rho_in[2]
    alpha = guarded_quotient((rho_in[0], rho_in[1]), (bv_re, bv_im), norm_b * vv)

    def update_own(s):
        here = pl.ds(s, 2 * TILE)
        half = residual_own[here] - scale(alpha, own[here])
        half_own[here] = half
        iterate[here] = iterate_in[here] + scale(alpha, direction_own[here])
        store_wide(wide, NYB + s, 2 * TILE, half)

    over_rows(blocks, 2 * TILE, update_own)
    for start, image in zip(halo_starts(me_ref[0], blocks), (partner, other)):
        remote = jnp.where(start == 0, 0, NYB)
        half = residual_rem[pl.ds(remote, NYB)] - scale(alpha, image[...])
        store_wide(wide, start, NYB, half)

    def update_contact(s):
        here = pl.ds(2 * NYB + s, 2 * TILE)
        half = residual_rem[here] - scale(alpha, contact_image[pl.ds(s, 2 * TILE)])
        store_wide(wide, 2 * NYB + blocks + s, 2 * TILE, half)

    over_rows(CONTACT, 2 * TILE, update_contact)
    apply_operator(near, spots, z, wide, ham, ovl, sigma, mats, sems, acc, turned)

    def terms(s):
        h, t = half_own[pl.ds(s, sum_step(blocks))], turned[pl.ds(s, sum_step(blocks))]
        return (*inner_terms(t, h), t * t)

    th_re, th_im, tt = sum_rows(blocks, sum_step(blocks), terms, 3, poles)
    sums_out[0] = pack_columns([*inner_pair(th_re, th_im), lane_sum(tt)])


def last_kernel(near_side, far_side, half_own, turned, iterate, solution_out, residual_out):
    th_re, th_im, tt = take_columns(gathered_sums(near_side, far_side, 0), 3)
    turned_sq = tt + SMALL_EPS
    omega = (th_re / turned_sq, th_im / turned_sq)

    def update(s):
        here = pl.ds(s, 2 * TILE)
        half = half_own[here]
        solution_out[here] = iterate[here] + scale(omega, half)
        residual_out[here] = half - scale(omega, turned[here])

    over_rows(half_own.shape[0], 2 * TILE, update)


def local(rhs, ham, ovl, sigma, neighbours, contact, pole_real, pole_imag):
    blocks, poles = rhs.shape[0], rhs.shape[1]
    cols = contact.shape[0]
    count = lax.axis_size("gx")
    me = lax.axis_index("gx")
    first_block = me * blocks
    near = ((neighbours - first_block + NYB) % (blocks * count)).reshape(-1)
    me_ref = jnp.reshape(me, (1,)).astype(jnp.int32)
    ext = blocks + 2 * NYB + CONTACT

    def flip(value, mask):
        return lax.ppermute(value, "gx", [(i, i ^ mask) for i in range(count)])

    def exchange(chunk, edges=None, beside=None):
        parts = [chunk] + [flip(chunk, mask) for mask in range(4, count, 4)]
        far = ()
        if edges is not None:
            other = [(i, (i + 1 if i % 2 else i - 1) % count) for i in range(count)]
            far = (lax.ppermute(edges[1], "gx", other),)
        line = jnp.stack(parts)
        extra = ()
        if beside is not None:
            after, line = lax.optimization_barrier((near, line))
            extra = (beside(after),)
        plane = jnp.concatenate([line, flip(line, 2)])
        if edges is None:
            return plane, flip(plane, 1)
        far, extra, plane = lax.optimization_barrier((far, extra, plane))
        return (*extra, flip(edges[0], 1), *far, plane, flip(plane, 1))

    def vec_shape(rows):
        return jax.ShapeDtypeStruct((rows, poles, LANES), F32)

    slabs = (ham.reshape(-1, LANES, LANES), ovl.reshape(-1, LANES, LANES), sigma)
    small = pltpu.CompilerParams(vmem_limit_bytes=8 << 20)
    large = pltpu.CompilerParams(vmem_limit_bytes=43 << 20)
    wide = pltpu.VMEM((ext, 2 * poles, LANES), BF16)
    acc = pltpu.VMEM((sigma.shape[0], TILE * 2 * poles), F32)
    held = pltpu.VMEM((sum(m.shape[0] for m in slabs), LANES, LANES), BF16)
    parts = max(2, blocks // 32)
    sems = [pltpu.SemaphoreType.DMA((p,)) for p in (parts, parts, max(1, sigma.shape[0] // 128))]
    hbm = pl.BlockSpec(memory_space=pl.ANY)
    pole_parts = jnp.concatenate([pole_real, pole_imag])
    fixed = (me_ref, near, contact, pole_parts)
    remote = 2 * NYB + CONTACT
    rows = cols + 1

    def call(kernel, inputs, out_rows, scratch, name):
        scratch = [pltpu.VMEM((r, poles, LANES), F32) for r in scratch]
        return pl.pallas_call(
            kernel,
            in_specs=[SMEM] * 4 + [VMEM] * (len(inputs) - 4) + [hbm] * 3,
            out_specs=[VMEM] * len(out_rows),
            out_shape=[vec_shape(r) for r in out_rows],
            scratch_shapes=[*scratch, wide, acc, held, *sems],
            compiler_params=large,
            name=name,
        )(*inputs, *slabs)

    chunk, *edges = pl.pallas_call(
        prepare_kernel,
        in_specs=[SMEM, SMEM, pl.BlockSpec(memory_space=pl.ANY)],
        out_specs=[VMEM] * 3,
        out_shape=[vec_shape(rows), vec_shape(NYB), vec_shape(NYB)],
        scratch_shapes=[pltpu.SemaphoreType.DMA((cols + 2,))],
        compiler_params=small,
        name="prepare",
    )(me_ref, contact, rhs)
    def own_part(near):
        return pl.pallas_call(
            functools.partial(own_kernel, 0),
            in_specs=[SMEM] * 2 + [VMEM] + [hbm] * 2,
            out_specs=VMEM,
            out_shape=vec_shape(blocks),
            scratch_shapes=[wide, held, *([pltpu.SemaphoreType.DMA((parts,))] * 2)],
            compiler_params=pltpu.CompilerParams(vmem_limit_bytes=50 << 20),
            cost_estimate=pl.CostEstimate(
                flops=4 * ham.size * 2 * poles, bytes_accessed=4 * ham.size, transcendentals=0
            ),
            name="own",
        )(near, pole_parts, rhs, *slabs[:2])

    rhs_ext, image, chunk, edge_a, edge_b = call(
        first_kernel, (*fixed, rhs, *exchange(chunk, edges, own_part)),
        [ext, blocks, rows, NYB, NYB], [], "first",
    )
    image_ext, half_ext, turned, chunk, edge_a, edge_b, scalars = call(
        second_kernel, (*fixed, rhs_ext, image, *exchange(chunk, (edge_a, edge_b))),
        [ext, ext, blocks, rows, NYB, NYB, 3], [], "second",
    )
    res_own, dir_own, res_rem, dir_rem, iterate, image, chunk, edge_a, edge_b, rho = call(
        third_kernel,
        (*fixed, scalars, rhs_ext, image_ext, half_ext, turned, *exchange(chunk, (edge_a, edge_b))),
        [blocks, blocks, remote, remote, blocks, blocks, rows, NYB, NYB, 3], [ext], "third",
    )
    half_own, turned, iterate, sums = call(
        fourth_kernel,
        (*fixed, rho, res_own, dir_own, res_rem, dir_rem, iterate, image,
         *exchange(chunk, (edge_a, edge_b))),
        [blocks, blocks, blocks, 1], [CONTACT], "fourth",
    )
    return tuple(
        pl.pallas_call(
            last_kernel,
            in_specs=[VMEM] * 5,
            out_specs=[VMEM] * 2,
            out_shape=[vec_shape(blocks)] * 2,
            compiler_params=small,
            name="last",
        )(*exchange(sums), half_own, turned, iterate)
    )


def solution(mesh):
    return jax.shard_map(
        local,
        mesh=mesh,
        in_specs=(
            P("gx", "grp", None),
            P("gx", None, None, None),
            P("gx", None, None, None),
            P("gx", None, None),
            P("gx", None),
            P("gx"),
            P("grp"),
            P("grp"),
        ),
        out_specs=(P("gx", "grp", None), P("gx", "grp", None)),
        check_vma=False,
    )
```
